32 devices in a mesh: dp: 8 (over z, x), mode: 4 (over y, core).
Axes of the slice: x: 2, y: 2, z: 4, core: 2. Of those that a mesh axis runs over, the one named last changes fastest.
Arguments:
- series: bfloat16 [768, 128, 7], P('mode', 'dp'), may hold values from -6 to 6
- future_values: float32 [768, 128, 7], P('mode', 'dp'), may hold values from -6 to 6
- step_mask: int32 [768, 128], P('mode', 'dp'), may hold values from 0 to 1
- mode_index: int32 [64], replicated, may hold values from 1 to 383, as said below
- dense: float32 [512, 5134], P(('dp', 'mode'))
- dense_m: float32 [512, 5134], P(('dp', 'mode'))
- dense_v: float32 [512, 5134], P(('dp', 'mode'))
- dense_ema: float32 [512, 5134], P(('dp', 'mode'))
- spectral: float32 [2, 64, 32768], P(None, 'mode', 'dp')
- spec_m: float32 [2, 64, 32768], P(None, 'mode', 'dp')
- fourier_variance_moment: float32 [2, 64, 32768], P(None, 'mode', 'dp')
- spec_ema: float32 [2, 64, 32768], P(None, 'mode', 'dp')
Outputs:
- loss: float32 [], replicated
- dense_new: float32 [512, 5134], P(('dp', 'mode'))
- dense_m_new: float32 [512, 5134], P(('dp', 'mode'))
- dense_v_new: float32 [512, 5134], P(('dp', 'mode'))
- dense_ema_new: float32 [512, 5134], P(('dp', 'mode'))
- dense_low: bfloat16 [512, 5134], P(('dp', 'mode'))
- spec_new: float32 [2, 64, 32768], P(None, 'mode', 'dp')
- spec_m_new: float32 [2, 64, 32768], P(None, 'mode', 'dp')
- spec_v_new: float32 [2, 64, 32768], P(None, 'mode', 'dp')
- spec_ema_new: float32 [2, 64, 32768], P(None, 'mode', 'dp')
- spec_low: bfloat16 [2, 64, 32768], P(None, 'mode', 'dp')
The draws below stay inside these ranges and needn't reach their ends.
Inputs may be any that keep to these rules, and one draw needn't show every extreme that they name: `mode_index`: distinct values.
All inputs are finite; a program needn't handle non-finite values.
Results may differ from the reference program's by a relative error of at most 0.0072.
Values may be sent and summed in bfloat16 or wider, within the bound.
No kernel may reach another device: no remote copies, remote signals or barrier semaphores. Data moves between devices by JAX's collectives and lax.ppermute only.
A program may use at most 192 MiB of HBM per device.

```python
import math
import jax
import jax.numpy as jnp
from jax import lax

D = 512
H = 8
E = 64
FF = 2048
M = 64
C = 7
S = 768
LABEL = 48
NB = 128
DW = 5134
HEE = 32768


def dense_scales():
    pieces = [jnp.full((D,), D ** (-0.5)), jnp.full((D,), D ** (-0.5)), jnp.full((FF,), D ** (-0.5)), jnp.full((FF,), FF ** (-0.5)), jnp.full((C,), C ** (-0.5)), jnp.full((C,), D ** (-0.5))]
    return jnp.concatenate(pieces).astype(jnp.float32)


def grad_scale():
    return 2.0 / (S * NB) ** 0.5


def spec_grad_scale():
    return 0.3 * grad_scale()


def draw_step_mask(key, part):
    key = jax.random.fold_in(key, 3)
    reach = S - LABEL
    fractions = jnp.array([2, 4, 7, 15], dtype=jnp.int32)
    pick = jax.random.randint(key, (NB,), 0, 4)
    horizon = reach * fractions[pick] // 15
    first = jnp.arange(NB, dtype=jnp.int32) == 0
    horizon = jnp.where(first, reach, horizon)
    steps = jnp.arange(S, dtype=jnp.int32)[:, None]
    within_band = (steps >= LABEL) & (steps < LABEL + horizon[None, :])
    return jnp.where(within_band, 1, 0).astype(jnp.int32)


def draw_mode_index(key, part):
    key = jax.random.fold_in(key, 4)
    order = jax.random.permutation(key, S // 2 - 1)
    return (order[:M] + 1).astype(jnp.int32)


def draw_dense(key, part):
    key = jax.random.fold_in(key, 5)
    return jax.random.normal(key, (D, DW), jnp.float32) * dense_scales()[None, :]


def draw_dense_ema(key, part):
    key = jax.random.fold_in(key, 6)
    return jax.random.normal(key, (D, DW), jnp.float32) * dense_scales()[None, :]


def draw_dense_m(key, part):
    key = jax.random.fold_in(key, 7)
    return jax.random.normal(key, (D, DW), jnp.float32) * grad_scale()


def draw_dense_v(key, part):
    key = jax.random.fold_in(key, 8)
    spread = jax.random.uniform(key, (D, DW), jnp.float32, 0.0, math.log(4.0))
    return jnp.exp(spread) * grad_scale() ** 2


def spec_scale():
    return (S / (4.0 * M * E)) ** 0.5


def draw_spectral(key, part):
    key = jax.random.fold_in(key, 9)
    return jax.random.normal(key, (2, M, HEE), jnp.float32) * spec_scale()


def draw_spec_ema(key, part):
    key = jax.random.fold_in(key, 10)
    return jax.random.normal(key, (2, M, HEE), jnp.float32) * spec_scale()


def draw_spec_m(key, part):
    key = jax.random.fold_in(key, 11)
    return jax.random.normal(key, (2, M, HEE), jnp.float32) * spec_grad_scale()


def draw_fourier_variance_moment(key, part):
    key = jax.random.fold_in(key, 12)
    spread = jax.random.uniform(key, (2, M, HEE), jnp.float32, 0.0, math.log(4.0))
    return jnp.exp(spread) * spec_grad_scale() ** 2


def shard_levels(stream_key, extent, cuts, smallest, top_value):
    gain, own = 1.0, jax.random.fold_in(stream_key, 6)
    for axis_at, shards_of in cuts:
        draws = jnp.exp(jax.random.uniform(jax.random.fold_in(own, axis_at), (shards_of,), jnp.float32, smallest / len(cuts), top_value / len(cuts)))
        gain = gain * jnp.repeat(draws, extent[axis_at] // shards_of).reshape([-1 if axis == axis_at else 1 for axis in range(len(extent))])
    return gain


def noise(stream_key, extent, scale, bound, cuts=(), kind=jnp.bfloat16):
    entries = scale * jax.random.normal(stream_key, extent, jnp.float32)
    if cuts:
        entries = entries * shard_levels(stream_key, extent, cuts, -0.22, 0.18)
    return jnp.clip(entries, -bound, bound).astype(kind)


def setup_inputs(seed: int = 0) -> dict:
    streams_of = jax.random.split(jax.random.key(seed), 13)
    return {
        "series": noise(streams_of[0], (S, NB, C), 1.0, 6.0, ((0, 4), (1, 8))),
        "future_values": noise(streams_of[1], (S, NB, C), 1.0, 6.0, ((0, 4), (1, 8)), jnp.float32),
        "step_mask": draw_step_mask(jax.random.fold_in(streams_of[12], 71), 0),
        "mode_index": draw_mode_index(jax.random.fold_in(streams_of[12], 71), 0),
        "dense": draw_dense(jax.random.fold_in(streams_of[12], 71), 0),
        "dense_m": draw_dense_m(jax.random.fold_in(streams_of[12], 71), 0),
        "dense_v": draw_dense_v(jax.random.fold_in(streams_of[12], 71), 0),
        "dense_ema": draw_dense_ema(jax.random.fold_in(streams_of[12], 71), 0),
        "spectral": draw_spectral(jax.random.fold_in(streams_of[12], 71), 0),
        "spec_m": draw_spec_m(jax.random.fold_in(streams_of[12], 71), 0),
        "fourier_variance_moment": draw_fourier_variance_moment(jax.random.fold_in(streams_of[12], 71), 0),
        "spec_ema": draw_spec_ema(jax.random.fold_in(streams_of[12], 71), 0),
    }


HIGH_FREQUENCY = lax.Precision.HIGHEST
SPECTRAL_WEIGHT = 0.5
RATE_DENSE = 0.02
RATE_SPEC = 0.1

@jax.custom_vjp
def lowpass_spectrum(v):
    return lax.optimization_barrier(v.astype(jnp.bfloat16)).astype(jnp.float32)

@jax.custom_vjp
def lowpass_backward(v):
    return v

def low_keep(v):
    return (lowpass_spectrum(v), None)

def low_pass(kept, grad):
    return (grad,)

def back_keep(v):
    return (v, None)

def back_low(kept, grad):
    return (lowpass_spectrum(grad),)
lowpass_spectrum.defvjp(low_keep, low_pass)
lowpass_backward.defvjp(back_keep, back_low)

def tables(mode_index):
    steps = jnp.arange(S, dtype=jnp.int32)
    phase = mode_index[:, None] * steps[None, :] % S
    angle = phase.astype(jnp.float32) * (2.0 * math.pi / S)
    return (jnp.cos(angle), jnp.sin(angle))

def unpack(whole):
    return (whole[:, :D], whole[:, D:2 * D], whole[:, 2 * D:2 * D + FF], whole[:, 2 * D + FF:2 * D + 2 * FF], whole[:, 2 * D + 2 * FF:2 * D + 2 * FF + C], whole[:, 2 * D + 2 * FF + C:])

def group_loss(dense, spectral, series, future_values, coefficient_filter, cos_all, sin_all, cos_low, sin_low, count):
    w_query, w_out, w_up, w_down, w_embed, head_weight = unpack(lowpass_spectrum(dense))
    spec = lowpass_spectrum(spectral)
    w_real = spec[0].reshape(M, H, E, E)
    w_imag = spec[1].reshape(M, H, E, E)
    group = series.shape[1]
    hidden = jnp.einsum('tbc,dc->tbd', series, w_embed, precision=HIGH_FREQUENCY)
    inner_zero = lowpass_spectrum(hidden)
    query = lowpass_spectrum(lowpass_backward(jnp.einsum('tbd,de->tbe', inner_zero, w_query, precision=HIGH_FREQUENCY)))
    spec_re = lowpass_spectrum(lowpass_backward(jnp.einsum('ms,sbd->mbd', cos_low, query, precision=HIGH_FREQUENCY))).reshape(M, group, H, E)
    spec_im = lowpass_spectrum(lowpass_backward(-jnp.einsum('ms,sbd->mbd', sin_low, query, precision=HIGH_FREQUENCY))).reshape(M, group, H, E)
    mix_re = jnp.einsum('mbhi,mhio->mbho', spec_re, w_real, precision=HIGH_FREQUENCY) - jnp.einsum('mbhi,mhio->mbho', spec_im, w_imag, precision=HIGH_FREQUENCY)
    mix_im = jnp.einsum('mbhi,mhio->mbho', spec_re, w_imag, precision=HIGH_FREQUENCY) + jnp.einsum('mbhi,mhio->mbho', spec_im, w_real, precision=HIGH_FREQUENCY)
    mix_re = lowpass_spectrum(lowpass_backward(mix_re)).reshape(M, group, D)
    mix_im = lowpass_spectrum(lowpass_backward(mix_im)).reshape(M, group, D)
    timeline = 2.0 / S * (jnp.einsum('ms,mbd->sbd', cos_low, mix_re, precision=HIGH_FREQUENCY) - jnp.einsum('ms,mbd->sbd', sin_low, mix_im, precision=HIGH_FREQUENCY))
    timeline = lowpass_spectrum(lowpass_backward(timeline))
    branch = lowpass_backward(jnp.einsum('tbd,de->tbe', timeline, w_out, precision=HIGH_FREQUENCY))
    after_block = hidden + branch
    inner_one = lowpass_spectrum(after_block)
    gate = lowpass_backward(jnp.einsum('tbd,df->tbf', inner_one, w_up, precision=HIGH_FREQUENCY))
    activation = lowpass_spectrum(jax.nn.gelu(gate))
    feed = lowpass_backward(jnp.einsum('tbf,df->tbd', activation, w_down, precision=HIGH_FREQUENCY))
    post_feedforward = after_block + feed
    estimated_values = lowpass_backward(jnp.einsum('omg,ge->ome', lowpass_spectrum(post_feedforward), head_weight, precision=HIGH_FREQUENCY))
    prediction_residual = estimated_values - future_values
    filtered_entries = coefficient_filter[..., None] * prediction_residual
    err_re = jnp.einsum('ms,sbc->mbc', cos_all, filtered_entries, precision=HIGH_FREQUENCY)
    err_im = -jnp.einsum('ms,sbc->mbc', sin_all, filtered_entries, precision=HIGH_FREQUENCY)
    power = jnp.sum(err_re * err_re + err_im * err_im)
    return jnp.sum(filtered_entries * filtered_entries) / count + SPECTRAL_WEIGHT * power / (NB * M * S)

def adamw(weight, grad, first, second, average, rate):
    first_new = 0.5 * first + 0.5 * grad
    second_new = 0.5 * second + 0.5 * grad * grad
    weight_new = weight - rate * (first_new / (jnp.sqrt(second_new) + 1e-08) + 0.01 * weight)
    average_new = 0.9 * average + 0.1 * weight_new
    return (weight_new, first_new, second_new, average_new, weight_new.astype(jnp.bfloat16))

def reference(series, future_values, step_mask, mode_index, dense, dense_m, dense_v, dense_ema, spectral, spec_m, fourier_variance_moment, spec_ema):
    cos_all, sin_all = tables(mode_index)
    cos_low = lowpass_spectrum(cos_all)
    sin_low = lowpass_spectrum(sin_all)
    coefficient_filter = step_mask.astype(jnp.float32)
    count = jnp.sum(coefficient_filter)
    group = 8
    blocks = NB // group

    def split(arr):
        shaped = arr.reshape((S, blocks, group) + arr.shape[2:])
        return jnp.moveaxis(shaped, 1, 0)
    series_g = split(series.astype(jnp.float32))
    target_g = split(future_values)
    mask_g = split(coefficient_filter)

    def step(carry, pieces):
        loss_sum, grad_dense, grad_spec = carry
        part_series, part_target, part_mask = pieces
        value, pull = jax.vjp(lambda left, right: group_loss(left, right, part_series, part_target, part_mask, cos_all, sin_all, cos_low, sin_low, count), dense, spectral)
        got_dense, got_spec = pull(jnp.ones_like(value))
        return ((loss_sum + value, grad_dense + got_dense, grad_spec + got_spec), None)
    start = (jnp.zeros((), jnp.float32), jnp.zeros(dense.shape, jnp.float32), jnp.zeros(spectral.shape, jnp.float32))
    (loss, grad_dense, grad_spec), _ = lax.scan(step, start, (series_g, target_g, mask_g))
    dense_out = adamw(dense, grad_dense, dense_m, dense_v, dense_ema, RATE_DENSE)
    spec_out = adamw(spectral, grad_spec, spec_m, fourier_variance_moment, spec_ema, RATE_SPEC)
    return (loss, dense_out[0], dense_out[1], dense_out[2], dense_out[3], dense_out[4], spec_out[0], spec_out[1], spec_out[2], spec_out[3], spec_out[4])
```

```python
import math

import jax
import jax.numpy as jnp
from jax import lax
from jax.sharding import PartitionSpec as P

D = 512
H = 8
E = 64
FF = 2048
M = 64
C = 7
S = 768
LANES = 128

SPECTRAL_WEIGHT = 0.5
RATE_DENSE = 0.02
RATE_SPEC = 0.1
BF = jnp.bfloat16
F32 = jnp.float32
AXES = ("dp", "mode")


def plain(spec, left, right):
    return jnp.einsum(spec, left, right, preferred_element_type=F32)


def exact(spec, left, right):
    return jnp.einsum(
        spec, left, right, precision=lax.Precision.HIGHEST, preferred_element_type=F32
    )


def tables(mode_index):
    steps = jnp.arange(S, dtype=jnp.int32)
    phase = mode_index[:, None] * steps[None, :] % S
    angle = phase.astype(F32) * (2.0 * math.pi / S)
    return (jnp.cos(angle), jnp.sin(angle))


def unpack(whole):
    return (
        whole[:, :D],
        whole[:, D : 2 * D],
        whole[:, 2 * D : 2 * D + FF],
        whole[:, 2 * D + FF : 2 * D + 2 * FF],
        whole[:, 2 * D + 2 * FF : 2 * D + 2 * FF + C],
        whole[:, 2 * D + 2 * FF + C :],
    )


def adamw(weight, grad, first, second, average, rate):
    first_new = 0.5 * first + 0.5 * grad
    second_new = 0.5 * second + 0.5 * grad * grad
    weight_new = weight - rate * (first_new / (jnp.sqrt(second_new) + 1e-08) + 0.01 * weight)
    average_new = 0.9 * average + 0.1 * weight_new
    return (weight_new, first_new, second_new, average_new, weight_new.astype(BF))


def halves(x):
    high = x.astype(BF)
    return high, (x - high.astype(F32)).astype(BF)


def place(shape, *parts):
    out = jnp.zeros(shape, parts[0][0].dtype)
    for part, at in parts:
        out = lax.dynamic_update_slice(out, part, at)
    return out


def exchange(x, axes):
    return lax.all_to_all(x, axes, 0, 0, tiled=True)


def per_device(
    series,
    future_values,
    step_mask,
    mode_index,
    dense,
    dense_m,
    dense_v,
    dense_ema,
    spectral,
    spec_m,
    fourier_variance_moment,
    spec_ema,
):
    n_mode = lax.axis_size("mode")
    n_data = lax.axis_size("dp")
    n_all = n_mode * n_data
    time_rows, batch, chans = series.shape
    nb = batch // n_mode
    total = batch * n_data
    modes = M // n_mode
    wide = D // n_data
    share = FF // n_all
    rows = dense.shape[0]
    scale = 2.0 / S
    msg_rows = max(modes, 16)

    packed = jnp.concatenate(
        [series.astype(F32), future_values, step_mask.astype(F32)[..., None]], axis=2
    )
    packed = packed.reshape(time_rows, n_mode, nb, 2 * chans + 1).transpose(1, 0, 2, 3)
    packed = exchange(packed, "mode").reshape(S, nb, 2 * chans + 1)
    x_in = packed[..., :chans].astype(BF)
    target = packed[..., chans : 2 * chans]
    keep = packed[..., 2 * chans :]

    cosv, sinv = tables(mode_index)
    basis = jnp.concatenate([cosv, -sinv], axis=0)
    low = basis.astype(BF)

    mine = dense.astype(BF)
    q_rows, o_rows, u_rows, d_rows, e_rows, h_rows = unpack(mine)
    whole = lax.all_gather(
        jnp.concatenate([o_rows, u_rows, e_rows, h_rows], axis=1), AXES, axis=0, tiled=True
    )
    w_out = whole[:, :D]
    w_up = whole[:, D : D + FF]
    w_embed = whole[:, D + FF : D + FF + C]
    w_head = whole[:, D + FF + C :]

    inner = plain("rt,tx->rx", low, x_in.reshape(S, nb * chans))
    inner = jnp.concatenate([inner[:M], inner[M:]], axis=1).reshape(n_mode, modes, 2 * nb * chans)
    query_part = plain("rc,re->ce", e_rows, q_rows).reshape(chans, n_data, wide).transpose(1, 0, 2)
    down_part = plain("rc,rf->cf", h_rows, d_rows).reshape(chans, n_all, share).transpose(1, 0, 2)
    steps_local = jnp.sum(keep)
    send = place(
        (n_data, n_mode, msg_rows, LANES),
        (jnp.broadcast_to(inner[None], (n_data,) + inner.shape), (0, 0, 0, 0)),
        (
            jnp.broadcast_to(query_part[:, None], (n_data, n_mode, chans, wide)),
            (0, 0, 0, 64),
        ),
        (down_part.reshape(n_data, n_mode, chans, share), (0, 0, 8, 64)),
        (jnp.broadcast_to(steps_local, (n_data, n_mode, 1, 1)), (0, 0, 7, 64)),
    ).reshape(n_all, msg_rows, LANES)
    got = exchange(send, AXES)
    thin = jnp.sum(got[:, :, 64:], axis=0)
    query_thin = thin[:chans, :wide]
    down_slice = thin[8 : 8 + chans, :share]
    steps_total = thin[7, 0]
    inner_all = got[:, :modes, : 2 * nb * chans].reshape(n_all, modes, 2, nb, chans)

    spec = exact("dmpkc,cf->mdkpf", inner_all, query_thin).astype(BF)
    spec = spec.reshape(modes, total, 2 * wide)
    w_low = spectral.astype(BF).reshape(2, modes, wide, E)
    mixer = jnp.concatenate(
        [
            jnp.concatenate([w_low[0], w_low[1]], axis=2),
            jnp.concatenate([-w_low[1], w_low[0]], axis=2),
        ],
        axis=1,
    )
    mixed = plain("mbi,mio->mbo", spec, mixer).astype(BF)
    mixed = mixed.reshape(modes, n_all, nb, 2 * E).transpose(1, 2, 0, 3)
    down_high, down_low = halves(down_slice)
    send = place(
        (n_all, nb * modes + 16, LANES),
        (mixed.reshape(n_all, nb * modes, 2 * E), (0, 0, 0)),
        (jnp.broadcast_to(down_high[None], (n_all, chans, share)), (0, nb * modes, 0)),
        (jnp.broadcast_to(down_low[None], (n_all, chans, share)), (0, nb * modes + 8, 0)),
    )
    got = exchange(send, AXES)
    thin = got[:, nb * modes :].transpose(1, 0, 2)[:, :, :share].reshape(16, FF)
    down_thin = (thin[:8].astype(F32) + thin[8:].astype(F32))[:chans]
    mixed = got[:, : nb * modes].reshape(n_data, n_mode, nb, modes, 2, E)
    mixed = mixed.transpose(2, 4, 1, 3, 0, 5).reshape(nb, 2 * M, n_data * E)

    w_out_heads = jnp.repeat(w_out.reshape(H, E, D), n_data // H, axis=0).reshape(n_data * E, D)
    line = (scale * plain("kmi,ie->kme", mixed, w_out_heads)).astype(BF)
    rank = jnp.concatenate(
        [line, jnp.broadcast_to(w_embed.T[None], (nb, chans, D))], axis=1
    )
    wide_basis = jnp.concatenate(
        [jnp.broadcast_to(low.T[None], (nb, S, 2 * M)), x_in.transpose(1, 0, 2)], axis=2
    )
    rank_up = plain("krd,df->krf", rank, w_up).astype(BF)
    gate = plain("ktr,krf->ktf", wide_basis, rank_up)
    activation, pull = jax.vjp(jax.nn.gelu, gate)
    activation = activation.astype(BF)
    rank_head = plain("krd,dc->krc", rank, w_head)
    rank_high, rank_low = halves(rank_head)
    thin_high, thin_low = halves(down_thin)
    estimated = (
        plain("ktr,krc->tkc", wide_basis, rank_high)
        + plain("ktr,krc->tkc", wide_basis, rank_low)
        + plain("ktf,cf->tkc", activation, thin_high)
        + plain("ktf,cf->tkc", activation, thin_low)
    )
    masked = keep * (estimated - target)
    flat = masked.reshape(S, nb * chans)
    err = exact("rt,tx->rx", basis, flat)
    spec_norm = SPECTRAL_WEIGHT / (total * M * S)
    square = jnp.sum(flat * flat)
    power = jnp.sum(err * err)
    back_time = exact("rt,rx->tx", basis, err).reshape(S, nb, chans)
    g_fc = (keep * (2.0 * masked / steps_total + 2.0 * spec_norm * back_time)).astype(BF)

    down_grad = plain("tkc,ktf->cf", g_fc, activation)
    fed = plain("tkc,cf->ktf", g_fc, thin_high) + plain("tkc,cf->ktf", g_fc, thin_low)
    g_gate = pull(fed)[0].astype(BF)
    back_gate = plain("ktr,ktf->krf", wide_basis, g_gate).astype(BF)
    up_grad = plain("krd,krf->df", rank, back_gate)
    back_fc = plain("ktr,tkc->krc", wide_basis, g_fc)
    back_block = plain("krf,df->krd", back_gate, w_up) + exact(
        "krc,dc->krd", back_fc, w_head.astype(F32)
    )
    head_grad = exact("krd,krc->dc", rank.astype(F32), back_fc)
    embed_grad = jnp.sum(back_block[:, 2 * M :], axis=0)
    turned = (scale * back_block[:, : 2 * M]).astype(BF)
    out_grad = plain("kmi,kme->ie", mixed, turned)
    out_grad = out_grad.reshape(H, n_data // H, E, D).sum(1).reshape(D, D)
    g_mixed = plain("kme,ie->kmi", turned, w_out_heads).astype(BF)
    g_mixed = g_mixed.reshape(nb, 2, n_mode, modes, n_data, E).transpose(4, 2, 0, 3, 1, 5)
    g_mixed = g_mixed.reshape(n_all, nb * modes, 2 * E)
    down_grad = down_grad.reshape(chans, n_all, share).transpose(1, 0, 2)
    embed_grad = embed_grad.reshape(chans, n_all, rows).transpose(1, 0, 2)
    head_grad = head_grad.T.reshape(chans, n_all, rows).transpose(1, 0, 2)
    thin_high, thin_low = halves(jnp.concatenate([down_grad, embed_grad, head_grad], axis=2))
    send = place(
        (n_all, nb * modes + 16, LANES),
        (g_mixed, (0, 0, 0)),
        (thin_high, (0, nb * modes, 0)),
        (thin_low, (0, nb * modes + 8, 0)),
    )
    got = exchange(send, AXES)
    big_sum = lax.psum_scatter(
        jnp.concatenate([out_grad, up_grad], axis=1).astype(BF),
        AXES,
        scatter_dimension=0,
        tiled=True,
    ).astype(F32)
    thin = jnp.sum(got[:, nb * modes :].astype(F32), axis=0)
    thin = (thin[:8] + thin[8:])[:chans]
    down_slice = thin[:, :share]
    embed_own = thin[:, share : share + rows].T
    head_own = thin[:, share + rows : share + 2 * rows].T

    g_mixed = got[:, : nb * modes].reshape(n_all, nb, modes, 2 * E)
    g_mixed = g_mixed.transpose(2, 0, 1, 3).reshape(modes, total, 2 * E)
    g_spec = plain("mbo,mio->mbi", g_mixed, mixer).astype(BF)
    g_mixer = plain("mbi,mbo->mio", spec, g_mixed)
    grad_spec = jnp.stack(
        [
            g_mixer[:, :wide, :E] + g_mixer[:, wide:, E:],
            g_mixer[:, :wide, E:] - g_mixer[:, wide:, :E],
        ]
    ).reshape(spectral.shape)
    g_spec = g_spec.reshape(modes, n_all, nb, 2, wide)
    query_back = exact("dmpkc,mdkpf->cf", inner_all, g_spec.astype(F32))
    send = place(
        (16, LANES),
        (query_back, (0, 0)),
        (down_slice, (0, 64)),
        (jnp.stack([square, power]).reshape(2, 1), (8, 0)),
    )
    got = exchange(jnp.broadcast_to(send[None], (n_all, 16, LANES)), AXES)
    query_total = jnp.sum(got[:, :chans, :wide].reshape(n_data, n_mode, chans, wide), axis=1)
    query_total = query_total.transpose(1, 0, 2).reshape(chans, D)
    down_total = got[:, :chans, 64 : 64 + share].transpose(1, 0, 2).reshape(chans, FF)
    loss = jnp.sum(got[:, 8, 0]) / steps_total + spec_norm * jnp.sum(got[:, 9, 0])

    up = lambda x: x.astype(F32)
    dense_sum = jnp.concatenate(
        [
            exact("rc,ce->re", up(e_rows), query_total),
            big_sum,
            exact("rc,cf->rf", up(h_rows), down_total),
            embed_own + exact("re,ce->rc", up(q_rows), query_total),
            head_own + exact("rf,cf->rc", up(d_rows), down_total),
        ],
        axis=1,
    )
    dense_out = adamw(dense, dense_sum, dense_m, dense_v, dense_ema, RATE_DENSE)
    spec_out = adamw(spectral, grad_spec, spec_m, fourier_variance_moment, spec_ema, RATE_SPEC)
    return (loss,) + dense_out + spec_out


def solution(mesh):
    rows = P(("dp", "mode"), None)
    mixing = P(None, "mode", "dp")
    return jax.shard_map(
        per_device,
        mesh=mesh,
        in_specs=(P("mode", "dp", None), P("mode", "dp", None), P("mode", "dp"), P())
        + (rows,) * 4
        + (mixing,) * 4,
        out_specs=(P(),) + (rows,) * 5 + (mixing,) * 5,
        check_vma=False,
    )
```

```python
import math

import jax
import jax.numpy as jnp
from jax import lax
from jax.sharding import PartitionSpec as P

D = 512
H = 8
E = 64
FF = 2048
M = 64
C = 7
S = 768
LANES = 128

SPECTRAL_WEIGHT = 0.5
RATE_DENSE = 0.02
RATE_SPEC = 0.1
BF = jnp.bfloat16
F32 = jnp.float32
AXES = ("dp", "mode")


def plain(spec, left, right):
    return jnp.einsum(spec, left, right, preferred_element_type=F32)


def exact(spec, left, right):
    return jnp.einsum(
        spec, left, right, precision=lax.Precision.HIGHEST, preferred_element_type=F32
    )


def tables(mode_index):
    steps = jnp.arange(S, dtype=jnp.int32)
    phase = mode_index[:, None] * steps[None, :] % S
    angle = phase.astype(F32) * (2.0 * math.pi / S)
    return (jnp.cos(angle), jnp.sin(angle))


def unpack(whole):
    return (
        whole[:, :D],
        whole[:, D : 2 * D],
        whole[:, 2 * D : 2 * D + FF],
        whole[:, 2 * D + FF : 2 * D + 2 * FF],
        whole[:, 2 * D + 2 * FF : 2 * D + 2 * FF + C],
        whole[:, 2 * D + 2 * FF + C :],
    )


def adamw(weight, grad, first, second, average, rate):
    first_new = 0.5 * first + 0.5 * grad
    second_new = 0.5 * second + 0.5 * grad * grad
    weight_new = weight - rate * (first_new / (jnp.sqrt(second_new) + 1e-08) + 0.01 * weight)
    average_new = 0.9 * average + 0.1 * weight_new
    return (weight_new, first_new, second_new, average_new, weight_new.astype(BF))


def halves(x):
    high = x.astype(BF)
    return high, (x - high.astype(F32)).astype(BF)


def fill(x, size, axis):
    wanted = list(x.shape)
    wanted[axis] = size - x.shape[axis]
    return jnp.concatenate([x, jnp.zeros(wanted, x.dtype)], axis=axis) if wanted[axis] else x


def exchange(x, axes):
    return lax.all_to_all(x, axes, 0, 0, tiled=True)


def partners(step):
    count = lax.axis_size("mode")
    return [(index, index ^ step) for index in range(count)]


def bit_of(step):
    return lax.div(lax.axis_index("mode"), step) % 2


def steps_of_mode():
    return [1 << bit for bit in range(lax.axis_size("mode").bit_length() - 1)]


def gather_rows(x):
    n_data = lax.axis_size("dp")
    held = exchange(jnp.broadcast_to(x[None], (n_data,) + x.shape), "dp")[:, None]
    for step in reversed(steps_of_mode()):
        other = lax.ppermute(held, "mode", partners(step))
        first = bit_of(step) == 0
        pair = [jnp.where(first, held, other), jnp.where(first, other, held)]
        held = jnp.concatenate(pair, axis=1) if step > 1 else jnp.stack(pair, axis=2)
    return held.reshape(-1, x.shape[1])


def scatter_rows(x, rows):
    n_data, n_mode = lax.axis_size("dp"), lax.axis_size("mode")
    held = x.reshape(n_data, n_mode, rows, x.shape[1])
    for step in steps_of_mode():
        held = held.reshape(n_data, held.shape[1] // 2, 2, rows, x.shape[1])
        bit = bit_of(step)
        away = lax.dynamic_index_in_dim(held, 1 - bit, 2, keepdims=False)
        stay = lax.dynamic_index_in_dim(held, bit, 2, keepdims=False)
        other = lax.ppermute(away, "mode", partners(step))
        held = (stay.astype(F32) + other.astype(F32)).astype(BF)
    held = exchange(held.reshape(n_data, rows, x.shape[1]), "dp")
    return jnp.sum(held.astype(F32), axis=0)


def per_device(
    series,
    future_values,
    step_mask,
    mode_index,
    dense,
    dense_m,
    dense_v,
    dense_ema,
    spectral,
    spec_m,
    fourier_variance_moment,
    spec_ema,
):
    n_mode = lax.axis_size("mode")
    n_data = lax.axis_size("dp")
    n_all = n_mode * n_data
    time_rows, batch, chans = series.shape
    nb = batch // n_mode
    total = batch * n_data
    modes = M // n_mode
    wide = D // n_data
    share = FF // n_all
    rows = dense.shape[0]
    scale = 2.0 / S
    msg_rows = max(modes, 16)

    packed = jnp.concatenate(
        [series.astype(F32), future_values, step_mask.astype(F32)[..., None]], axis=2
    )
    packed = packed.reshape(time_rows, n_mode, nb, 2 * chans + 1).transpose(1, 0, 2, 3)
    packed = exchange(packed, "mode").reshape(S, nb, 2 * chans + 1)
    x_in = packed[..., :chans].astype(BF)
    target = packed[..., chans : 2 * chans]
    keep = packed[..., 2 * chans :]

    cosv, sinv = tables(mode_index)
    basis = jnp.concatenate([cosv, -sinv], axis=0)
    low = basis.astype(BF)

    mine = dense.astype(BF)
    q_rows, o_rows, u_rows, d_rows, e_rows, h_rows = unpack(mine)
    whole = gather_rows(jnp.concatenate([o_rows, u_rows, e_rows, h_rows], axis=1))
    w_out = whole[:, :D]
    w_up = whole[:, D : D + FF]
    w_embed = whole[:, D + FF : D + FF + C]
    w_head = whole[:, D + FF + C :]

    inner = plain("rt,tx->rx", low, x_in.reshape(S, nb * chans))
    inner = jnp.concatenate([inner[:M], inner[M:]], axis=1).reshape(n_mode, modes, 2 * nb * chans)
    query_part = plain("rc,re->ce", e_rows, q_rows).reshape(chans, n_data, wide).transpose(1, 0, 2)
    down_part = plain("rc,rf->cf", h_rows, d_rows).reshape(chans, n_all, share).transpose(1, 0, 2)
    steps_local = jnp.sum(keep)
    inner = fill(fill(inner, 64, 2), msg_rows, 1)
    count = jnp.broadcast_to(steps_local, (n_data, n_mode, 1, 64))
    thin = jnp.concatenate(
        [
            jnp.broadcast_to(fill(query_part, 64, 2)[:, None], (n_data, n_mode, chans, 64)),
            count,
            fill(down_part, 64, 2).reshape(n_data, n_mode, chans, 64),
        ],
        axis=2,
    )
    send = jnp.concatenate(
        [jnp.broadcast_to(inner[None], (n_data,) + inner.shape), fill(thin, msg_rows, 2)], axis=3
    ).reshape(n_all, msg_rows, LANES)
    got = exchange(send, AXES)
    thin = jnp.sum(got[:, :, 64:], axis=0)
    query_thin = thin[:chans, :wide]
    down_slice = thin[8 : 8 + chans, :share]
    steps_total = thin[7, 0]
    inner_all = got[:, :modes, : 2 * nb * chans].reshape(n_all, modes, 2, nb, chans)

    spec = exact("dmpkc,cf->mdkpf", inner_all, query_thin).astype(BF)
    spec = spec.reshape(modes, total, 2 * wide)
    w_low = spectral.astype(BF).reshape(2, modes, wide, E)
    mixer = jnp.concatenate(
        [
            jnp.concatenate([w_low[0], w_low[1]], axis=2),
            jnp.concatenate([-w_low[1], w_low[0]], axis=2),
        ],
        axis=1,
    )
    mixed = plain("mbi,mio->mbo", spec, mixer).astype(BF)
    mixed = mixed.reshape(modes, n_all, nb, 2 * E).transpose(1, 2, 0, 3)
    down_high, down_low = halves(down_slice)
    thin = jnp.concatenate([fill(down_high, 8, 0), fill(down_low, 8, 0)], axis=0)
    send = jnp.concatenate(
        [
            mixed.reshape(n_all, nb * modes, 2 * E),
            jnp.broadcast_to(fill(thin, LANES, 1)[None], (n_all, 16, LANES)),
        ],
        axis=1,
    )
    got = exchange(send, AXES)
    thin = got[:, nb * modes :].transpose(1, 0, 2)[:, :, :share].reshape(16, FF)
    down_thin = (thin[:8].astype(F32) + thin[8:].astype(F32))[:chans]
    mixed = got[:, : nb * modes].reshape(n_data, n_mode, nb, modes, 2, E)
    mixed = mixed.transpose(2, 4, 1, 3, 0, 5).reshape(nb, 2 * M, n_data * E)

    w_out_heads = jnp.repeat(w_out.reshape(H, E, D), n_data // H, axis=0).reshape(n_data * E, D)
    line = (scale * plain("kmi,ie->kme", mixed, w_out_heads)).astype(BF)
    rank = jnp.concatenate(
        [line, jnp.broadcast_to(w_embed.T[None], (nb, chans, D))], axis=1
    )
    wide_basis = jnp.concatenate(
        [jnp.broadcast_to(low.T[None], (nb, S, 2 * M)), x_in.transpose(1, 0, 2)], axis=2
    )
    rank_up = plain("krd,df->krf", rank, w_up).astype(BF)
    gate = plain("ktr,krf->ktf", wide_basis, rank_up)
    activation, pull = jax.vjp(jax.nn.gelu, gate)
    activation = activation.astype(BF)
    rank_head = plain("krd,dc->krc", rank, w_head)
    rank_high, rank_low = halves(rank_head)
    thin_high, thin_low = halves(down_thin)
    estimated = (
        plain("ktr,krc->tkc", wide_basis, rank_high)
        + plain("ktr,krc->tkc", wide_basis, rank_low)
        + plain("ktf,cf->tkc", activation, thin_high)
        + plain("ktf,cf->tkc", activation, thin_low)
    )
    masked = keep * (estimated - target)
    flat = masked.reshape(S, nb * chans)
    err = exact("rt,tx->rx", basis, flat)
    spec_norm = SPECTRAL_WEIGHT / (total * M * S)
    square = jnp.sum(flat * flat)
    power = jnp.sum(err * err)
    back_time = exact("rt,rx->tx", basis, err).reshape(S, nb, chans)
    g_fc = (keep * (2.0 * masked / steps_total + 2.0 * spec_norm * back_time)).astype(BF)

    down_grad = plain("tkc,ktf->cf", g_fc, activation)
    fed = plain("tkc,cf->ktf", g_fc, thin_high) + plain("tkc,cf->ktf", g_fc, thin_low)
    g_gate = pull(fed)[0].astype(BF)
    back_gate = plain("ktr,ktf->krf", wide_basis, g_gate).astype(BF)
    up_grad = plain("krd,krf->df", rank, back_gate)
    back_fc = plain("ktr,tkc->krc", wide_basis, g_fc)
    back_block = plain("krf,df->krd", back_gate, w_up) + exact(
        "krc,dc->krd", back_fc, w_head.astype(F32)
    )
    head_grad = exact("krd,krc->dc", rank.astype(F32), back_fc)
    embed_grad = jnp.sum(back_block[:, 2 * M :], axis=0)
    turned = (scale * back_block[:, : 2 * M]).astype(BF)
    out_grad = plain("kmi,kme->ie", mixed, turned)
    out_grad = out_grad.reshape(H, n_data // H, E, D).sum(1).reshape(D, D)
    g_mixed = plain("kme,ie->kmi", turned, w_out_heads).astype(BF)
    g_mixed = g_mixed.reshape(nb, 2, n_mode, modes, n_data, E).transpose(4, 2, 0, 3, 1, 5)
    g_mixed = g_mixed.reshape(n_all, nb * modes, 2 * E)
    down_grad = down_grad.reshape(chans, n_all, share).transpose(1, 0, 2)
    embed_grad = embed_grad.reshape(chans, n_all, rows).transpose(1, 0, 2)
    head_grad = head_grad.T.reshape(chans, n_all, rows).transpose(1, 0, 2)
    thin_high, thin_low = halves(jnp.concatenate([down_grad, embed_grad, head_grad], axis=2))
    thin = jnp.concatenate([fill(thin_high, 8, 1), fill(thin_low, 8, 1)], axis=1)
    send = jnp.concatenate([g_mixed, fill(thin, LANES, 2)], axis=1)
    got = exchange(send, AXES)
    big_sum = scatter_rows(jnp.concatenate([out_grad, up_grad], axis=1).astype(BF), rows)
    thin = jnp.sum(got[:, nb * modes :].astype(F32), axis=0)
    thin = (thin[:8] + thin[8:])[:chans]
    down_slice = thin[:, :share]
    embed_own = thin[:, share : share + rows].T
    head_own = thin[:, share + rows : share + 2 * rows].T

    g_mixed = got[:, : nb * modes].reshape(n_all, nb, modes, 2 * E)
    g_mixed = g_mixed.transpose(2, 0, 1, 3).reshape(modes, total, 2 * E)
    g_spec = plain("mbo,mio->mbi", g_mixed, mixer).astype(BF)
    g_mixer = plain("mbi,mbo->mio", spec, g_mixed)
    grad_spec = jnp.stack(
        [
            g_mixer[:, :wide, :E] + g_mixer[:, wide:, E:],
            g_mixer[:, :wide, E:] - g_mixer[:, wide:, :E],
        ]
    ).reshape(spectral.shape)
    g_spec = g_spec.reshape(modes, n_all, nb, 2, wide)
    query_back = exact("dmpkc,mdkpf->cf", inner_all, g_spec.astype(F32))
    tail = jnp.broadcast_to(jnp.stack([square, power]).reshape(2, 1), (2, LANES))
    send = jnp.concatenate([fill(query_back, 64, 1), fill(down_slice, 64, 1)], axis=1)
    send = fill(jnp.concatenate([fill(send, 8, 0), tail], axis=0), 16, 0)
    got = exchange(jnp.broadcast_to(send[None], (n_all, 16, LANES)), AXES)
    query_total = jnp.sum(got[:, :chans, :wide].reshape(n_data, n_mode, chans, wide), axis=1)
    query_total = query_total.transpose(1, 0, 2).reshape(chans, D)
    down_total = got[:, :chans, 64 : 64 + share].transpose(1, 0, 2).reshape(chans, FF)
    loss = jnp.sum(got[:, 8, 0]) / steps_total + spec_norm * jnp.sum(got[:, 9, 0])

    up = lambda x: x.astype(F32)
    dense_sum = jnp.concatenate(
        [
            exact("rc,ce->re", up(e_rows), query_total),
            big_sum,
            exact("rc,cf->rf", up(h_rows), down_total),
            embed_own + exact("re,ce->rc", up(q_rows), query_total),
            head_own + exact("rf,cf->rc", up(d_rows), down_total),
        ],
        axis=1,
    )
    dense_out = adamw(dense, dense_sum, dense_m, dense_v, dense_ema, RATE_DENSE)
    spec_out = adamw(spectral, grad_spec, spec_m, fourier_variance_moment, spec_ema, RATE_SPEC)
    return (loss,) + dense_out + spec_out


def solution(mesh):
    rows = P(("dp", "mode"), None)
    mixing = P(None, "mode", "dp")
    return jax.shard_map(
        per_device,
        mesh=mesh,
        in_specs=(P("mode", "dp", None), P("mode", "dp", None), P("mode", "dp"), P())
        + (rows,) * 4
        + (mixing,) * 4,
        out_specs=(P(),) + (rows,) * 5 + (mixing,) * 5,
        check_vma=False,
    )
```

```python
import math
from functools import partial

import jax
import jax.numpy as jnp
from jax import lax
from jax.experimental import pallas as pl
from jax.experimental.pallas import tpu as pltpu
from jax.sharding import PartitionSpec as P

D = 512
H = 8
E = 64
FF = 2048
M = 64
C = 7
S = 768
LANES = 128

SPECTRAL_WEIGHT = 0.5
RATE_DENSE = 0.02
RATE_SPEC = 0.1
BF = jnp.bfloat16
F32 = jnp.float32
AXES = ("dp", "mode")
SLOPE = jnp.bfloat16
VMEM_BYTES = 52 * 1024 * 1024


def plain(spec, left, right):
    return jnp.einsum(spec, left, right, preferred_element_type=F32)


def exact(spec, left, right):
    return jnp.einsum(
        spec, left, right, precision=lax.Precision.HIGHEST, preferred_element_type=F32
    )


def tables(mode_index):
    steps = jnp.arange(S, dtype=jnp.int32)
    phase = mode_index[:, None] * steps[None, :] % S
    angle = phase.astype(F32) * (2.0 * math.pi / S)
    return (jnp.cos(angle), jnp.sin(angle))


def unpack(whole):
    return (
        whole[:, :D],
        whole[:, D : 2 * D],
        whole[:, 2 * D : 2 * D + FF],
        whole[:, 2 * D + FF : 2 * D + 2 * FF],
        whole[:, 2 * D + 2 * FF : 2 * D + 2 * FF + C],
        whole[:, 2 * D + 2 * FF + C :],
    )


def adamw(weight, grad, first, second, average, rate):
    first_new = 0.5 * first + 0.5 * grad
    second_new = 0.5 * second + 0.5 * grad * grad
    weight_new = weight - rate * (first_new / (jnp.sqrt(second_new) + 1e-08) + 0.01 * weight)
    average_new = 0.9 * average + 0.1 * weight_new
    return (weight_new, first_new, second_new, average_new, weight_new.astype(BF))


def halves(x):
    high = x.astype(BF)
    return high, (x - high.astype(F32)).astype(BF)


def fill(x, size, axis):
    wanted = list(x.shape)
    wanted[axis] = size - x.shape[axis]
    return jnp.concatenate([x, jnp.zeros(wanted, x.dtype)], axis=axis) if wanted[axis] else x


def exchange(x, axes):
    return lax.all_to_all(x, axes, 0, 0, tiled=True)


def partners(step):
    count = lax.axis_size("mode")
    return [(index, index ^ step) for index in range(count)]


def bit_of(step):
    return lax.div(lax.axis_index("mode"), step) % 2


def steps_of_mode():
    return [1 << bit for bit in range(lax.axis_size("mode").bit_length() - 1)]


def gather_rows(x):
    n_data = lax.axis_size("dp")
    held = exchange(jnp.broadcast_to(x[None], (n_data,) + x.shape), "dp")[:, None]
    for step in reversed(steps_of_mode()):
        other = lax.ppermute(held, "mode", partners(step))
        first = bit_of(step) == 0
        pair = [jnp.where(first, held, other), jnp.where(first, other, held)]
        held = jnp.concatenate(pair, axis=1) if step > 1 else jnp.stack(pair, axis=2)
    return held.reshape(-1, x.shape[1])


def scatter_rows(x, rows):
    n_data, n_mode = lax.axis_size("dp"), lax.axis_size("mode")
    held = x.reshape(n_data, n_mode, rows, x.shape[1])
    for step in steps_of_mode():
        held = held.reshape(n_data, held.shape[1] // 2, 2, rows, x.shape[1])
        bit = bit_of(step)
        away = lax.dynamic_index_in_dim(held, 1 - bit, 2, keepdims=False)
        stay = lax.dynamic_index_in_dim(held, bit, 2, keepdims=False)
        other = lax.ppermute(away, "mode", partners(step))
        held = (stay.astype(F32) + other.astype(F32)).astype(BF)
    held = exchange(held.reshape(n_data, rows, x.shape[1]), "dp")
    return jnp.sum(held.astype(F32), axis=0)


NN = (((1,), (0,)), ((), ()))
NT = (((1,), (1,)), ((), ()))
TN = (((0,), (0,)), ((), ()))
FIRST = 2.0 * math.sqrt(2.0 / math.pi)
THIRD = FIRST * 0.044715
GATES = 256
LEAD = 8
HALF = 64


def mm(left, right, dims=NN):
    return lax.dot_general(left, right, dims, preferred_element_type=F32)


def iota(shape, axis):
    return lax.broadcasted_iota(jnp.int32, shape, axis)


def split(x):
    high = x.astype(BF).astype(F32)
    return high, x - high


def by_halves(x):
    high, low = split(x)
    return jnp.where(iota(x.shape, 1) < HALF, high, low).astype(BF)


def fold(x):
    return x + pltpu.roll(x, HALF, 1)


def rows_at(x, first, count):
    parts = []
    if first:
        parts.append(jnp.zeros((first, x.shape[1]), F32))
    parts.append(x)
    if count - first - x.shape[0]:
        parts.append(jnp.zeros((count - first - x.shape[0], x.shape[1]), F32))
    return jnp.concatenate(parts, axis=0)


def row_groups(x):
    return sum(x[at : at + LEAD] for at in range(0, x.shape[0], LEAD))


def block_kernel(
    sizes,
    count_ref,
    got_ref,
    w_ref,
    a_ref,
    at_ref,
    rest_ref,
    rest_t_ref,
    target_ref,
    keep_ref,
    send_ref,
    big_ref,
    stat_ref,
    wdup_ref,
    x_ref,
    v_ref,
    r_ref,
    wd_ref,
    act_ref,
    slope_ref,
    fc_ref,
    zx_ref,
    j_ref,
):
    n_data, n_mode, nb, total = sizes
    n_all = n_data * n_mode
    modes = M // n_mode
    nbm = nb * modes
    share = FF // n_all
    rows = D // n_all
    scale = 2.0 / S
    norm = SPECTRAL_WEIGHT / (total * M * S)
    chunks = FF // GATES

    for i in range(n_data):
        head = i * H // n_data
        block = w_ref[head * E : (head + 1) * E, :D]
        wdup_ref[2 * i * E : (2 * i + 1) * E, :] = block
        wdup_ref[(2 * i + 1) * E : (2 * i + 2) * E, :] = block
    for i in range(n_data):
        blocks = [got_ref[i * n_mode + j, :nbm, :].astype(F32) for j in range(n_mode)]
        for k in range(nb):
            column = [block[k * modes : (k + 1) * modes] for block in blocks]
            x_ref[k * M : (k + 1) * M, i * LANES : (i + 1) * LANES] = jnp.concatenate(
                column, axis=0
            ).astype(BF)
    x_all = x_ref[...]
    real_lane = iota(x_all.shape, 1) % LANES < HALF
    zero = jnp.zeros_like(x_all)
    x_real = jnp.where(real_lane, x_all, zero)
    x_imag = jnp.where(real_lane, zero, x_all)
    line_real = scale * mm(x_real, wdup_ref[...])
    line_imag = scale * mm(x_imag, wdup_ref[...])
    for k in range(nb):
        v_ref[2 * k * M : (2 * k + 1) * M, :] = line_real[k * M : (k + 1) * M].astype(BF)
        v_ref[(2 * k + 1) * M : (2 * k + 2) * M, :] = line_imag[k * M : (k + 1) * M].astype(BF)

    thin_t = w_ref[:, D + FF :].astype(F32).T
    embed_t = thin_t[:LEAD]
    head_t = thin_t[LEAD : 2 * LEAD]
    pad = [jnp.zeros((HALF - nb * LEAD, D), F32)] if nb * LEAD < HALF else []
    embed_all = jnp.concatenate([embed_t] * nb + pad, axis=0).astype(BF)
    head_all = jnp.concatenate([head_t] * nb + pad, axis=0).astype(BF)
    head_twice = jnp.concatenate([head_all, head_all], axis=0)
    embed_twice = jnp.concatenate([embed_t, embed_t], axis=0).astype(BF)

    per = LANES // share
    for at in range(FF // LANES):
        block = jnp.zeros((16, LANES), F32)
        for q in range(per):
            piece = got_ref[at * per + q, nbm : nbm + 16, :].astype(F32)
            piece = pltpu.roll(piece, q * share, 1) if q else piece
            block = jnp.where(iota(block.shape, 1) // share == q, piece, block)
        for k in range(nb):
            spread = jnp.concatenate(
                [rows_at(block[:LEAD], k * LEAD, HALF), rows_at(block[LEAD:], k * LEAD, HALF)],
                axis=0,
            )
            wd_ref[k, :, at * LANES : (at + 1) * LANES] = spread.astype(BF)

    for c in range(FF // 512):
        cols = slice(c * 512, (c + 1) * 512)
        w_up = w_ref[:, D + c * 512 : D + (c + 1) * 512]
        lifted = mm(v_ref[...], w_up)
        thin = mm(embed_twice, w_up)[:LEAD]
        high, low = split(thin)
        for k in range(nb):
            r_ref[k, : 2 * M, cols] = lifted[2 * k * M : 2 * (k + 1) * M].astype(BF)
            r_ref[k, 2 * M :, cols] = jnp.concatenate(
                [rows_at(high, k * LEAD, HALF), rows_at(low, k * LEAD, HALF)], axis=0
            ).astype(BF)

    parts = [mm(head_all[:16], v_ref[2 * k * M : 2 * (k + 1) * M, :], NT)[:LEAD] for k in range(nb)]
    by_head = rows_at(jnp.concatenate(parts, axis=0), 0, HALF)
    cross = mm(head_all, jnp.concatenate([embed_all, jnp.zeros_like(embed_all)], axis=0), NT)
    cross = jnp.where(iota(cross.shape, 0) // LEAD == iota(cross.shape, 1) // LEAD, cross, 0.0)
    high, low = split(jnp.concatenate([by_head, cross], axis=1))
    by_head = jnp.concatenate([high, low], axis=0).astype(BF)
    fc_ref[...] = mm(a_ref[...], by_head, NT)

    def forward(step, carry):
        k = step // chunks
        cols = pl.ds(pl.multiple_of(step % chunks * GATES, GATES), GATES)
        gate = mm(a_ref[...], r_ref[k, :, cols])
        square = gate * gate
        sig = 0.5 * jnp.tanh(gate * (square * (0.5 * THIRD) + 0.5 * FIRST)) + 0.5
        act = gate * sig
        low = act.astype(BF)
        act_ref[k, :, cols] = low
        slope = sig + act * (1.0 - sig) * (square * (3.0 * THIRD) + FIRST)
        slope_ref[k, :, cols] = slope.astype(slope_ref.dtype)
        fc_ref[...] += mm(low, wd_ref[k, :, cols], NT)
        return carry

    lax.fori_loop(0, nb * chunks, forward, 0)

    keep = keep_ref[...]
    masked = keep * (fold(fc_ref[...]) - target_ref[...])
    two = by_halves(masked)
    err = fold(mm(at_ref[: 2 * M, :], two) + mm(rest_ref[...], two))
    stat_ref[...] = jnp.concatenate(
        [
            jnp.full((1, LANES), 0.5 * jnp.sum(masked * masked)),
            jnp.full((1, LANES), 0.5 * jnp.sum(err * err)),
            jnp.zeros((6, LANES), F32),
        ],
        axis=0,
    )
    two = by_halves(err)
    back = fold(mm(a_ref[:, : 2 * M], two) + mm(rest_t_ref[...], two))
    g_fc = keep * ((2.0 / count_ref[0]) * masked + (2.0 * norm) * back)
    g_low = g_fc.astype(BF)
    g_turn = g_fc.T[:HALF].astype(BF)
    fc_ref[...] = g_fc
    zx_ref[...] = jnp.zeros_like(zx_ref)
    j_ref[...] = jnp.zeros_like(j_ref)

    def backward(step, carry):
        k = step // chunks
        cols = pl.ds(pl.multiple_of(step % chunks * GATES, GATES), GATES)
        fed = mm(g_low, wd_ref[k, :, cols])
        g_gate = (fed * slope_ref[k, :, cols].astype(F32)).astype(BF)
        turned = mm(at_ref[...], g_gate)
        r_ref[k, : 2 * M, cols] = turned[: 2 * M].astype(BF)
        own = iota((HALF, GATES), 0) // LEAD == k
        zx_ref[:, cols] += jnp.where(own, turned[2 * M :], 0.0)
        j_ref[:, cols] += jnp.where(own, mm(g_turn, act_ref[k, :, cols]), 0.0)
        return carry

    lax.fori_loop(0, nb * chunks, backward, 0)

    back_fc = by_halves(mm(at_ref[...], g_low))
    lane_of = iota((2 * M, LANES), 1) % HALF // LEAD
    nothing = jnp.zeros((2 * M, LANES), F32)
    back_rows = jnp.concatenate(
        [jnp.where(lane_of == k, back_fc[: 2 * M].astype(F32), nothing) for k in range(nb)], axis=0
    ).astype(BF)
    cross = jnp.where(
        iota((HALF, LANES), 0) // LEAD == iota((HALF, LANES), 1) % HALF // LEAD,
        back_fc[2 * M :].astype(F32),
        0.0,
    ).astype(BF)
    v_all = v_ref[...]
    z_all = r_ref[:, : 2 * M, :].reshape(nb * 2 * M, FF)
    high, low = split(row_groups(zx_ref[...]))
    zx = jnp.concatenate([high, low], axis=0).astype(BF)
    w_up = w_ref[:, D : D + FF]
    back_block = mm(z_all, w_up, NT) + mm(back_rows, head_twice)
    turned = (scale * back_block).astype(BF)
    embed_grad = row_groups(mm(zx, w_up, NT)) + row_groups(mm(cross, head_twice))
    head_grad = row_groups(mm(back_rows, v_all, TN)) + row_groups(mm(cross, embed_all, TN))
    down_grad = row_groups(j_ref[...])

    turned_real = jnp.concatenate(
        [turned[2 * k * M : (2 * k + 1) * M] for k in range(nb)], axis=0
    )
    turned_imag = jnp.concatenate(
        [turned[(2 * k + 1) * M : (2 * k + 2) * M] for k in range(nb)], axis=0
    )
    p_real = mm(turned_real, wdup_ref[...], NT)
    p_imag = mm(turned_imag, wdup_ref[...], NT)
    real_lane = iota((modes, LANES), 1) < HALF
    lane = iota((LEAD, LANES), 1)
    for i in range(n_data):
        cols = slice(i * LANES, (i + 1) * LANES)
        for j in range(n_mode):
            d = i * n_mode + j
            pieces = []
            for k in range(nb):
                at = slice(k * M + j * modes, k * M + (j + 1) * modes)
                pieces.append(jnp.where(real_lane, p_real[at, cols], p_imag[at, cols]))
            send_ref[d, :nbm, :] = jnp.concatenate(pieces, axis=0).astype(BF)
            out = jnp.zeros((LEAD, LANES), F32)
            for source, width, place in (
                (down_grad, share, 0),
                (embed_grad, rows, HALF),
                (head_grad, rows, HALF + rows),
            ):
                first = d * width // LANES * LANES
                piece = source[:, first : first + LANES]
                shift = (place - (d * width - first)) % LANES
                piece = pltpu.roll(piece, shift, 1) if shift else piece
                out = jnp.where((lane >= place) & (lane < place + width), piece, out)
            high, low = split(out)
            send_ref[d, nbm:, :] = jnp.concatenate([high, low], axis=0).astype(BF)

    x_all = x_ref[...]
    real_lane = iota(x_all.shape, 1) % LANES < HALF
    x_real = jnp.where(real_lane, x_all, zero)
    x_imag = jnp.where(real_lane, zero, x_all)
    out_grad = mm(x_real, turned_real, TN) + mm(x_imag, turned_imag, TN)
    each = n_data // H
    for head in range(H):
        block = 0.0
        for i in range(head * each, (head + 1) * each):
            block += out_grad[2 * i * E : (2 * i + 1) * E] + out_grad[(2 * i + 1) * E : (2 * i + 2) * E]
        big_ref[head * E : (head + 1) * E, :D] = block.astype(BF)
    for c in range(FF // 512):
        cols = slice(c * 512, (c + 1) * 512)
        up_grad = mm(v_all, z_all[:, cols], TN) + mm(embed_twice, zx[:, cols], TN)
        big_ref[:, D + c * 512 : D + (c + 1) * 512] = up_grad.astype(BF)


def block(count, got, weights, a, at, rest, rest_t, target, keep, sizes):
    n_data, n_mode, nb, _ = sizes
    whole = pl.BlockSpec(memory_space=pltpu.VMEM)
    return pl.pallas_call(
        partial(block_kernel, sizes),
        out_shape=(
            jax.ShapeDtypeStruct(got.shape, BF),
            jax.ShapeDtypeStruct((D, D + FF), BF),
            jax.ShapeDtypeStruct((8, LANES), F32),
        ),
        in_specs=[pl.BlockSpec(memory_space=pltpu.SMEM)] + [whole] * 8,
        out_specs=(whole,) * 3,
        scratch_shapes=[
            pltpu.VMEM((2 * n_data * E, D), BF),
            pltpu.VMEM((nb * M, n_data * LANES), BF),
            pltpu.VMEM((nb * 2 * M, D), BF),
            pltpu.VMEM((nb, 4 * M, FF), BF),
            pltpu.VMEM((nb, LANES, FF), BF),
            pltpu.VMEM((nb, S, FF), BF),
            pltpu.VMEM((nb, S, FF), SLOPE),
            pltpu.VMEM((S, LANES), F32),
            pltpu.VMEM((HALF, FF), F32),
            pltpu.VMEM((HALF, FF), F32),
        ],
        compiler_params=pltpu.CompilerParams(vmem_limit_bytes=VMEM_BYTES),
        name="block",
    )(count, got, weights, a, at, rest, rest_t, target, keep)


def per_device(
    series,
    future_values,
    step_mask,
    mode_index,
    dense,
    dense_m,
    dense_v,
    dense_ema,
    spectral,
    spec_m,
    fourier_variance_moment,
    spec_ema,
):
    n_mode = lax.axis_size("mode")
    n_data = lax.axis_size("dp")
    n_all = n_mode * n_data
    time_rows, batch, chans = series.shape
    nb = batch // n_mode
    total = batch * n_data
    modes = M // n_mode
    wide = D // n_data
    share = FF // n_all
    rows = dense.shape[0]
    msg_rows = max(modes, 16)

    packed = jnp.concatenate(
        [series.astype(F32), future_values, step_mask.astype(F32)[..., None]], axis=2
    )
    packed = packed.reshape(time_rows, n_mode, nb, 2 * chans + 1).transpose(1, 0, 2, 3)
    packed = exchange(packed, "mode").reshape(S, nb, 2 * chans + 1)
    x_in = packed[..., :chans].astype(BF)
    target = packed[..., chans : 2 * chans]
    keep = packed[..., 2 * chans :]

    cosv, sinv = tables(mode_index)
    basis = jnp.concatenate([cosv, -sinv], axis=0)
    low = basis.astype(BF)
    rest = (basis - low.astype(F32)).astype(BF)

    def lanes(x):
        return fill(fill(x, LEAD, 2).reshape(S, nb * LEAD), HALF, 1)

    x_lanes = lanes(x_in)
    a = jnp.concatenate([low.T, x_lanes, x_lanes], axis=1)
    a_turn = jnp.concatenate([low, x_lanes.T], axis=0)
    target = jnp.concatenate([lanes(target)] * 2, axis=1)
    keep_lanes = lanes(jnp.broadcast_to(keep, (S, nb, LEAD)))
    keep_lanes = jnp.concatenate([keep_lanes] * 2, axis=1)

    mine = dense.astype(BF)
    q_rows, o_rows, u_rows, d_rows, e_rows, h_rows = unpack(mine)
    weights = gather_rows(
        jnp.concatenate(
            [o_rows, u_rows, fill(e_rows, LEAD, 1), fill(h_rows, LANES - LEAD, 1)], axis=1
        )
    )

    inner = plain("rt,tx->rx", low, x_in.reshape(S, nb * chans))
    inner = jnp.concatenate([inner[:M], inner[M:]], axis=1).reshape(n_mode, modes, 2 * nb * chans)
    query_part = plain("rc,re->ce", e_rows, q_rows).reshape(chans, n_data, wide).transpose(1, 0, 2)
    down_part = plain("rc,rf->cf", h_rows, d_rows).reshape(chans, n_all, share).transpose(1, 0, 2)
    steps_local = jnp.sum(keep)
    inner = fill(fill(inner, 64, 2), msg_rows, 1)
    count = jnp.broadcast_to(steps_local, (n_data, n_mode, 1, 64))
    thin = jnp.concatenate(
        [
            jnp.broadcast_to(fill(query_part, 64, 2)[:, None], (n_data, n_mode, chans, 64)),
            count,
            fill(down_part, 64, 2).reshape(n_data, n_mode, chans, 64),
        ],
        axis=2,
    )
    send = jnp.concatenate(
        [jnp.broadcast_to(inner[None], (n_data,) + inner.shape), fill(thin, msg_rows, 2)], axis=3
    ).reshape(n_all, msg_rows, LANES)
    got = exchange(send, AXES)
    thin = jnp.sum(got[:, :, 64:], axis=0)
    query_thin = thin[:chans, :wide]
    down_slice = thin[8 : 8 + chans, :share]
    steps_total = thin[7, 0]
    inner_all = got[:, :modes, : 2 * nb * chans].reshape(n_all, modes, 2, nb, chans)

    spec = exact("dmpkc,cf->mdkpf", inner_all, query_thin).astype(BF)
    spec = spec.reshape(modes, total, 2 * wide)
    w_low = spectral.astype(BF).reshape(2, modes, wide, E)
    mixer = jnp.concatenate(
        [
            jnp.concatenate([w_low[0], w_low[1]], axis=2),
            jnp.concatenate([-w_low[1], w_low[0]], axis=2),
        ],
        axis=1,
    )
    mixed = plain("mbi,mio->mbo", spec, mixer).astype(BF)
    mixed = mixed.reshape(modes, n_all, nb, 2 * E).transpose(1, 2, 0, 3)
    down_high, down_low = halves(down_slice)
    thin = jnp.concatenate([fill(down_high, 8, 0), fill(down_low, 8, 0)], axis=0)
    send = jnp.concatenate(
        [
            mixed.reshape(n_all, nb * modes, 2 * E),
            jnp.broadcast_to(fill(thin, LANES, 1)[None], (n_all, 16, LANES)),
        ],
        axis=1,
    )
    got = exchange(send, AXES)
    send, big, stats = block(
        steps_total.reshape(1),
        got,
        weights,
        a,
        a_turn,
        rest,
        rest.T,
        target,
        keep_lanes,
        (n_data, n_mode, nb, total),
    )
    got = exchange(send, AXES)
    big_sum = scatter_rows(big, rows)
    thin = jnp.sum(got[:, nb * modes :].astype(F32), axis=0)
    thin = (thin[:8] + thin[8:])[:chans]
    down_slice = thin[:, :share]
    embed_own = thin[:, HALF : HALF + rows].T
    head_own = thin[:, HALF + rows : HALF + 2 * rows].T

    g_mixed = got[:, : nb * modes].reshape(n_all, nb, modes, 2 * E)
    g_mixed = g_mixed.transpose(2, 0, 1, 3).reshape(modes, total, 2 * E)
    g_spec = plain("mbo,mio->mbi", g_mixed, mixer).astype(BF)
    g_mixer = plain("mbi,mbo->mio", spec, g_mixed)
    grad_spec = jnp.stack(
        [
            g_mixer[:, :wide, :E] + g_mixer[:, wide:, E:],
            g_mixer[:, :wide, E:] - g_mixer[:, wide:, :E],
        ]
    ).reshape(spectral.shape)
    g_spec = g_spec.reshape(modes, n_all, nb, 2, wide)
    query_back = exact("dmpkc,mdkpf->cf", inner_all, g_spec.astype(F32))
    send = jnp.concatenate([fill(query_back, 64, 1), fill(down_slice, 64, 1)], axis=1)
    send = jnp.concatenate([fill(send, 8, 0), stats], axis=0)
    got = exchange(jnp.broadcast_to(send[None], (n_all, 16, LANES)), AXES)
    query_total = jnp.sum(got[:, :chans, :wide].reshape(n_data, n_mode, chans, wide), axis=1)
    query_total = query_total.transpose(1, 0, 2).reshape(chans, D)
    down_total = got[:, :chans, 64 : 64 + share].transpose(1, 0, 2).reshape(chans, FF)
    spec_norm = SPECTRAL_WEIGHT / (total * M * S)
    loss = jnp.sum(got[:, 8, 0]) / steps_total + spec_norm * jnp.sum(got[:, 9, 0])

    up = lambda x: x.astype(F32)
    dense_sum = jnp.concatenate(
        [
            exact("rc,ce->re", up(e_rows), query_total),
            big_sum,
            exact("rc,cf->rf", up(h_rows), down_total),
            embed_own + exact("re,ce->rc", up(q_rows), query_total),
            head_own + exact("rf,cf->rc", up(d_rows), down_total),
        ],
        axis=1,
    )
    dense_out = adamw(dense, dense_sum, dense_m, dense_v, dense_ema, RATE_DENSE)
    spec_out = adamw(spectral, grad_spec, spec_m, fourier_variance_moment, spec_ema, RATE_SPEC)
    return (loss,) + dense_out + spec_out


def solution(mesh):
    rows = P(("dp", "mode"), None)
    mixing = P(None, "mode", "dp")
    return jax.shard_map(
        per_device,
        mesh=mesh,
        in_specs=(P("mode", "dp", None), P("mode", "dp", None), P("mode", "dp"), P())
        + (rows,) * 4
        + (mixing,) * 4,
        out_specs=(P(),) + (rows,) * 5 + (mixing,) * 5,
        check_vma=False,
    )
```

```python
import math
from functools import partial

import jax
import jax.numpy as jnp
from jax import lax
from jax.experimental import pallas as pl
from jax.experimental.pallas import tpu as pltpu
from jax.sharding import PartitionSpec as P

D = 512
H = 8
E = 64
FF = 2048
M = 64
C = 7
S = 768
LANES = 128

SPECTRAL_WEIGHT = 0.5
RATE_DENSE = 0.02
RATE_SPEC = 0.1
BF = jnp.bfloat16
F32 = jnp.float32
AXES = ("dp", "mode")
SLOPE = jnp.bfloat16
VMEM_BYTES = 52 * 1024 * 1024


def plain(spec, left, right):
    return jnp.einsum(spec, left, right, preferred_element_type=F32)


def exact(spec, left, right):
    return jnp.einsum(
        spec, left, right, precision=lax.Precision.HIGHEST, preferred_element_type=F32
    )


def tables(mode_index):
    steps = jnp.arange(S, dtype=jnp.int32)
    phase = mode_index[:, None] * steps[None, :] % S
    angle = phase.astype(F32) * (2.0 * math.pi / S)
    return (jnp.cos(angle), jnp.sin(angle))


def unpack(whole):
    return (
        whole[:, :D],
        whole[:, D : 2 * D],
        whole[:, 2 * D : 2 * D + FF],
        whole[:, 2 * D + FF : 2 * D + 2 * FF],
        whole[:, 2 * D + 2 * FF : 2 * D + 2 * FF + C],
        whole[:, 2 * D + 2 * FF + C :],
    )


def adamw(weight, grad, first, second, average, rate):
    first_new = 0.5 * first + 0.5 * grad
    second_new = 0.5 * second + 0.5 * grad * grad
    weight_new = weight - rate * (first_new / (jnp.sqrt(second_new) + 1e-08) + 0.01 * weight)
    average_new = 0.9 * average + 0.1 * weight_new
    return (weight_new, first_new, second_new, average_new, weight_new.astype(BF))


def halves(x):
    high = x.astype(BF)
    return high, (x - high.astype(F32)).astype(BF)


def fill(x, size, axis):
    wanted = list(x.shape)
    wanted[axis] = size - x.shape[axis]
    return jnp.concatenate([x, jnp.zeros(wanted, x.dtype)], axis=axis) if wanted[axis] else x


def exchange(x, axes):
    return lax.all_to_all(x, axes, 0, 0, tiled=True)


def partners(step):
    count = lax.axis_size("mode")
    return [(index, index ^ step) for index in range(count)]


def bit_of(step):
    return lax.div(lax.axis_index("mode"), step) % 2


def steps_of_mode():
    return [1 << bit for bit in range(lax.axis_size("mode").bit_length() - 1)]


def by_xor(x, axis, step):
    count = lax.axis_size(axis)
    return lax.ppermute(x, axis, [(index, index ^ step) for index in range(count)])


def assemble_kernel(offsets, n_mode, rows, me_ref, *refs):
    out_ref = refs[-1]
    for ref, (data, mode) in zip(refs[:-1], offsets, strict=True):
        for at, (one, two) in enumerate(zip(data, mode, strict=True)):
            owner = (me_ref[0] ^ one) * n_mode + (me_ref[1] ^ two)
            out_ref[pl.ds(pl.multiple_of(owner * rows, rows), rows), :] = ref[at]


def gather_tiles(x, me):
    n_data, n_mode = lax.axis_size("dp"), lax.axis_size("mode")
    deep = [x] + [by_xor(x, "dp", 2 * step) for step in range(1, n_data // 2)]
    cut = len(deep) // 2
    first, second = jnp.stack(deep[:cut]), jnp.stack(deep[cut:])
    first = jnp.concatenate([first, by_xor(first, "dp", 1)])
    second = jnp.concatenate([second, by_xor(second, "mode", 2)])
    pieces = [first, by_xor(first, "mode", 2), second, by_xor(second, "dp", 1)]
    pieces += [by_xor(piece, "mode", 1) for piece in pieces]
    low = [2 * step for step in range(cut)]
    high = [2 * step for step in range(cut, 2 * cut)]
    ones = lambda data: [index + 1 for index in data]
    offsets = [
        (low + ones(low), [0] * 2 * cut),
        (low + ones(low), [2] * 2 * cut),
        (high + high, [0] * cut + [2] * cut),
        (ones(high) + ones(high), [0] * cut + [2] * cut),
    ]
    offsets += [(data, [index + 1 for index in mode]) for data, mode in offsets]
    whole = pl.BlockSpec(memory_space=pltpu.VMEM)
    return pl.pallas_call(
        partial(assemble_kernel, offsets, n_mode, x.shape[0]),
        out_shape=jax.ShapeDtypeStruct((n_data * n_mode * x.shape[0], x.shape[1]), x.dtype),
        in_specs=[pl.BlockSpec(memory_space=pltpu.SMEM)] + [whole] * len(pieces),
        out_specs=whole,
        compiler_params=pltpu.CompilerParams(vmem_limit_bytes=VMEM_BYTES),
        name="assemble",
    )(me, *pieces)


def tile_order(n_data):
    cut = n_data // 4
    low = [2 * step for step in range(cut)]
    high = [2 * step for step in range(cut, 2 * cut)]
    groups = [
        [(data + x, 2) for data in low for x in (0, 1)],
        [(data + x, 0) for data in low for x in (0, 1)],
        [(data + 1, 2 * y) for data in high for y in (0, 1)],
        [(data, 2 * y) for data in high for y in (0, 1)],
    ]
    return [[(data, mode + core) for data, mode in group] for core in (1, 0) for group in groups]


def together(*values):
    return lax.optimization_barrier(values)


def add(left, right):
    return (left.astype(F32) + right.astype(F32)).astype(BF)


def scatter_tiles_first(away, stay):
    pairs = lambda x: x.reshape((x.shape[0] // 2, 2) + x.shape[1:])
    come = by_xor(away, "mode", 1)
    groups = [add(come[g], stay[g]) for g in range(4)]
    first = by_xor(groups[0], "mode", 2)
    second = by_xor(groups[2], "dp", 1)
    return [pairs(x) for x in (first, groups[1], second, groups[3])]


def scatter_tiles_second(one, two, three, four):
    first_come = by_xor(add(one[:, 1], two[:, 1]), "dp", 1)
    second_come = by_xor(add(three[:, 1], four[:, 1]), "mode", 2)
    return [first_come, add(one[:, 0], two[:, 0]), second_come, add(three[:, 0], four[:, 0])]


def scatter_tiles_third(one, two, three, four):
    cut = one.shape[0]
    total = one[0].astype(F32) + two[0].astype(F32)
    for step in range(1, 2 * cut):
        left, right, at = (one, two, step) if step < cut else (three, four, step - cut)
        total += by_xor(add(left[at], right[at]), "dp", 2 * step).astype(F32)
    return total


def gather_rows(x):
    n_data = lax.axis_size("dp")
    held = exchange(jnp.broadcast_to(x[None], (n_data,) + x.shape), "dp")[:, None]
    for step in reversed(steps_of_mode()):
        other = lax.ppermute(held, "mode", partners(step))
        first = bit_of(step) == 0
        pair = [jnp.where(first, held, other), jnp.where(first, other, held)]
        held = jnp.concatenate(pair, axis=1) if step > 1 else jnp.stack(pair, axis=2)
    return held.reshape(-1, x.shape[1])


def scatter_rows(x, rows):
    n_data, n_mode = lax.axis_size("dp"), lax.axis_size("mode")
    held = x.reshape(n_data, n_mode, rows, x.shape[1])
    for step in steps_of_mode():
        held = held.reshape(n_data, held.shape[1] // 2, 2, rows, x.shape[1])
        bit = bit_of(step)
        away = lax.dynamic_index_in_dim(held, 1 - bit, 2, keepdims=False)
        stay = lax.dynamic_index_in_dim(held, bit, 2, keepdims=False)
        other = lax.ppermute(away, "mode", partners(step))
        held = (stay.astype(F32) + other.astype(F32)).astype(BF)
    held = exchange(held.reshape(n_data, rows, x.shape[1]), "dp")
    return jnp.sum(held.astype(F32), axis=0)


NN = (((1,), (0,)), ((), ()))
NT = (((1,), (1,)), ((), ()))
TN = (((0,), (0,)), ((), ()))
FIRST = 2.0 * math.sqrt(2.0 / math.pi)
THIRD = FIRST * 0.044715
GATES = 256
LEAD = 8
HALF = 64


def mm(left, right, dims=NN):
    return lax.dot_general(left, right, dims, preferred_element_type=F32)


def iota(shape, axis):
    return lax.broadcasted_iota(jnp.int32, shape, axis)


def split(x):
    high = x.astype(BF).astype(F32)
    return high, x - high


def by_halves(x):
    high, low = split(x)
    return jnp.where(iota(x.shape, 1) < HALF, high, low).astype(BF)


def fold(x):
    return x + pltpu.roll(x, HALF, 1)


def rows_at(x, first, count):
    parts = []
    if first:
        parts.append(jnp.zeros((first, x.shape[1]), F32))
    parts.append(x)
    if count - first - x.shape[0]:
        parts.append(jnp.zeros((count - first - x.shape[0], x.shape[1]), F32))
    return jnp.concatenate(parts, axis=0)


def row_groups(x):
    return sum(x[at : at + LEAD] for at in range(0, x.shape[0], LEAD))


def block_kernel(
    sizes,
    count_ref,
    me_ref,
    got_ref,
    w_ref,
    a_ref,
    at_ref,
    rest_ref,
    rest_t_ref,
    target_ref,
    keep_ref,
    send_ref,
    stat_ref,
    *refs,
):
    if len(sizes) > 4:
        away_ref, stay_ref, big_ref, *refs = refs
    else:
        big_ref, *refs = refs
    block_steps(
        sizes,
        count_ref,
        got_ref,
        w_ref,
        a_ref,
        at_ref,
        rest_ref,
        rest_t_ref,
        target_ref,
        keep_ref,
        send_ref,
        big_ref,
        stat_ref,
        *refs,
    )
    if len(sizes) > 4:
        n_data, n_mode = sizes[:2]
        rows = D // n_data // n_mode
        order = tile_order(n_data)
        for at, group in enumerate(order):
            ref = away_ref if at < 4 else stay_ref
            for index, (data, mode) in enumerate(group):
                owner = (me_ref[0] ^ data) * n_mode + (me_ref[1] ^ mode)
                ref[at % 4, index] = big_ref[pl.ds(pl.multiple_of(owner * rows, rows), rows), :]


def block_steps(
    sizes,
    count_ref,
    got_ref,
    w_ref,
    a_ref,
    at_ref,
    rest_ref,
    rest_t_ref,
    target_ref,
    keep_ref,
    send_ref,
    big_ref,
    stat_ref,
    wdup_ref,
    x_ref,
    v_ref,
    r_ref,
    wd_ref,
    act_ref,
    slope_ref,
    fc_ref,
    zx_ref,
    j_ref,
):
    n_data, n_mode, nb, total = sizes[:4]
    n_all = n_data * n_mode
    modes = M // n_mode
    nbm = nb * modes
    share = FF // n_all
    rows = D // n_all
    scale = 2.0 / S
    norm = SPECTRAL_WEIGHT / (total * M * S)
    chunks = FF // GATES

    for i in range(n_data):
        head = i * H // n_data
        block = w_ref[head * E : (head + 1) * E, :D]
        wdup_ref[2 * i * E : (2 * i + 1) * E, :] = block
        wdup_ref[(2 * i + 1) * E : (2 * i + 2) * E, :] = block
    for i in range(n_data):
        blocks = [got_ref[i * n_mode + j, :nbm, :].astype(F32) for j in range(n_mode)]
        for k in range(nb):
            column = [block[k * modes : (k + 1) * modes] for block in blocks]
            x_ref[k * M : (k + 1) * M, i * LANES : (i + 1) * LANES] = jnp.concatenate(
                column, axis=0
            ).astype(BF)
    x_all = x_ref[...]
    real_lane = iota(x_all.shape, 1) % LANES < HALF
    zero = jnp.zeros_like(x_all)
    x_real = jnp.where(real_lane, x_all, zero)
    x_imag = jnp.where(real_lane, zero, x_all)
    line_real = scale * mm(x_real, wdup_ref[...])
    line_imag = scale * mm(x_imag, wdup_ref[...])
    for k in range(nb):
        v_ref[2 * k * M : (2 * k + 1) * M, :] = line_real[k * M : (k + 1) * M].astype(BF)
        v_ref[(2 * k + 1) * M : (2 * k + 2) * M, :] = line_imag[k * M : (k + 1) * M].astype(BF)

    thin_t = w_ref[:, D + FF :].astype(F32).T
    embed_t = thin_t[:LEAD]
    head_t = thin_t[LEAD : 2 * LEAD]
    pad = [jnp.zeros((HALF - nb * LEAD, D), F32)] if nb * LEAD < HALF else []
    embed_all = jnp.concatenate([embed_t] * nb + pad, axis=0).astype(BF)
    head_all = jnp.concatenate([head_t] * nb + pad, axis=0).astype(BF)
    head_twice = jnp.concatenate([head_all, head_all], axis=0)
    embed_twice = jnp.concatenate([embed_t, embed_t], axis=0).astype(BF)

    per = LANES // share
    for at in range(FF // LANES):
        block = jnp.zeros((16, LANES), F32)
        for q in range(per):
            piece = got_ref[at * per + q, nbm : nbm + 16, :].astype(F32)
            piece = pltpu.roll(piece, q * share, 1) if q else piece
            block = jnp.where(iota(block.shape, 1) // share == q, piece, block)
        for k in range(nb):
            spread = jnp.concatenate(
                [rows_at(block[:LEAD], k * LEAD, HALF), rows_at(block[LEAD:], k * LEAD, HALF)],
                axis=0,
            )
            wd_ref[k, :, at * LANES : (at + 1) * LANES] = spread.astype(BF)

    for c in range(FF // 512):
        cols = slice(c * 512, (c + 1) * 512)
        w_up = w_ref[:, D + c * 512 : D + (c + 1) * 512]
        lifted = mm(v_ref[...], w_up)
        thin = mm(embed_twice, w_up)[:LEAD]
        high, low = split(thin)
        for k in range(nb):
            r_ref[k, : 2 * M, cols] = lifted[2 * k * M : 2 * (k + 1) * M].astype(BF)
            r_ref[k, 2 * M :, cols] = jnp.concatenate(
                [rows_at(high, k * LEAD, HALF), rows_at(low, k * LEAD, HALF)], axis=0
            ).astype(BF)

    parts = [mm(head_all[:16], v_ref[2 * k * M : 2 * (k + 1) * M, :], NT)[:LEAD] for k in range(nb)]
    by_head = rows_at(jnp.concatenate(parts, axis=0), 0, HALF)
    cross = mm(head_all, jnp.concatenate([embed_all, jnp.zeros_like(embed_all)], axis=0), NT)
    cross = jnp.where(iota(cross.shape, 0) // LEAD == iota(cross.shape, 1) // LEAD, cross, 0.0)
    high, low = split(jnp.concatenate([by_head, cross], axis=1))
    by_head = jnp.concatenate([high, low], axis=0).astype(BF)
    fc_ref[...] = mm(a_ref[...], by_head, NT)

    def forward(step, carry):
        k = step // chunks
        cols = pl.ds(pl.multiple_of(step % chunks * GATES, GATES), GATES)
        gate = mm(a_ref[...], r_ref[k, :, cols])
        square = gate * gate
        sig = 0.5 * jnp.tanh(gate * (square * (0.5 * THIRD) + 0.5 * FIRST)) + 0.5
        act = gate * sig
        low = act.astype(BF)
        act_ref[k, :, cols] = low
        slope = sig + act * (1.0 - sig) * (square * (3.0 * THIRD) + FIRST)
        slope_ref[k, :, cols] = slope.astype(slope_ref.dtype)
        fc_ref[...] += mm(low, wd_ref[k, :, cols], NT)
        return carry

    lax.fori_loop(0, nb * chunks, forward, 0)

    keep = keep_ref[...]
    masked = keep * (fold(fc_ref[...]) - target_ref[...])
    two = by_halves(masked)
    err = fold(mm(at_ref[: 2 * M, :], two) + mm(rest_ref[...], two))
    stat_ref[...] = jnp.concatenate(
        [
            jnp.full((1, LANES), 0.5 * jnp.sum(masked * masked)),
            jnp.full((1, LANES), 0.5 * jnp.sum(err * err)),
            jnp.zeros((6, LANES), F32),
        ],
        axis=0,
    )
    two = by_halves(err)
    back = fold(mm(a_ref[:, : 2 * M], two) + mm(rest_t_ref[...], two))
    g_fc = keep * ((2.0 / count_ref[0]) * masked + (2.0 * norm) * back)
    g_low = g_fc.astype(BF)
    g_turn = g_fc.T[:HALF].astype(BF)
    fc_ref[...] = g_fc
    zx_ref[...] = jnp.zeros_like(zx_ref)
    j_ref[...] = jnp.zeros_like(j_ref)

    def backward(step, carry):
        k = step // chunks
        cols = pl.ds(pl.multiple_of(step % chunks * GATES, GATES), GATES)
        fed = mm(g_low, wd_ref[k, :, cols])
        g_gate = (fed * slope_ref[k, :, cols].astype(F32)).astype(BF)
        turned = mm(at_ref[...], g_gate)
        r_ref[k, : 2 * M, cols] = turned[: 2 * M].astype(BF)
        own = iota((HALF, GATES), 0) // LEAD == k
        zx_ref[:, cols] += jnp.where(own, turned[2 * M :], 0.0)
        j_ref[:, cols] += jnp.where(own, mm(g_turn, act_ref[k, :, cols]), 0.0)
        return carry

    lax.fori_loop(0, nb * chunks, backward, 0)

    back_fc = by_halves(mm(at_ref[...], g_low))
    lane_of = iota((2 * M, LANES), 1) % HALF // LEAD
    nothing = jnp.zeros((2 * M, LANES), F32)
    back_rows = jnp.concatenate(
        [jnp.where(lane_of == k, back_fc[: 2 * M].astype(F32), nothing) for k in range(nb)], axis=0
    ).astype(BF)
    cross = jnp.where(
        iota((HALF, LANES), 0) // LEAD == iota((HALF, LANES), 1) % HALF // LEAD,
        back_fc[2 * M :].astype(F32),
        0.0,
    ).astype(BF)
    v_all = v_ref[...]
    z_all = r_ref[:, : 2 * M, :].reshape(nb * 2 * M, FF)
    high, low = split(row_groups(zx_ref[...]))
    zx = jnp.concatenate([high, low], axis=0).astype(BF)
    w_up = w_ref[:, D : D + FF]
    back_block = mm(z_all, w_up, NT) + mm(back_rows, head_twice)
    turned = (scale * back_block).astype(BF)
    embed_grad = row_groups(mm(zx, w_up, NT)) + row_groups(mm(cross, head_twice))
    head_grad = row_groups(mm(back_rows, v_all, TN)) + row_groups(mm(cross, embed_all, TN))
    down_grad = row_groups(j_ref[...])

    turned_real = jnp.concatenate(
        [turned[2 * k * M : (2 * k + 1) * M] for k in range(nb)], axis=0
    )
    turned_imag = jnp.concatenate(
        [turned[(2 * k + 1) * M : (2 * k + 2) * M] for k in range(nb)], axis=0
    )
    p_real = mm(turned_real, wdup_ref[...], NT)
    p_imag = mm(turned_imag, wdup_ref[...], NT)
    real_lane = iota((modes, LANES), 1) < HALF
    lane = iota((LEAD, LANES), 1)
    for i in range(n_data):
        cols = slice(i * LANES, (i + 1) * LANES)
        for j in range(n_mode):
            d = i * n_mode + j
            pieces = []
            for k in range(nb):
                at = slice(k * M + j * modes, k * M + (j + 1) * modes)
                pieces.append(jnp.where(real_lane, p_real[at, cols], p_imag[at, cols]))
            send_ref[d, :nbm, :] = jnp.concatenate(pieces, axis=0).astype(BF)
            out = jnp.zeros((LEAD, LANES), F32)
            for source, width, place in (
                (down_grad, share, 0),
                (embed_grad, rows, HALF),
                (head_grad, rows, HALF + rows),
            ):
                first = d * width // LANES * LANES
                piece = source[:, first : first + LANES]
                shift = (place - (d * width - first)) % LANES
                piece = pltpu.roll(piece, shift, 1) if shift else piece
                out = jnp.where((lane >= place) & (lane < place + width), piece, out)
            high, low = split(out)
            send_ref[d, nbm:, :] = jnp.concatenate([high, low], axis=0).astype(BF)

    x_all = x_ref[...]
    real_lane = iota(x_all.shape, 1) % LANES < HALF
    x_real = jnp.where(real_lane, x_all, zero)
    x_imag = jnp.where(real_lane, zero, x_all)
    out_grad = mm(x_real, turned_real, TN) + mm(x_imag, turned_imag, TN)
    each = n_data // H
    for head in range(H):
        block = 0.0
        for i in range(head * each, (head + 1) * each):
            block += out_grad[2 * i * E : (2 * i + 1) * E] + out_grad[(2 * i + 1) * E : (2 * i + 2) * E]
        big_ref[head * E : (head + 1) * E, :D] = block.astype(BF)
    for c in range(FF // 512):
        cols = slice(c * 512, (c + 1) * 512)
        up_grad = mm(v_all, z_all[:, cols], TN) + mm(embed_twice, zx[:, cols], TN)
        big_ref[:, D + c * 512 : D + (c + 1) * 512] = up_grad.astype(BF)


def block(count, me, got, weights, a, at, rest, rest_t, target, keep, sizes):
    n_data, n_mode, nb = sizes[:3]
    whole = pl.BlockSpec(memory_space=pltpu.VMEM)
    big = [jax.ShapeDtypeStruct((D, D + FF), BF)]
    if len(sizes) > 4:
        half = (4, n_data * n_mode // 8, D // n_data // n_mode, D + FF)
        big = [jax.ShapeDtypeStruct(half, BF)] * 2
    return pl.pallas_call(
        partial(block_kernel, sizes),
        out_shape=(
            jax.ShapeDtypeStruct(got.shape, BF),
            jax.ShapeDtypeStruct((8, LANES), F32),
            *big,
        ),
        in_specs=[pl.BlockSpec(memory_space=pltpu.SMEM)] * 2 + [whole] * 8,
        out_specs=(whole,) * (2 + len(big)),
        scratch_shapes=([pltpu.VMEM((D, D + FF), BF)] if len(sizes) > 4 else [])
        + [
            pltpu.VMEM((2 * n_data * E, D), BF),
            pltpu.VMEM((nb * M, n_data * LANES), BF),
            pltpu.VMEM((nb * 2 * M, D), BF),
            pltpu.VMEM((nb, 4 * M, FF), BF),
            pltpu.VMEM((nb, LANES, FF), BF),
            pltpu.VMEM((nb, S, FF), BF),
            pltpu.VMEM((nb, S, FF), SLOPE),
            pltpu.VMEM((S, LANES), F32),
            pltpu.VMEM((HALF, FF), F32),
            pltpu.VMEM((HALF, FF), F32),
        ],
        compiler_params=pltpu.CompilerParams(vmem_limit_bytes=VMEM_BYTES),
        name="block",
    )(count, me, got, weights, a, at, rest, rest_t, target, keep)


def at_lane(x, first, width):
    x = pltpu.roll(x, first, 1) if first else x
    lane = iota(x.shape, 1)
    return jnp.where((lane >= first) & (lane < first + width), x, 0.0)


def from_lane(x, first, width):
    base = first // LANES * LANES
    x = x[:, base : base + LANES]
    shift = (LANES - (first - base)) % LANES
    x = pltpu.roll(x, shift, 1) if shift else x
    return jnp.where(iota(x.shape, 1) < width, x, 0.0)


def call(kernel, outs, ins, scratch=(), name=None):
    whole = pl.BlockSpec(memory_space=pltpu.VMEM)
    return pl.pallas_call(
        kernel,
        out_shape=outs,
        in_specs=[whole] * len(ins),
        out_specs=jax.tree.map(lambda _: whole, outs),
        scratch_shapes=list(scratch),
        compiler_params=pltpu.CompilerParams(vmem_limit_bytes=VMEM_BYTES),
        name=name,
    )(*ins)


def spectra_kernel(sizes, x_ref, keep_ref, low_ref, dense_ref, send_ref):
    n_data, n_mode, nb, _ = sizes
    n_all = n_data * n_mode
    modes = M // n_mode
    wide = D // n_data
    share = FF // n_all
    x = x_ref[...].astype(F32)
    x = jnp.concatenate([x, jnp.zeros_like(x)], axis=1)
    inner = mm(low_ref[:M, :], x.astype(BF))
    inner += mm(low_ref[M:, :], pltpu.roll(x, nb * LEAD, 1).astype(BF))
    thin = dense_ref[:, 2 * D + 2 * FF :]
    thin = jnp.concatenate([thin, jnp.zeros((thin.shape[0], LANES - 2 * C), F32)], axis=1)
    thin = at_lane(thin, 0, C) + at_lane(from_lane(thin, C, C), LEAD, C)
    thin = thin.astype(BF)
    query = mm(thin, dense_ref[:, :D].astype(BF), TN)[:LEAD]
    down = mm(thin, dense_ref[:, 2 * D + FF : 2 * D + 2 * FF].astype(BF), TN)[LEAD : 2 * LEAD]
    count = jnp.sum(keep_ref[...]) * (0.5 / LEAD)
    row = iota((LEAD, LANES), 0)
    lane = iota((LEAD, LANES), 1)
    for i in range(n_data):
        ours = at_lane(from_lane(query, i * wide, wide), HALF, wide)
        ours = jnp.where((row == C) & (lane == HALF), count, ours)
        for j in range(n_mode):
            d = i * n_mode + j
            block = inner[j * modes : (j + 1) * modes]
            if modes < 16:
                block = jnp.concatenate([block, jnp.zeros((16 - modes, LANES), F32)], axis=0)
            theirs = at_lane(from_lane(down, d * share, share), HALF, share)
            send_ref[d] = block + jnp.concatenate([ours, theirs], axis=0)


def mix_kernel(sizes, got_ref, mixer_ref, send_ref, spec_ref, thin_ref, wide_ref, out_ref):
    n_data, n_mode, nb, _ = sizes
    n_all = n_data * n_mode
    modes = M // n_mode
    nbm = nb * modes
    wide = D // n_data
    share = FF // n_all
    got = got_ref[...]
    thin = jnp.sum(got, axis=0)
    thin_ref[...] = thin
    query = from_lane(thin[:LEAD], HALF, wide)
    query = jnp.where(iota(query.shape, 0) < C, query, 0.0)
    down = from_lane(thin[LEAD:], HALF, share)
    high, low = split(down)
    down = jnp.concatenate([high, low], axis=0).astype(BF)
    spread = []
    for part in range(2):
        block = at_lane(query, part * wide, wide)
        zero = jnp.zeros_like(block)
        for k in range(nb):
            blocks = [block if g == k else zero for g in range(nb)]
            spread.append(jnp.concatenate(blocks, axis=1))
    spread = jnp.concatenate(spread, axis=0)
    inner = got.reshape(n_all * 16, LANES)[:, : 2 * nb * LEAD]
    spec = lax.dot_general(
        inner, spread, NN, precision=lax.Precision.HIGHEST, preferred_element_type=F32
    )
    for k in range(nb):
        wide_ref[k] = spec[:, k * LANES : (k + 1) * LANES]
    for m in range(modes):
        spec = [wide_ref[k, pl.ds(m, n_all, stride=16), :][:, : 2 * wide] for k in range(nb)]
        spec = jnp.concatenate(spec, axis=0).astype(BF)
        spec_ref[m] = spec
        mixed = mm(spec, mixer_ref[m])
        for k in range(nb):
            out_ref[pl.ds(k * modes + m, n_all, stride=nbm), :] = mixed[
                k * n_all : (k + 1) * n_all
            ]
    for d in range(n_all):
        send_ref[d, :nbm, :] = out_ref[d * nbm : (d + 1) * nbm, :].astype(BF)
        send_ref[d, nbm:, :] = down


def mix_back_kernel(
    sizes, got_ref, mixer_ref, first_ref, stat_ref, send_ref, grad_ref, thin_ref, in_ref, wide_ref
):
    n_data, n_mode, nb, _ = sizes
    n_all = n_data * n_mode
    modes = M // n_mode
    nbm = nb * modes
    wide = D // n_data
    share = FF // n_all
    thin = jnp.zeros((16, LANES), F32)
    for d in range(n_all):
        in_ref[d * nbm : (d + 1) * nbm, :] = got_ref[d, :nbm, :].astype(F32)
        thin += got_ref[d, nbm:, :].astype(F32)
    thin = thin[:LEAD] + thin[LEAD:]
    thin_ref[...] = thin
    if modes < 16:
        wide_ref[...] = jnp.zeros_like(wide_ref)
    for m in range(modes):
        grad = [in_ref[pl.ds(k * modes + m, n_all, stride=nbm), :] for k in range(nb)]
        grad = jnp.concatenate(grad, axis=0).astype(BF)
        grad_ref[m] = grad
        back = mm(grad, mixer_ref[m], NT).astype(BF).astype(F32)
        if 2 * wide < LANES:
            back = jnp.concatenate(
                [back, jnp.zeros((back.shape[0], LANES - 2 * wide), F32)], axis=1
            )
        for k in range(nb):
            wide_ref[k, pl.ds(m, n_all, stride=16), :] = back[k * n_all : (k + 1) * n_all]
    inner = first_ref[...].reshape(n_all * 16, LANES)
    inner = jnp.where(iota(inner.shape, 1) < HALF, inner, 0.0)
    inner = by_halves(fold(inner))
    total = jnp.zeros((LEAD, LANES), F32)
    for k in range(nb):
        query = mm(inner, wide_ref[k].astype(BF), TN)
        query = query[:HALF] + query[HALF:]
        for part in range(2):
            at = (part * nb + k) * LEAD
            total += from_lane(query[at : at + LEAD], part * wide, wide)
    block = total + at_lane(from_lane(thin, 0, share), HALF, share)
    block = jnp.concatenate([block, stat_ref[...]], axis=0)
    for d in range(n_all):
        send_ref[d] = block


def spectral_kernel(
    modes,
    wide,
    spec_ref,
    grad_ref,
    w_ref,
    m_ref,
    v_ref,
    ema_ref,
    w_out,
    m_out,
    v_out,
    ema_out,
    low_out,
    pair_ref,
    turn_ref,
):
    lower = iota((wide, LANES), 1) < HALF
    half_lower = iota((wide // 2, LANES), 1) < HALF
    for m in range(modes):
        slopes = mm(spec_ref[m], grad_ref[m], TN)
        other = pltpu.roll(slopes[wide:], HALF, 1)
        pair_ref[m] = jnp.where(lower, slopes[:wide] + other, slopes[:wide] - other)
        even = pair_ref[m, pl.ds(0, wide // 2, stride=2), :]
        odd = pair_ref[m, pl.ds(1, wide // 2, stride=2), :]
        real = jnp.where(half_lower, even, pltpu.roll(odd, HALF, 1))
        imag = jnp.where(half_lower, pltpu.roll(even, HALF, 1), odd)
        turn_ref[0, pl.ds(m, wide // 2, stride=modes), :] = real
        turn_ref[1, pl.ds(m, wide // 2, stride=modes), :] = imag
    for part in range(2):
        for at in range(wide // 2):
            cols = slice(at * LANES, (at + 1) * LANES)
            grad = turn_ref[part, at * modes : (at + 1) * modes, :]
            new = adamw(
                w_ref[part, :, cols],
                grad,
                m_ref[part, :, cols],
                v_ref[part, :, cols],
                ema_ref[part, :, cols],
                RATE_SPEC,
            )
            for ref, value in zip((w_out, m_out, v_out, ema_out, low_out), new, strict=True):
                ref[part, :, cols] = value


def per_device(
    series,
    future_values,
    step_mask,
    mode_index,
    dense,
    dense_m,
    dense_v,
    dense_ema,
    spectral,
    spec_m,
    fourier_variance_moment,
    spec_ema,
):
    n_mode = lax.axis_size("mode")
    n_data = lax.axis_size("dp")
    n_all = n_mode * n_data
    time_rows, batch, chans = series.shape
    nb = batch // n_mode
    total = batch * n_data
    modes = M // n_mode
    wide = D // n_data
    share = FF // n_all
    rows = dense.shape[0]
    msg_rows = max(modes, 16)

    packed = jnp.concatenate(
        [series.astype(F32), future_values, step_mask.astype(F32)[..., None]], axis=2
    )
    packed = packed.reshape(time_rows, n_mode, nb, 2 * chans + 1).transpose(1, 0, 2, 3)
    packed = exchange(packed, "mode").reshape(S, nb, 2 * chans + 1)
    x_in = packed[..., :chans].astype(BF)
    target = packed[..., chans : 2 * chans]
    keep = packed[..., 2 * chans :]

    cosv, sinv = tables(mode_index)
    basis = jnp.concatenate([cosv, -sinv], axis=0)
    low = basis.astype(BF)
    rest = (basis - low.astype(F32)).astype(BF)

    def lanes(x):
        return fill(fill(x, LEAD, 2).reshape(S, nb * LEAD), HALF, 1)

    x_lanes = lanes(x_in)
    a = jnp.concatenate([low.T, x_lanes, x_lanes], axis=1)
    a_turn = jnp.concatenate([low, x_lanes.T], axis=0)
    target = jnp.concatenate([lanes(target)] * 2, axis=1)
    keep_lanes = lanes(jnp.broadcast_to(keep, (S, nb, LEAD)))
    keep_lanes = jnp.concatenate([keep_lanes] * 2, axis=1)

    mine = dense.astype(BF)
    q_rows, o_rows, u_rows, d_rows, e_rows, h_rows = unpack(mine)
    sizes = (n_data, n_mode, nb, total)
    tiled = rows % 16 == 0 and n_mode == 4 and n_data >= 4
    me = jnp.stack([lax.axis_index("dp"), lax.axis_index("mode")]).astype(jnp.int32)
    weights = jnp.concatenate(
        [o_rows, u_rows, fill(e_rows, LEAD, 1), fill(h_rows, LANES - LEAD, 1)], axis=1
    )
    weights = gather_tiles(weights, me) if tiled else gather_rows(weights)

    shape = jax.ShapeDtypeStruct
    send = call(
        partial(spectra_kernel, sizes),
        shape((n_all, 16, LANES), F32),
        (x_lanes, keep_lanes, low, dense),
        name="spectra",
    )
    first = exchange(send, AXES)

    w_low = spectral.astype(BF).reshape(2, modes, wide, E)
    mixer = jnp.concatenate(
        [
            jnp.concatenate([w_low[0], w_low[1]], axis=2),
            jnp.concatenate([-w_low[1], w_low[0]], axis=2),
        ],
        axis=1,
    )
    scratch = [
        pltpu.VMEM((nb, n_all * 16, LANES), F32),
        pltpu.VMEM((n_all * nb * modes, LANES), F32),
    ]
    send, spec, thin = call(
        partial(mix_kernel, sizes),
        (
            shape((n_all, nb * modes + 16, LANES), BF),
            shape((modes, total, 2 * wide), BF),
            shape((16, LANES), F32),
        ),
        (first, mixer),
        scratch,
        name="mix",
    )
    steps_total = thin[7, HALF]
    got = exchange(send, AXES)

    send, stats, *big = block(
        steps_total.reshape(1),
        me,
        got,
        weights,
        a,
        a_turn,
        rest,
        rest.T,
        target,
        keep_lanes,
        sizes + (True,) if tiled else sizes,
    )
    got = exchange(send, AXES)
    if tiled:
        big = scatter_tiles_first(*big)
        got, *big = together(got, *big)
        big = scatter_tiles_second(*big)
    send, grad_mixed, thin = call(
        partial(mix_back_kernel, sizes),
        (
            shape((n_all, 16, LANES), F32),
            shape((modes, total, LANES), BF),
            shape((LEAD, LANES), F32),
        ),
        (got, mixer, first, stats),
        scratch[::-1],
        name="mix_back",
    )
    embed_own = thin[:C, HALF : HALF + rows].T
    head_own = thin[:C, HALF + rows : HALF + 2 * rows].T
    spec_out = call(
        partial(spectral_kernel, modes, wide),
        (shape(spectral.shape, F32),) * 4 + (shape(spectral.shape, BF),),
        (spec, grad_mixed, spectral, spec_m, fourier_variance_moment, spec_ema),
        [
            pltpu.VMEM((modes, wide, LANES), F32),
            pltpu.VMEM((2, modes * wide // 2, LANES), F32),
        ],
        name="spectral",
    )
    if tiled:
        send, *big = together(send, *big)
    got = exchange(send, AXES)
    big_sum = scatter_tiles_third(*big) if tiled else scatter_rows(big[0], rows)
    query_total = jnp.sum(got[:, :chans, :wide].reshape(n_data, n_mode, chans, wide), axis=1)
    query_total = query_total.transpose(1, 0, 2).reshape(chans, D)
    down_total = got[:, :chans, 64 : 64 + share].transpose(1, 0, 2).reshape(chans, FF)
    spec_norm = SPECTRAL_WEIGHT / (total * M * S)
    loss = jnp.sum(got[:, 8, 0]) / steps_total + spec_norm * jnp.sum(got[:, 9, 0])

    up = lambda x: x.astype(F32)
    dense_sum = jnp.concatenate(
        [
            exact("rc,ce->re", up(e_rows), query_total),
            big_sum,
            exact("rc,cf->rf", up(h_rows), down_total),
            embed_own + exact("re,ce->rc", up(q_rows), query_total),
            head_own + exact("rf,cf->rc", up(d_rows), down_total),
        ],
        axis=1,
    )
    dense_out = adamw(dense, dense_sum, dense_m, dense_v, dense_ema, RATE_DENSE)
    return (loss,) + tuple(dense_out) + tuple(spec_out)


def solution(mesh):
    rows = P(("dp", "mode"), None)
    mixing = P(None, "mode", "dp")
    return jax.shard_map(
        per_device,
        mesh=mesh,
        in_specs=(P("mode", "dp", None), P("mode", "dp", None), P("mode", "dp"), P())
        + (rows,) * 4
        + (mixing,) * 4,
        out_specs=(P(),) + (rows,) * 5 + (mixing,) * 5,
        check_vma=False,
    )
```

```python
import math
from functools import partial

import jax
import jax.numpy as jnp
from jax import lax
from jax.experimental import pallas as pl
from jax.experimental.pallas import tpu as pltpu
from jax.sharding import PartitionSpec as P

D = 512
H = 8
E = 64
FF = 2048
M = 64
C = 7
S = 768
LANES = 128

SPECTRAL_WEIGHT = 0.5
RATE_DENSE = 0.02
RATE_SPEC = 0.1
BF = jnp.bfloat16
F32 = jnp.float32
AXES = ("dp", "mode")
SLOPE = jnp.bfloat16
VMEM_BYTES = 60 * 1024 * 1024
FULL_BYTES = 60 * 1024 * 1024
SMALL_BYTES = 16 * 1024 * 1024


def plain(spec, left, right):
    return jnp.einsum(spec, left, right, preferred_element_type=F32)


def exact(spec, left, right):
    return jnp.einsum(
        spec, left, right, precision=lax.Precision.HIGHEST, preferred_element_type=F32
    )


def tables(mode_index):
    steps = jnp.arange(S, dtype=jnp.int32)
    phase = mode_index[:, None] * steps[None, :] % S
    angle = phase.astype(F32) * (2.0 * math.pi / S)
    return (jnp.cos(angle), jnp.sin(angle))


def unpack(whole):
    return (
        whole[:, :D],
        whole[:, D : 2 * D],
        whole[:, 2 * D : 2 * D + FF],
        whole[:, 2 * D + FF : 2 * D + 2 * FF],
        whole[:, 2 * D + 2 * FF : 2 * D + 2 * FF + C],
        whole[:, 2 * D + 2 * FF + C :],
    )


def adamw(weight, grad, first, second, average, rate):
    first_new = 0.5 * first + 0.5 * grad
    second_new = 0.5 * second + 0.5 * grad * grad
    weight_new = weight - rate * (first_new / (jnp.sqrt(second_new) + 1e-08) + 0.01 * weight)
    average_new = 0.9 * average + 0.1 * weight_new
    return (weight_new, first_new, second_new, average_new, weight_new.astype(BF))


def halves(x):
    high = x.astype(BF)
    return high, (x - high.astype(F32)).astype(BF)


def fill(x, size, axis):
    wanted = list(x.shape)
    wanted[axis] = size - x.shape[axis]
    return jnp.concatenate([x, jnp.zeros(wanted, x.dtype)], axis=axis) if wanted[axis] else x


def exchange(x, axes):
    return lax.all_to_all(x, axes, 0, 0, tiled=True)


def partners(step):
    count = lax.axis_size("mode")
    return [(index, index ^ step) for index in range(count)]


def bit_of(step):
    return lax.div(lax.axis_index("mode"), step) % 2


def steps_of_mode():
    return [1 << bit for bit in range(lax.axis_size("mode").bit_length() - 1)]


def by_xor(x, axis, step):
    count = lax.axis_size(axis)
    return lax.ppermute(x, axis, [(index, index ^ step) for index in range(count)])


def tile_offsets(n_data):
    cut = n_data // 4
    low = [2 * step for step in range(cut)]
    high = [2 * step for step in range(cut, 2 * cut)]
    ones = lambda data: [index + 1 for index in data]
    offsets = [
        (low + ones(low), [0] * 2 * cut),
        (low + ones(low), [2] * 2 * cut),
        (high + high, [0] * cut + [2] * cut),
        (ones(high) + ones(high), [0] * cut + [2] * cut),
    ]
    return offsets + [(data, [index + 1 for index in mode]) for data, mode in offsets]


def gather_tiles_first(x):
    n_data = lax.axis_size("dp")
    deep = [x] + [by_xor(x, "dp", 2 * step) for step in range(1, n_data // 2)]
    cut = len(deep) // 2
    return jnp.stack(deep[:cut]), jnp.stack(deep[cut:])


def gather_tiles_second(first, second):
    first = jnp.concatenate([first, by_xor(first, "dp", 1)])
    return first, jnp.concatenate([second, by_xor(second, "mode", 2)])


def gather_tiles_third(first, second):
    return [first, by_xor(first, "mode", 2), second, by_xor(second, "dp", 1)]


def gather_tiles_last(pieces):
    return pieces + [by_xor(piece, "mode", 1) for piece in pieces]


def tile_order(n_data):
    cut = n_data // 4
    low = [2 * step for step in range(cut)]
    high = [2 * step for step in range(cut, 2 * cut)]
    groups = [
        [(data + x, 2) for data in low for x in (0, 1)],
        [(data + x, 0) for data in low for x in (0, 1)],
        [(data + 1, 2 * y) for data in high for y in (0, 1)],
        [(data, 2 * y) for data in high for y in (0, 1)],
    ]
    return [[(data, mode + core) for data, mode in group] for core in (1, 0) for group in groups]


def together(*values):
    return lax.optimization_barrier(values)


def total_of(terms, pick):
    return sum(term[pick].astype(F32) for term in terms)


def scatter_tiles_first(away, stay):
    terms = [stay, by_xor(away, "mode", 1)]
    first = by_xor(total_of(terms, 0).astype(BF), "mode", 2)
    second = by_xor(total_of(terms, 2).astype(BF), "dp", 1)
    return [terms[0], terms[1], first, second]


def scatter_tiles_second(stay, come, first, second):
    pairs = lambda terms: [x.reshape((x.shape[0] // 2, 2) + x.shape[1:]) for x in terms]
    first = pairs([stay[1], come[1], first])
    second = pairs([stay[3], come[3], second])
    halves = (slice(None), 1)
    return [
        [x[:, 0] for x in first] + [by_xor(total_of(first, halves).astype(BF), "dp", 1)],
        [x[:, 0] for x in second] + [by_xor(total_of(second, halves).astype(BF), "mode", 2)],
    ]


def scatter_tiles_third(first, second):
    cut = first[0].shape[0]
    come = []
    for step in range(1, 2 * cut):
        terms, at = (first, step) if step < cut else (second, step - cut)
        come.append(by_xor(total_of(terms, at).astype(BF), "dp", 2 * step))
    return [total_of(first, 0)] + come


def gather_rows(x):
    n_data = lax.axis_size("dp")
    held = exchange(jnp.broadcast_to(x[None], (n_data,) + x.shape), "dp")[:, None]
    for step in reversed(steps_of_mode()):
        other = lax.ppermute(held, "mode", partners(step))
        first = bit_of(step) == 0
        pair = [jnp.where(first, held, other), jnp.where(first, other, held)]
        held = jnp.concatenate(pair, axis=1) if step > 1 else jnp.stack(pair, axis=2)
    return held.reshape(-1, x.shape[1])


def scatter_rows(x, rows):
    n_data, n_mode = lax.axis_size("dp"), lax.axis_size("mode")
    held = x.reshape(n_data, n_mode, rows, x.shape[1])
    for step in steps_of_mode():
        held = held.reshape(n_data, held.shape[1] // 2, 2, rows, x.shape[1])
        bit = bit_of(step)
        away = lax.dynamic_index_in_dim(held, 1 - bit, 2, keepdims=False)
        stay = lax.dynamic_index_in_dim(held, bit, 2, keepdims=False)
        other = lax.ppermute(away, "mode", partners(step))
        held = (stay.astype(F32) + other.astype(F32)).astype(BF)
    held = exchange(held.reshape(n_data, rows, x.shape[1]), "dp")
    return jnp.sum(held.astype(F32), axis=0)


NN = (((1,), (0,)), ((), ()))
NT = (((1,), (1,)), ((), ()))
TN = (((0,), (0,)), ((), ()))
FIRST = 2.0 * math.sqrt(2.0 / math.pi)
THIRD = FIRST * 0.044715
GATES = 512
UNROLL = 4
LEAD = 8
HALF = 64


def mm(left, right, dims=NN):
    return lax.dot_general(left, right, dims, preferred_element_type=F32)


def iota(shape, axis):
    return lax.broadcasted_iota(jnp.int32, shape, axis)


def split(x):
    high = x.astype(BF).astype(F32)
    return high, x - high


def by_halves(x):
    high, low = split(x)
    return jnp.where(iota(x.shape, 1) < HALF, high, low).astype(BF)


def fold(x):
    return x + pltpu.roll(x, HALF, 1)


def rows_at(x, first, count):
    parts = []
    if first:
        parts.append(jnp.zeros((first, x.shape[1]), F32))
    parts.append(x)
    if count - first - x.shape[0]:
        parts.append(jnp.zeros((count - first - x.shape[0], x.shape[1]), F32))
    return jnp.concatenate(parts, axis=0)


def row_groups(x):
    return sum(x[at : at + LEAD] for at in range(0, x.shape[0], LEAD))


def block_kernel(sizes, count_ref, me_ref, *refs):
    if len(sizes) == 4:
        block_steps(sizes, lambda what: None, count_ref, *refs)
        return
    n_data, n_mode = sizes[:2]
    rows = D // n_data // n_mode
    offsets = tile_offsets(n_data)
    n_pieces = len(offsets)
    pieces, got_ref, sources, refs = refs[:n_pieces], refs[n_pieces], refs[n_pieces + 1 : n_pieces + 7], refs[n_pieces + 7 :]
    send_ref, stat_ref, away_ref, stay_ref, row_sems, sems, w_ref = refs[:7]
    places, scratch = refs[7:13], refs[13:]
    act_ref = scratch[5]

    def rows_of(data, mode):
        owner = (me_ref[0] ^ data) * n_mode + (me_ref[1] ^ mode)
        return pl.ds(pl.multiple_of(owner * rows, rows), rows)

    row_copies = []
    for ref, (data, mode) in zip(pieces, offsets, strict=True):
        for at, (one, two) in enumerate(zip(data, mode, strict=True)):
            place = w_ref.at[rows_of(one, two), :]
            row_copies.append(
                pltpu.make_async_copy(ref.at[at], place, row_sems.at[len(row_copies)])
            )
            row_copies[-1].start()
    copies = [
        pltpu.make_async_copy(source, place, sems.at[at])
        for at, (source, place) in enumerate(zip(sources, places, strict=True))
    ]
    for copy in copies:
        copy.start()
    waits = {"rows": row_copies, "a": copies[:1], "rest": copies[1:]}

    def ready(what):
        for copy in waits[what]:
            copy.wait()

    block_steps(sizes, ready, count_ref, w_ref, got_ref, *places, send_ref, stat_ref, None, *scratch)
    for at, group in enumerate(tile_order(n_data)):
        ref = away_ref if at < 4 else stay_ref
        for index, (data, mode) in enumerate(group):
            ref[at % 4, index, :, :D] = act_ref[1, rows_of(data, mode), :D]
            ref[at % 4, index, :, D:] = act_ref[0, rows_of(data, mode), :]


def block_steps(
    sizes,
    ready,
    count_ref,
    w_ref,
    got_ref,
    a_ref,
    at_ref,
    rest_ref,
    rest_t_ref,
    target_ref,
    keep_ref,
    send_ref,
    stat_ref,
    big_ref,
    wdup_ref,
    x_ref,
    v_ref,
    r_ref,
    wd_ref,
    act_ref,
    slope_ref,
    fc_ref,
    zx_ref,
    j_ref,
):
    n_data, n_mode, nb, total = sizes[:4]
    n_all = n_data * n_mode
    modes = M // n_mode
    nbm = nb * modes
    share = FF // n_all
    rows = D // n_all
    scale = 2.0 / S
    norm = SPECTRAL_WEIGHT / (total * M * S)
    chunks = FF // GATES

    for i in range(n_data):
        blocks = [got_ref[i * n_mode + j, :nbm, :].astype(F32) for j in range(n_mode)]
        for k in range(nb):
            column = [block[k * modes : (k + 1) * modes] for block in blocks]
            x_ref[k * M : (k + 1) * M, i * LANES : (i + 1) * LANES] = jnp.concatenate(
                column, axis=0
            ).astype(BF)

    per = LANES // share
    for at in range(FF // LANES):
        block = jnp.zeros((16, LANES), F32)
        for q in range(per):
            piece = got_ref[at * per + q, nbm : nbm + 16, :].astype(F32)
            piece = pltpu.roll(piece, q * share, 1) if q else piece
            block = jnp.where(iota(block.shape, 1) // share == q, piece, block)
        spread = [
            rows_at(jnp.concatenate([half] * nb, axis=0), 0, HALF)
            for half in (block[:LEAD], block[LEAD:])
        ]
        wd_ref[:, at * LANES : (at + 1) * LANES] = jnp.concatenate(spread, axis=0).astype(BF)
    ready("rows")
    for i in range(n_data):
        head = i * H // n_data
        block = w_ref[head * E : (head + 1) * E, :D]
        wdup_ref[2 * i * E : (2 * i + 1) * E, :] = block
        wdup_ref[(2 * i + 1) * E : (2 * i + 2) * E, :] = block
    x_all = x_ref[...]
    real_lane = iota(x_all.shape, 1) % LANES < HALF
    zero = jnp.zeros_like(x_all)
    x_real = jnp.where(real_lane, x_all, zero)
    x_imag = jnp.where(real_lane, zero, x_all)
    line_real = scale * mm(x_real, wdup_ref[...])
    line_imag = scale * mm(x_imag, wdup_ref[...])
    for k in range(nb):
        v_ref[2 * k * M : (2 * k + 1) * M, :] = line_real[k * M : (k + 1) * M].astype(BF)
        v_ref[(2 * k + 1) * M : (2 * k + 2) * M, :] = line_imag[k * M : (k + 1) * M].astype(BF)

    thin_t = w_ref[:, D + FF :].astype(F32).T
    embed_t = thin_t[:LEAD]
    head_t = thin_t[LEAD : 2 * LEAD]
    pad = [jnp.zeros((HALF - nb * LEAD, D), F32)] if nb * LEAD < HALF else []
    embed_all = jnp.concatenate([embed_t] * nb + pad, axis=0).astype(BF)
    head_all = jnp.concatenate([head_t] * nb + pad, axis=0).astype(BF)
    head_twice = jnp.concatenate([head_all, head_all], axis=0)
    embed_twice = jnp.concatenate([embed_t, embed_t], axis=0).astype(BF)

    for c in range(FF // 512):
        cols = slice(c * 512, (c + 1) * 512)
        w_up = w_ref[:, D + c * 512 : D + (c + 1) * 512]
        lifted = mm(v_ref[...], w_up)
        thin = mm(embed_twice, w_up)[:LEAD]
        high, low = split(thin)
        for k in range(nb):
            r_ref[k, : 2 * M, cols] = lifted[2 * k * M : 2 * (k + 1) * M].astype(BF)
            r_ref[k, 2 * M :, cols] = jnp.concatenate(
                [rows_at(high, k * LEAD, HALF), rows_at(low, k * LEAD, HALF)], axis=0
            ).astype(BF)

    parts = [mm(head_all[:16], v_ref[2 * k * M : 2 * (k + 1) * M, :], NT)[:LEAD] for k in range(nb)]
    by_head = rows_at(jnp.concatenate(parts, axis=0), 0, HALF)
    cross = mm(head_all, jnp.concatenate([embed_all, jnp.zeros_like(embed_all)], axis=0), NT)
    cross = jnp.where(iota(cross.shape, 0) // LEAD == iota(cross.shape, 1) // LEAD, cross, 0.0)
    high, low = split(jnp.concatenate([by_head, cross], axis=1))
    by_head = jnp.concatenate([high, low], axis=0).astype(BF)
    ready("a")
    fc_ref[...] = mm(a_ref[...], by_head, NT)

    own_lane = iota((S, LANES), 1) % HALF // LEAD

    def forward(step, carry):
        k = step // chunks
        cols = pl.ds(pl.multiple_of(step % chunks * GATES, GATES), GATES)
        gate = mm(a_ref[...], r_ref[k, :, cols])
        square = gate * gate
        sig = 0.5 * jnp.tanh(gate * (square * (0.5 * THIRD) + 0.5 * FIRST)) + 0.5
        act = gate * sig
        low = act.astype(BF)
        act_ref[k, :, cols] = low
        slope = sig + act * (1.0 - sig) * (square * (3.0 * THIRD) + FIRST)
        slope_ref[k, :, cols] = slope.astype(slope_ref.dtype)
        fc_ref[...] += jnp.where(own_lane == k, mm(low, wd_ref[:, cols], NT), 0.0)
        return carry

    lax.fori_loop(0, nb * chunks, forward, 0, unroll=UNROLL)

    ready("rest")
    keep = keep_ref[...]
    masked = keep * (fold(fc_ref[...]) - target_ref[...])
    two = by_halves(masked)
    err = fold(mm(at_ref[: 2 * M, :], two) + mm(rest_ref[...], two))
    stat_ref[...] = jnp.concatenate(
        [
            jnp.full((1, LANES), 0.5 * jnp.sum(masked * masked)),
            jnp.full((1, LANES), 0.5 * jnp.sum(err * err)),
            jnp.zeros((6, LANES), F32),
        ],
        axis=0,
    )
    two = by_halves(err)
    back = fold(mm(a_ref[:, : 2 * M], two) + mm(rest_t_ref[...], two))
    g_fc = keep * ((2.0 / count_ref[0]) * masked + (2.0 * norm) * back)
    g_low = g_fc.astype(BF)
    g_turn = g_fc.T[:HALF].astype(BF)
    zx_ref[...] = jnp.zeros_like(zx_ref)
    j_ref[...] = jnp.zeros_like(j_ref)

    def backward(step, carry):
        k = step // chunks
        cols = pl.ds(pl.multiple_of(step % chunks * GATES, GATES), GATES)
        fed = mm(jnp.where(own_lane == k, g_fc, 0.0).astype(BF), wd_ref[:, cols])
        g_gate = (fed * slope_ref[k, :, cols].astype(F32)).astype(BF)
        turned = mm(at_ref[...], g_gate)
        r_ref[k, : 2 * M, cols] = turned[: 2 * M].astype(BF)
        own = iota((HALF, GATES), 0) // LEAD == k
        zx_ref[:, cols] += jnp.where(own, turned[2 * M :], 0.0)
        j_ref[:, cols] += jnp.where(own, mm(g_turn, act_ref[k, :, cols]), 0.0)
        return carry

    lax.fori_loop(0, nb * chunks, backward, 0, unroll=UNROLL)

    back_fc = by_halves(mm(at_ref[...], g_low))
    lane_of = iota((2 * M, LANES), 1) % HALF // LEAD
    nothing = jnp.zeros((2 * M, LANES), F32)
    back_rows = jnp.concatenate(
        [jnp.where(lane_of == k, back_fc[: 2 * M].astype(F32), nothing) for k in range(nb)], axis=0
    ).astype(BF)
    cross = jnp.where(
        iota((HALF, LANES), 0) // LEAD == iota((HALF, LANES), 1) % HALF // LEAD,
        back_fc[2 * M :].astype(F32),
        0.0,
    ).astype(BF)
    v_all = v_ref[...]
    z_all = r_ref[:, : 2 * M, :].reshape(nb * 2 * M, FF)
    high, low = split(row_groups(zx_ref[...]))
    zx = jnp.concatenate([high, low], axis=0).astype(BF)
    w_up = w_ref[:, D : D + FF]
    back_block = mm(z_all, w_up, NT) + mm(back_rows, head_twice)
    turned = (scale * back_block).astype(BF)
    embed_grad = row_groups(mm(zx, w_up, NT)) + row_groups(mm(cross, head_twice))
    head_grad = row_groups(mm(back_rows, v_all, TN)) + row_groups(mm(cross, embed_all, TN))
    down_grad = row_groups(j_ref[...])

    turned_real = jnp.concatenate(
        [turned[2 * k * M : (2 * k + 1) * M] for k in range(nb)], axis=0
    )
    turned_imag = jnp.concatenate(
        [turned[(2 * k + 1) * M : (2 * k + 2) * M] for k in range(nb)], axis=0
    )
    p_real = mm(turned_real, wdup_ref[...], NT)
    p_imag = mm(turned_imag, wdup_ref[...], NT)
    real_lane = iota((modes, LANES), 1) < HALF
    lane = iota((LEAD, LANES), 1)
    for i in range(n_data):
        cols = slice(i * LANES, (i + 1) * LANES)
        for j in range(n_mode):
            d = i * n_mode + j
            pieces = []
            for k in range(nb):
                at = slice(k * M + j * modes, k * M + (j + 1) * modes)
                pieces.append(jnp.where(real_lane, p_real[at, cols], p_imag[at, cols]))
            send_ref[d, :nbm, :] = jnp.concatenate(pieces, axis=0).astype(BF)
            out = jnp.zeros((LEAD, LANES), F32)
            for source, width, place in (
                (down_grad, share, 0),
                (embed_grad, rows, HALF),
                (head_grad, rows, HALF + rows),
            ):
                first = d * width // LANES * LANES
                piece = source[:, first : first + LANES]
                shift = (place - (d * width - first)) % LANES
                piece = pltpu.roll(piece, shift, 1) if shift else piece
                out = jnp.where((lane >= place) & (lane < place + width), piece, out)
            high, low = split(out)
            send_ref[d, nbm:, :] = jnp.concatenate([high, low], axis=0).astype(BF)

    x_all = x_ref[...]
    real_lane = iota(x_all.shape, 1) % LANES < HALF
    x_real = jnp.where(real_lane, x_all, zero)
    x_imag = jnp.where(real_lane, zero, x_all)
    out_grad = mm(x_real, turned_real, TN) + mm(x_imag, turned_imag, TN)
    each = n_data // H
    for head in range(H):
        block = 0.0
        for i in range(head * each, (head + 1) * each):
            block += out_grad[2 * i * E : (2 * i + 1) * E] + out_grad[(2 * i + 1) * E : (2 * i + 2) * E]
        out = act_ref.at[1] if big_ref is None else big_ref
        out[head * E : (head + 1) * E, :D] = block.astype(BF)
    for c in range(FF // 512):
        cols = slice(c * 512, (c + 1) * 512)
        up_grad = mm(v_all, z_all[:, cols], TN) + mm(embed_twice, zx[:, cols], TN)
        if big_ref is None:
            act_ref[0, :D, cols] = up_grad.astype(BF)
        else:
            big_ref[:, D + c * 512 : D + (c + 1) * 512] = up_grad.astype(BF)


def block(count, me, weights, ins, sizes):
    n_data, n_mode, nb = sizes[:3]
    tiled = len(sizes) > 4
    whole = pl.BlockSpec(memory_space=pltpu.VMEM)
    far = pl.BlockSpec(memory_space=pl.ANY if tiled else pltpu.VMEM)
    big = [jax.ShapeDtypeStruct((D, D + FF), BF)]
    scratch = []
    if tiled:
        half = (4, n_data * n_mode // 8, D // n_data // n_mode, D + FF)
        big = [jax.ShapeDtypeStruct(half, BF)] * 2
        scratch = [
            pltpu.SemaphoreType.DMA((n_data * n_mode,)),
            pltpu.SemaphoreType.DMA((6,)),
            pltpu.VMEM((D, D + FF + LANES), BF),
        ]
        scratch += [pltpu.VMEM(x.shape, x.dtype) for x in ins[1:]]
    return pl.pallas_call(
        partial(block_kernel, sizes),
        out_shape=(
            jax.ShapeDtypeStruct(ins[0].shape, BF),
            jax.ShapeDtypeStruct((8, LANES), F32),
            *big,
        ),
        in_specs=[pl.BlockSpec(memory_space=pltpu.SMEM)] * 2
        + [far] * len(weights)
        + [whole]
        + [far] * (len(ins) - 1),
        out_specs=(whole,) * (2 + len(big)),
        scratch_shapes=scratch
        + [
            pltpu.VMEM((2 * n_data * E, D), BF),
            pltpu.VMEM((nb * M, n_data * LANES), BF),
            pltpu.VMEM((nb * 2 * M, D), BF),
            pltpu.VMEM((nb, 4 * M, FF), BF),
            pltpu.VMEM((LANES, FF), BF),
            pltpu.VMEM((nb, S, FF), BF),
            pltpu.VMEM((nb, S, FF), SLOPE),
            pltpu.VMEM((S, LANES), F32),
            pltpu.VMEM((HALF, FF), F32),
            pltpu.VMEM((HALF, FF), F32),
        ],
        compiler_params=pltpu.CompilerParams(vmem_limit_bytes=VMEM_BYTES),
        name="block",
    )(count, me, *weights, *ins)


def at_lane(x, first, width):
    x = pltpu.roll(x, first, 1) if first else x
    lane = iota(x.shape, 1)
    return jnp.where((lane >= first) & (lane < first + width), x, 0.0)


def from_lane(x, first, width):
    base = first // LANES * LANES
    x = x[:, base : base + LANES]
    shift = (LANES - (first - base)) % LANES
    x = pltpu.roll(x, shift, 1) if shift else x
    return jnp.where(iota(x.shape, 1) < width, x, 0.0)


def staged(kernel, ahead, *refs):
    sems = refs[-1]
    n_held = len(refs) - 1 - len(ahead)
    held = list(refs[:n_held])
    copies = []
    for at, (index, place) in enumerate(zip(ahead, refs[n_held:-1], strict=True)):
        copies.append(pltpu.make_async_copy(refs[index], place, sems.at[at]))
        copies[-1].start()
        held[index] = place

    def ready():
        for copy in copies:
            copy.wait()

    kernel(ready, *held)


def call(kernel, outs, ins, scratch=(), name=None, cost=0, ahead=()):
    whole = pl.BlockSpec(memory_space=pltpu.VMEM)
    in_specs = [whole] * len(ins)
    scratch = list(scratch)
    if ahead:
        kernel = partial(staged, kernel, ahead)
        for index in ahead:
            in_specs[index] = pl.BlockSpec(memory_space=pl.ANY)
            scratch.append(pltpu.VMEM(ins[index].shape, ins[index].dtype))
        scratch.append(pltpu.SemaphoreType.DMA((len(ahead),)))
    return pl.pallas_call(
        kernel,
        out_shape=outs,
        in_specs=in_specs,
        out_specs=jax.tree.map(lambda _: whole, outs),
        scratch_shapes=scratch,
        compiler_params=pltpu.CompilerParams(vmem_limit_bytes=FULL_BYTES if ahead else SMALL_BYTES),
        name=name,
        cost_estimate=pl.CostEstimate(flops=cost, bytes_accessed=cost // 10, transcendentals=0)
        if cost
        else None,
    )(*ins)


def thin_rows(dense_ref):
    thin = dense_ref[:, 2 * D + 2 * FF :]
    thin = jnp.concatenate([thin, jnp.zeros((thin.shape[0], LANES - 2 * C), F32)], axis=1)
    return at_lane(thin, 0, C) + at_lane(from_lane(thin, C, C), LEAD, C)


def pack_kernel(sizes, ready, series_ref, future_ref, mask_ref, dense_ref, send_ref, rows_ref, one_ref, two_ref):
    n_mode, nb = sizes[1:3]
    ready()
    one_ref[...] = series_ref[...].astype(F32)
    two_ref[...] = mask_ref[...].astype(F32)
    for j in range(n_mode):
        for k in range(nb):
            b = j * nb + k
            for c in range(C):
                send_ref[j, k * LEAD + c, :] = one_ref[c, b, :]
                send_ref[j, (nb + k) * LEAD + c, :] = future_ref[c, b, :]
            send_ref[j, k * LEAD + C, :] = two_ref[b, :]
            send_ref[j, (nb + k) * LEAD + C, :] = jnp.zeros_like(two_ref[b, :])
    rows_ref[:, : D + FF] = dense_ref[:, D : 2 * D + FF].astype(BF)
    rows_ref[:, D + FF :] = thin_rows(dense_ref).astype(BF)


def own_rows(got_ref, all_ref):
    steps = got_ref.shape[2]
    for j in range(got_ref.shape[0]):
        all_ref[:, j * steps : (j + 1) * steps] = got_ref[j]
    half = all_ref.shape[0] // 2
    inputs = all_ref[:half, :]
    mask = inputs
    inputs = jnp.where(iota(inputs.shape, 0) % LEAD == C, 0.0, inputs)
    return inputs, mask, all_ref[half:, :]


def spectra_kernel(sizes, got_ref, cos_ref, sin_ref, dense_ref, send_ref, all_ref):
    n_data, n_mode, nb, _ = sizes
    n_all = n_data * n_mode
    modes = M // n_mode
    wide = D // n_data
    share = FF // n_all
    x, mask, _ = own_rows(got_ref, all_ref)
    count = jnp.sum(jnp.where(iota(mask.shape, 0) % LEAD == C, mask, 0.0))
    low = cos_ref[...].astype(BF)
    inner = mm(low, rows_at(x, 0, LANES).astype(BF), NT)
    low = (-sin_ref[...]).astype(BF)
    inner += mm(low, rows_at(x, nb * LEAD, LANES).astype(BF), NT)
    thin = thin_rows(dense_ref).astype(BF)
    query = mm(thin, dense_ref[:, :D].astype(BF), TN)[:LEAD]
    down = mm(thin, dense_ref[:, 2 * D + FF : 2 * D + 2 * FF].astype(BF), TN)[LEAD : 2 * LEAD]
    row = iota((LEAD, LANES), 0)
    lane = iota((LEAD, LANES), 1)
    for i in range(n_data):
        ours = at_lane(from_lane(query, i * wide, wide), HALF, wide)
        ours = jnp.where((row == C) & (lane == HALF), count, ours)
        for j in range(n_mode):
            d = i * n_mode + j
            block = inner[j * modes : (j + 1) * modes]
            if modes < 16:
                block = jnp.concatenate([block, jnp.zeros((16 - modes, LANES), F32)], axis=0)
            theirs = at_lane(from_lane(down, d * share, share), HALF, share)
            send_ref[d] = block + jnp.concatenate([ours, theirs], axis=0)


def tables_kernel(
    got_ref, cos_ref, sin_ref, a_ref, at_ref, rest_ref, rest_t_ref, target_ref, keep_ref, all_ref
):
    x, mask, target = own_rows(got_ref, all_ref)
    count = x.shape[0]
    keep = [
        jnp.broadcast_to(mask[at + C : at + LEAD], (LEAD, S)) for at in range(0, count, LEAD)
    ]
    keep = jnp.concatenate(keep, axis=0)
    twice = lambda rows: jnp.concatenate([rows_at(rows, 0, HALF)] * 2, axis=0).T
    a_ref[:, 2 * M :] = twice(x).astype(BF)
    at_ref[2 * M :, :] = rows_at(x, 0, HALF).astype(BF)
    target_ref[...] = twice(target)
    keep_ref[...] = twice(keep)
    basis = jnp.concatenate([cos_ref[...], -sin_ref[...]], axis=0)
    low = basis.astype(BF)
    at_ref[: 2 * M, :] = low
    rest_ref[...] = (basis - low.astype(F32)).astype(BF)
    turned = basis.T
    low = turned.astype(BF)
    a_ref[:, : 2 * M] = low
    rest_t_ref[...] = (turned - low.astype(F32)).astype(BF)


def mix_kernel(sizes, got_ref, mixer_ref, send_ref, spec_ref, thin_ref, wide_ref, out_ref):
    n_data, n_mode, nb, _ = sizes
    n_all = n_data * n_mode
    modes = M // n_mode
    nbm = nb * modes
    wide = D // n_data
    share = FF // n_all
    got = got_ref[...]
    thin = jnp.sum(got, axis=0)
    thin_ref[...] = thin
    query = from_lane(thin[:LEAD], HALF, wide)
    query = jnp.where(iota(query.shape, 0) < C, query, 0.0)
    down = from_lane(thin[LEAD:], HALF, share)
    high, low = split(down)
    down = jnp.concatenate([high, low], axis=0).astype(BF)
    spread = []
    for part in range(2):
        block = at_lane(query, part * wide, wide)
        zero = jnp.zeros_like(block)
        for k in range(nb):
            blocks = [block if g == k else zero for g in range(nb)]
            spread.append(jnp.concatenate(blocks, axis=1))
    spread = jnp.concatenate(spread, axis=0)
    inner = got.reshape(n_all * 16, LANES)[:, : 2 * nb * LEAD]
    spec = lax.dot_general(
        inner, spread, NN, precision=lax.Precision.HIGHEST, preferred_element_type=F32
    )
    for k in range(nb):
        wide_ref[k] = spec[:, k * LANES : (k + 1) * LANES]
    for m in range(modes):
        spec = [wide_ref[k, pl.ds(m, n_all, stride=16), :][:, : 2 * wide] for k in range(nb)]
        spec = jnp.concatenate(spec, axis=0).astype(BF)
        spec_ref[m] = spec
        mixed = mm(spec, mixer_ref[m])
        for k in range(nb):
            out_ref[pl.ds(k * modes + m, n_all, stride=nbm), :] = mixed[
                k * n_all : (k + 1) * n_all
            ]
    for d in range(n_all):
        send_ref[d, :nbm, :] = out_ref[d * nbm : (d + 1) * nbm, :].astype(BF)
        send_ref[d, nbm:, :] = down


def mix_back_kernel(
    sizes, got_ref, mixer_ref, first_ref, stat_ref, send_ref, grad_ref, thin_ref, in_ref, wide_ref
):
    n_data, n_mode, nb, _ = sizes
    n_all = n_data * n_mode
    modes = M // n_mode
    nbm = nb * modes
    wide = D // n_data
    share = FF // n_all
    thin = jnp.zeros((16, LANES), F32)
    for d in range(n_all):
        in_ref[d * nbm : (d + 1) * nbm, :] = got_ref[d, :nbm, :].astype(F32)
        thin += got_ref[d, nbm:, :].astype(F32)
    thin = thin[:LEAD] + thin[LEAD:]
    thin_ref[...] = thin
    if modes < 16:
        wide_ref[...] = jnp.zeros_like(wide_ref)
    for m in range(modes):
        grad = [in_ref[pl.ds(k * modes + m, n_all, stride=nbm), :] for k in range(nb)]
        grad = jnp.concatenate(grad, axis=0).astype(BF)
        grad_ref[m] = grad
        back = mm(grad, mixer_ref[m], NT).astype(BF).astype(F32)
        if 2 * wide < LANES:
            back = jnp.concatenate(
                [back, jnp.zeros((back.shape[0], LANES - 2 * wide), F32)], axis=1
            )
        for k in range(nb):
            wide_ref[k, pl.ds(m, n_all, stride=16), :] = back[k * n_all : (k + 1) * n_all]
    inner = first_ref[...].reshape(n_all * 16, LANES)
    inner = jnp.where(iota(inner.shape, 1) < HALF, inner, 0.0)
    inner = by_halves(fold(inner))
    total = jnp.zeros((LEAD, LANES), F32)
    for k in range(nb):
        query = mm(inner, wide_ref[k].astype(BF), TN)
        query = query[:HALF] + query[HALF:]
        for part in range(2):
            at = (part * nb + k) * LEAD
            total += from_lane(query[at : at + LEAD], part * wide, wide)
    block = total + at_lane(from_lane(thin, 0, share), HALF, share)
    block = jnp.concatenate([block, stat_ref[...]], axis=0)
    for d in range(n_all):
        send_ref[d] = block


def spectral_kernel(
    modes,
    wide,
    ready,
    spec_ref,
    grad_ref,
    w_ref,
    m_ref,
    v_ref,
    ema_ref,
    w_out,
    m_out,
    v_out,
    ema_out,
    low_out,
    pair_ref,
    turn_ref,
):
    ready()
    lower = iota((wide, LANES), 1) < HALF
    half_lower = iota((wide // 2, LANES), 1) < HALF
    for m in range(modes):
        slopes = mm(spec_ref[m], grad_ref[m], TN)
        other = pltpu.roll(slopes[wide:], HALF, 1)
        pair_ref[m] = jnp.where(lower, slopes[:wide] + other, slopes[:wide] - other)
        even = pair_ref[m, pl.ds(0, wide // 2, stride=2), :]
        odd = pair_ref[m, pl.ds(1, wide // 2, stride=2), :]
        real = jnp.where(half_lower, even, pltpu.roll(odd, HALF, 1))
        imag = jnp.where(half_lower, pltpu.roll(even, HALF, 1), odd)
        turn_ref[0, pl.ds(m, wide // 2, stride=modes), :] = real
        turn_ref[1, pl.ds(m, wide // 2, stride=modes), :] = imag
    for part in range(2):
        for at in range(wide // 2):
            cols = slice(at * LANES, (at + 1) * LANES)
            grad = turn_ref[part, at * modes : (at + 1) * modes, :]
            new = adamw(
                w_ref[part, :, cols],
                grad,
                m_ref[part, :, cols],
                v_ref[part, :, cols],
                ema_ref[part, :, cols],
                RATE_SPEC,
            )
            for ref, value in zip((w_out, m_out, v_out, ema_out, low_out), new, strict=True):
                ref[part, :, cols] = value


def rows_kernel(
    sizes,
    n_big,
    got_ref,
    thin_ref,
    steps_ref,
    w_ref,
    m_ref,
    v_ref,
    ema_ref,
    *refs,
):
    big_refs, (loss_ref, w_out, m_out, v_out, ema_out, low_out) = refs[:n_big], refs[n_big:]
    n_data, n_mode, _, total = sizes
    n_all = n_data * n_mode
    wide = D // n_data
    share = FF // n_all
    rows = w_ref.shape[0]
    query = []
    for at in range(D // LANES):
        block = jnp.zeros((LEAD, LANES), F32)
        for i in range(at * LANES // wide, (at + 1) * LANES // wide):
            part = sum(got_ref[i * n_mode + j, :LEAD, :] for j in range(n_mode))
            block += at_lane(part, i * wide % LANES, wide)
        query.append(block)
    query = jnp.concatenate(query, axis=1)
    down = []
    for at in range(FF // LANES):
        block = jnp.zeros((LEAD, LANES), F32)
        for d in range(at * LANES // share, (at + 1) * LANES // share):
            block += at_lane(from_lane(got_ref[d, :LEAD, :], HALF, share), d * share % LANES, share)
        down.append(block)
    down = jnp.concatenate(down, axis=1)
    norm = SPECTRAL_WEIGHT / (total * M * S)
    stats = sum(got_ref[d, LEAD:, :] for d in range(n_all))
    loss_ref[...] = stats[:1, :1] / steps_ref[C : C + 1, HALF : HALF + 1] + norm * stats[1:2, :1]

    keep = iota((LEAD, D), 0) < C
    query = jnp.where(keep, query, 0.0)
    query = jnp.concatenate(split(query), axis=0).astype(BF)
    down = jnp.concatenate(split(down), axis=0).astype(BF)
    thin = thin_rows(w_ref)
    embed = at_lane(thin, 0, C) + at_lane(from_lane(thin, 0, C), LEAD, C)
    head = from_lane(thin, LEAD, C)
    head = at_lane(head, 0, C) + at_lane(head, LEAD, C)

    def back(weights, sums):
        sums = jnp.concatenate([sums, jnp.zeros((LANES - 16, sums.shape[1]), BF)], axis=0)
        out = mm(weights.astype(BF), sums, NT)
        return from_lane(out, 0, LEAD) + from_lane(out, LEAD, LEAD)

    own = jnp.concatenate([thin_ref[...], jnp.zeros((LANES - LEAD, LANES), F32)], axis=0).T
    embed_grad = own[HALF : HALF + rows] + back(w_ref[:, :D], query)
    head_grad = own[HALF + rows : HALF + 2 * rows] + back(
        w_ref[:, 2 * D + FF : 2 * D + 2 * FF], down
    )
    last = at_lane(embed_grad, 0, C) + at_lane(head_grad, C, C)

    def update(grad, cols):
        new = adamw(w_ref[:, cols], grad, m_ref[:, cols], v_ref[:, cols], ema_ref[:, cols], RATE_DENSE)
        for ref, value in zip((w_out, m_out, v_out, ema_out, low_out), new, strict=True):
            ref[:, cols] = value

    update(mm(embed[:, :16].astype(BF), query), slice(0, D))
    update(sum(ref[...].astype(F32) for ref in big_refs), slice(D, 2 * D + FF))
    update(mm(head[:, :16].astype(BF), down), slice(2 * D + FF, 2 * D + 2 * FF))
    update(last[:, : 2 * C], slice(2 * D + 2 * FF, 2 * D + 2 * FF + 2 * C))


def per_device(
    series,
    future_values,
    step_mask,
    mode_index,
    dense,
    dense_m,
    dense_v,
    dense_ema,
    spectral,
    spec_m,
    fourier_variance_moment,
    spec_ema,
):
    n_mode = lax.axis_size("mode")
    n_data = lax.axis_size("dp")
    n_all = n_mode * n_data
    time_rows, batch, chans = series.shape
    nb = batch // n_mode
    total = batch * n_data
    modes = M // n_mode
    wide = D // n_data
    rows = dense.shape[0]
    shape = jax.ShapeDtypeStruct
    sizes = (n_data, n_mode, nb, total)
    tiled = rows % 16 == 0 and n_mode == 4 and n_data >= 4

    send, weights = call(
        partial(pack_kernel, sizes),
        (shape((n_mode, 2 * nb * LEAD, time_rows), F32), shape((rows, D + FF + LANES), BF)),
        (series.transpose(2, 1, 0), future_values.transpose(2, 1, 0), step_mask.T, dense),
        [pltpu.VMEM((chans, batch, time_rows), F32), pltpu.VMEM((batch, time_rows), F32)],
        name="pack",
        ahead=(0, 1, 2, 3),
    )
    me = jnp.stack([lax.axis_index("dp"), lax.axis_index("mode")]).astype(jnp.int32)
    own = exchange(send, "mode")
    cosv, sinv = tables(mode_index)
    weights = [gather_rows(weights)] if not tiled else gather_tiles_first(weights)
    if tiled:
        own, *weights = together(own, *weights)
        weights = gather_tiles_second(*weights)

    whole_rows = [pltpu.VMEM((2 * nb * LEAD, S), F32)]
    send = call(
        partial(spectra_kernel, sizes),
        shape((n_all, 16, LANES), F32),
        (own, cosv, sinv, dense),
        whole_rows,
        name="spectra",
    )
    first = exchange(send, AXES)
    ins = call(
        tables_kernel,
        (
            shape((S, 4 * M), BF),
            shape((3 * M, S), BF),
            shape((2 * M, S), BF),
            shape((S, 2 * M), BF),
            shape((S, LANES), F32),
            shape((S, LANES), F32),
        ),
        (own, cosv, sinv),
        whole_rows,
        name="tables",
        cost=10**10,
    )
    first, *ins = together(first, *ins)
    if tiled:
        weights = gather_tiles_third(*weights)

    w_low = spectral.astype(BF).reshape(2, modes, wide, E)
    mixer = jnp.concatenate(
        [
            jnp.concatenate([w_low[0], w_low[1]], axis=2),
            jnp.concatenate([-w_low[1], w_low[0]], axis=2),
        ],
        axis=1,
    )
    scratch = [
        pltpu.VMEM((nb, n_all * 16, LANES), F32),
        pltpu.VMEM((n_all * nb * modes, LANES), F32),
    ]
    send, spec, thin = call(
        partial(mix_kernel, sizes),
        (
            shape((n_all, nb * modes + 16, LANES), BF),
            shape((modes, total, 2 * wide), BF),
            shape((16, LANES), F32),
        ),
        (first, mixer),
        scratch,
        name="mix",
    )
    if tiled:
        send, *weights = together(send, *weights)
        weights = gather_tiles_last(weights)
    got = exchange(send, AXES)
    steps = thin

    send, stats, *big = block(
        steps[C, HALF].reshape(1),
        me,
        weights,
        (got, *ins),
        sizes + (True,) if tiled else sizes,
    )
    got = exchange(send, AXES)
    if tiled:
        big = scatter_tiles_first(*big)
        got, *big = together(got, *big)
        big = scatter_tiles_second(*big)
    send, grad_mixed, thin = call(
        partial(mix_back_kernel, sizes),
        (
            shape((n_all, 16, LANES), F32),
            shape((modes, total, LANES), BF),
            shape((LEAD, LANES), F32),
        ),
        (got, mixer, first, stats),
        scratch[::-1],
        name="mix_back",
        cost=10**10,
    )
    if tiled:
        grad_mixed, big = together(grad_mixed, big)
    spec_out = call(
        partial(spectral_kernel, modes, wide),
        (shape(spectral.shape, F32),) * 4 + (shape(spectral.shape, BF),),
        (spec, grad_mixed, spectral, spec_m, fourier_variance_moment, spec_ema),
        [
            pltpu.VMEM((modes, wide, LANES), F32),
            pltpu.VMEM((2, modes * wide // 2, LANES), F32),
        ],
        name="spectral",
        ahead=(0, 1, 2, 3, 4, 5),
        cost=10**10,
    )
    got = exchange(send, AXES)
    big = scatter_tiles_third(*big) if tiled else [scatter_rows(big[0], rows)]
    loss, *dense_out = call(
        partial(rows_kernel, sizes, len(big)),
        (shape((1, 1), F32),) + (shape(dense.shape, F32),) * 4 + (shape(dense.shape, BF),),
        (got, thin, steps, dense, dense_m, dense_v, dense_ema, *big),
        name="rows",
    )
    return (loss.reshape(()),) + tuple(dense_out) + tuple(spec_out)


def solution(mesh):
    rows = P(("dp", "mode"), None)
    mixing = P(None, "mode", "dp")
    return jax.shard_map(
        per_device,
        mesh=mesh,
        in_specs=(P("mode", "dp", None), P("mode", "dp", None), P("mode", "dp"), P())
        + (rows,) * 4
        + (mixing,) * 4,
        out_specs=(P(),) + (rows,) * 5 + (mixing,) * 5,
        check_vma=False,
    )
```

```python
import math
from functools import partial

import jax
import jax.numpy as jnp
from jax import lax
from jax.experimental import pallas as pl
from jax.experimental.pallas import tpu as pltpu
from jax.sharding import PartitionSpec as P

D = 512
H = 8
E = 64
FF = 2048
M = 64
C = 7
S = 768
LANES = 128

SPECTRAL_WEIGHT = 0.5
RATE_DENSE = 0.02
RATE_SPEC = 0.1
BF = jnp.bfloat16
F32 = jnp.float32
AXES = ("dp", "mode")
SLOPE = jnp.bfloat16
VMEM_BYTES = 60 * 1024 * 1024
FULL_BYTES = 60 * 1024 * 1024
SMALL_BYTES = 16 * 1024 * 1024


def plain(spec, left, right):
    return jnp.einsum(spec, left, right, preferred_element_type=F32)


def exact(spec, left, right):
    return jnp.einsum(
        spec, left, right, precision=lax.Precision.HIGHEST, preferred_element_type=F32
    )


def tables(mode_index):
    steps = jnp.arange(S, dtype=jnp.int32)
    phase = mode_index[:, None] * steps[None, :] % S
    angle = phase.astype(F32) * (2.0 * math.pi / S)
    return (jnp.cos(angle), jnp.sin(angle))


def unpack(whole):
    return (
        whole[:, :D],
        whole[:, D : 2 * D],
        whole[:, 2 * D : 2 * D + FF],
        whole[:, 2 * D + FF : 2 * D + 2 * FF],
        whole[:, 2 * D + 2 * FF : 2 * D + 2 * FF + C],
        whole[:, 2 * D + 2 * FF + C :],
    )


def adamw(weight, grad, first, second, average, rate):
    first_new = 0.5 * first + 0.5 * grad
    second_new = 0.5 * second + 0.5 * grad * grad
    weight_new = weight - rate * (first_new / (jnp.sqrt(second_new) + 1e-08) + 0.01 * weight)
    average_new = 0.9 * average + 0.1 * weight_new
    return (weight_new, first_new, second_new, average_new, weight_new.astype(BF))


def halves(x):
    high = x.astype(BF)
    return high, (x - high.astype(F32)).astype(BF)


def fill(x, size, axis):
    wanted = list(x.shape)
    wanted[axis] = size - x.shape[axis]
    return jnp.concatenate([x, jnp.zeros(wanted, x.dtype)], axis=axis) if wanted[axis] else x


def exchange(x, axes):
    return lax.all_to_all(x, axes, 0, 0, tiled=True)


def partners(step):
    count = lax.axis_size("mode")
    return [(index, index ^ step) for index in range(count)]


def bit_of(step):
    return lax.div(lax.axis_index("mode"), step) % 2


def steps_of_mode():
    return [1 << bit for bit in range(lax.axis_size("mode").bit_length() - 1)]


def by_xor(x, axis, step):
    count = lax.axis_size(axis)
    return lax.ppermute(x, axis, [(index, index ^ step) for index in range(count)])


def tile_offsets(n_data):
    cut = n_data // 4
    low = [2 * step for step in range(cut)]
    high = [2 * step for step in range(cut, 2 * cut)]
    ones = lambda data: [index + 1 for index in data]
    offsets = [
        (low + ones(low), [0] * 2 * cut),
        (low + ones(low), [2] * 2 * cut),
        (high + high, [0] * cut + [2] * cut),
        (ones(high) + ones(high), [0] * cut + [2] * cut),
    ]
    return offsets + [(data, [index + 1 for index in mode]) for data, mode in offsets]


def gather_tiles_first(x):
    n_data = lax.axis_size("dp")
    deep = [x] + [by_xor(x, "dp", 2 * step) for step in range(1, n_data // 2)]
    cut = len(deep) // 2
    return jnp.stack(deep[:cut]), jnp.stack(deep[cut:])


def gather_tiles_second(first, second):
    first = jnp.concatenate([first, by_xor(first, "dp", 1)])
    return first, jnp.concatenate([second, by_xor(second, "mode", 2)])


def gather_tiles_third(first, second):
    return [first, by_xor(first, "mode", 2), second, by_xor(second, "dp", 1)]


def gather_tiles_last(pieces):
    return pieces + [by_xor(piece, "mode", 1) for piece in pieces]


def tile_order(n_data):
    cut = n_data // 4
    low = [2 * step for step in range(cut)]
    high = [2 * step for step in range(cut, 2 * cut)]
    groups = [
        [(data + x, 2) for data in low for x in (0, 1)],
        [(data + x, 0) for data in low for x in (0, 1)],
        [(data + 1, 2 * y) for data in high for y in (0, 1)],
        [(data, 2 * y) for data in high for y in (0, 1)],
    ]
    return [[(data, mode + core) for data, mode in group] for core in (1, 0) for group in groups]


def together(*values):
    return lax.optimization_barrier(values)


def total_of(terms, pick):
    return sum(term[pick].astype(F32) for term in terms)


def scatter_tiles_first(away, stay):
    pairs = lambda terms: [x.reshape((x.shape[0] // 2, 2) + x.shape[1:]) for x in terms]
    come = by_xor(away, "mode", 1)
    first = by_xor(total_of([stay, come], 0).astype(BF), "mode", 2)
    second = by_xor(total_of([stay, come], 2).astype(BF), "dp", 1)
    first = pairs([stay[1], come[1], first])
    second = pairs([stay[3], come[3], second])
    away = [total_of(terms, (slice(None), 1)).astype(BF) for terms in (first, second)]
    return away + [[x[:, 0] for x in terms] for terms in (first, second)]


def scatter_tiles_second(first_away, second_away, first, second):
    return [first + [by_xor(first_away, "dp", 1)], second + [by_xor(second_away, "mode", 2)]]


def scatter_tiles_third(first, second):
    cut = first[0].shape[0]
    come = []
    for step in range(1, 2 * cut):
        terms, at = (first, step) if step < cut else (second, step - cut)
        come.append(by_xor(total_of(terms, at).astype(BF), "dp", 2 * step))
    return [total_of(first, 0)] + come


def gather_rows(x):
    n_data = lax.axis_size("dp")
    held = exchange(jnp.broadcast_to(x[None], (n_data,) + x.shape), "dp")[:, None]
    for step in reversed(steps_of_mode()):
        other = lax.ppermute(held, "mode", partners(step))
        first = bit_of(step) == 0
        pair = [jnp.where(first, held, other), jnp.where(first, other, held)]
        held = jnp.concatenate(pair, axis=1) if step > 1 else jnp.stack(pair, axis=2)
    return held.reshape(-1, x.shape[1])


def scatter_rows(x, rows):
    n_data, n_mode = lax.axis_size("dp"), lax.axis_size("mode")
    held = x.reshape(n_data, n_mode, rows, x.shape[1])
    for step in steps_of_mode():
        held = held.reshape(n_data, held.shape[1] // 2, 2, rows, x.shape[1])
        bit = bit_of(step)
        away = lax.dynamic_index_in_dim(held, 1 - bit, 2, keepdims=False)
        stay = lax.dynamic_index_in_dim(held, bit, 2, keepdims=False)
        other = lax.ppermute(away, "mode", partners(step))
        held = (stay.astype(F32) + other.astype(F32)).astype(BF)
    held = exchange(held.reshape(n_data, rows, x.shape[1]), "dp")
    return jnp.sum(held.astype(F32), axis=0)


NN = (((1,), (0,)), ((), ()))
NT = (((1,), (1,)), ((), ()))
TN = (((0,), (0,)), ((), ()))
FIRST = 2.0 * math.sqrt(2.0 / math.pi)
THIRD = FIRST * 0.044715
GATES = 512
UNROLL = 4
LEAD = 8
HALF = 64


def mm(left, right, dims=NN):
    return lax.dot_general(left, right, dims, preferred_element_type=F32)


def iota(shape, axis):
    return lax.broadcasted_iota(jnp.int32, shape, axis)


def split(x):
    high = x.astype(BF).astype(F32)
    return high, x - high


def by_halves(x):
    high, low = split(x)
    return jnp.where(iota(x.shape, 1) < HALF, high, low).astype(BF)


def fold(x):
    return x + pltpu.roll(x, HALF, 1)


def rows_at(x, first, count):
    parts = []
    if first:
        parts.append(jnp.zeros((first, x.shape[1]), F32))
    parts.append(x)
    if count - first - x.shape[0]:
        parts.append(jnp.zeros((count - first - x.shape[0], x.shape[1]), F32))
    return jnp.concatenate(parts, axis=0)


def row_groups(x):
    return sum(x[at : at + LEAD] for at in range(0, x.shape[0], LEAD))


def block_kernel(sizes, count_ref, me_ref, *refs):
    if len(sizes) == 4:
        block_steps(sizes, lambda what: None, count_ref, *refs)
        return
    n_data, n_mode = sizes[:2]
    rows = D // n_data // n_mode
    offsets = tile_offsets(n_data)
    n_pieces = len(offsets)
    pieces, got_ref, sources, refs = refs[:n_pieces], refs[n_pieces], refs[n_pieces + 1 : n_pieces + 7], refs[n_pieces + 7 :]
    send_ref, stat_ref, away_ref, stay_ref, row_sems, sems, w_ref = refs[:7]
    places, scratch = refs[7:13], refs[13:]
    act_ref = scratch[5]

    def rows_of(data, mode):
        owner = (me_ref[0] ^ data) * n_mode + (me_ref[1] ^ mode)
        return pl.ds(pl.multiple_of(owner * rows, rows), rows)

    row_copies = []
    for ref, (data, mode) in zip(pieces, offsets, strict=True):
        for at, (one, two) in enumerate(zip(data, mode, strict=True)):
            place = w_ref.at[rows_of(one, two), :]
            row_copies.append(
                pltpu.make_async_copy(ref.at[at], place, row_sems.at[len(row_copies)])
            )
            row_copies[-1].start()
    copies = [
        pltpu.make_async_copy(source, place, sems.at[at])
        for at, (source, place) in enumerate(zip(sources, places, strict=True))
    ]
    for copy in copies:
        copy.start()
    waits = {"rows": row_copies, "a": copies[:1], "rest": copies[1:]}

    def ready(what):
        for copy in waits[what]:
            copy.wait()

    block_steps(sizes, ready, count_ref, w_ref, got_ref, *places, send_ref, stat_ref, None, *scratch)
    for at, group in enumerate(tile_order(n_data)):
        ref = away_ref if at < 4 else stay_ref
        for index, (data, mode) in enumerate(group):
            ref[at % 4, index, :, :D] = act_ref[1, rows_of(data, mode), :D]
            ref[at % 4, index, :, D:] = act_ref[0, rows_of(data, mode), :]


def block_steps(
    sizes,
    ready,
    count_ref,
    w_ref,
    got_ref,
    a_ref,
    at_ref,
    rest_ref,
    rest_t_ref,
    target_ref,
    keep_ref,
    send_ref,
    stat_ref,
    big_ref,
    wdup_ref,
    x_ref,
    v_ref,
    r_ref,
    wd_ref,
    act_ref,
    slope_ref,
    fc_ref,
    zx_ref,
    j_ref,
):
    n_data, n_mode, nb, total = sizes[:4]
    n_all = n_data * n_mode
    modes = M // n_mode
    nbm = nb * modes
    share = FF // n_all
    rows = D // n_all
    scale = 2.0 / S
    norm = SPECTRAL_WEIGHT / (total * M * S)
    chunks = FF // GATES

    for i in range(n_data):
        blocks = [got_ref[i * n_mode + j, :nbm, :].astype(F32) for j in range(n_mode)]
        for k in range(nb):
            column = [block[k * modes : (k + 1) * modes] for block in blocks]
            x_ref[k * M : (k + 1) * M, i * LANES : (i + 1) * LANES] = jnp.concatenate(
                column, axis=0
            ).astype(BF)

    per = LANES // share
    for at in range(FF // LANES):
        block = jnp.zeros((16, LANES), F32)
        for q in range(per):
            piece = got_ref[at * per + q, nbm : nbm + 16, :].astype(F32)
            piece = pltpu.roll(piece, q * share, 1) if q else piece
            block = jnp.where(iota(block.shape, 1) // share == q, piece, block)
        spread = [
            rows_at(jnp.concatenate([half] * nb, axis=0), 0, HALF)
            for half in (block[:LEAD], block[LEAD:])
        ]
        wd_ref[:, at * LANES : (at + 1) * LANES] = jnp.concatenate(spread, axis=0).astype(BF)
    ready("rows")
    for i in range(n_data):
        head = i * H // n_data
        block = w_ref[head * E : (head + 1) * E, :D]
        wdup_ref[2 * i * E : (2 * i + 1) * E, :] = block
        wdup_ref[(2 * i + 1) * E : (2 * i + 2) * E, :] = block
    x_all = x_ref[...]
    real_lane = iota(x_all.shape, 1) % LANES < HALF
    zero = jnp.zeros_like(x_all)
    x_real = jnp.where(real_lane, x_all, zero)
    x_imag = jnp.where(real_lane, zero, x_all)
    line_real = scale * mm(x_real, wdup_ref[...])
    line_imag = scale * mm(x_imag, wdup_ref[...])
    for k in range(nb):
        v_ref[2 * k * M : (2 * k + 1) * M, :] = line_real[k * M : (k + 1) * M].astype(BF)
        v_ref[(2 * k + 1) * M : (2 * k + 2) * M, :] = line_imag[k * M : (k + 1) * M].astype(BF)

    thin_t = w_ref[:, D + FF :].astype(F32).T
    embed_t = thin_t[:LEAD]
    head_t = thin_t[LEAD : 2 * LEAD]
    pad = [jnp.zeros((HALF - nb * LEAD, D), F32)] if nb * LEAD < HALF else []
    embed_all = jnp.concatenate([embed_t] * nb + pad, axis=0).astype(BF)
    head_all = jnp.concatenate([head_t] * nb + pad, axis=0).astype(BF)
    head_twice = jnp.concatenate([head_all, head_all], axis=0)
    embed_twice = jnp.concatenate([embed_t, embed_t], axis=0).astype(BF)

    for c in range(FF // 512):
        cols = slice(c * 512, (c + 1) * 512)
        w_up = w_ref[:, D + c * 512 : D + (c + 1) * 512]
        lifted = mm(v_ref[...], w_up)
        thin = mm(embed_twice, w_up)[:LEAD]
        high, low = split(thin)
        for k in range(nb):
            r_ref[k, : 2 * M, cols] = lifted[2 * k * M : 2 * (k + 1) * M].astype(BF)
            r_ref[k, 2 * M :, cols] = jnp.concatenate(
                [rows_at(high, k * LEAD, HALF), rows_at(low, k * LEAD, HALF)], axis=0
            ).astype(BF)

    parts = [mm(head_all[:16], v_ref[2 * k * M : 2 * (k + 1) * M, :], NT)[:LEAD] for k in range(nb)]
    by_head = rows_at(jnp.concatenate(parts, axis=0), 0, HALF)
    cross = mm(head_all, jnp.concatenate([embed_all, jnp.zeros_like(embed_all)], axis=0), NT)
    cross = jnp.where(iota(cross.shape, 0) // LEAD == iota(cross.shape, 1) // LEAD, cross, 0.0)
    high, low = split(jnp.concatenate([by_head, cross], axis=1))
    by_head = jnp.concatenate([high, low], axis=0).astype(BF)
    ready("a")
    fc_ref[...] = mm(a_ref[...], by_head, NT)

    own_lane = iota((S, LANES), 1) % HALF // LEAD

    def forward(step, carry):
        k = step // chunks
        cols = pl.ds(pl.multiple_of(step % chunks * GATES, GATES), GATES)
        gate = mm(a_ref[...], r_ref[k, :, cols])
        square = gate * gate
        sig = 0.5 * jnp.tanh(gate * (square * (0.5 * THIRD) + 0.5 * FIRST)) + 0.5
        act = gate * sig
        low = act.astype(BF)
        act_ref[k, :, cols] = low
        slope = sig + act * (1.0 - sig) * (square * (3.0 * THIRD) + FIRST)
        slope_ref[k, :, cols] = slope.astype(slope_ref.dtype)
        fc_ref[...] += jnp.where(own_lane == k, mm(low, wd_ref[:, cols], NT), 0.0)
        return carry

    lax.fori_loop(0, nb * chunks, forward, 0, unroll=UNROLL)

    ready("rest")
    keep = keep_ref[...]
    masked = keep * (fold(fc_ref[...]) - target_ref[...])
    two = by_halves(masked)
    err = fold(mm(at_ref[: 2 * M, :], two) + mm(rest_ref[...], two))
    stat_ref[...] = jnp.concatenate(
        [
            jnp.full((1, LANES), 0.5 * jnp.sum(masked * masked)),
            jnp.full((1, LANES), 0.5 * jnp.sum(err * err)),
            jnp.zeros((6, LANES), F32),
        ],
        axis=0,
    )
    two = by_halves(err)
    back = fold(mm(a_ref[:, : 2 * M], two) + mm(rest_t_ref[...], two))
    g_fc = keep * ((2.0 / count_ref[0]) * masked + (2.0 * norm) * back)
    g_low = g_fc.astype(BF)
    g_turn = g_fc.T[:HALF].astype(BF)
    zx_ref[...] = jnp.zeros_like(zx_ref)
    j_ref[...] = jnp.zeros_like(j_ref)

    def backward(step, carry):
        k = step // chunks
        cols = pl.ds(pl.multiple_of(step % chunks * GATES, GATES), GATES)
        fed = mm(jnp.where(own_lane == k, g_fc, 0.0).astype(BF), wd_ref[:, cols])
        g_gate = (fed * slope_ref[k, :, cols].astype(F32)).astype(BF)
        turned = mm(at_ref[...], g_gate)
        r_ref[k, : 2 * M, cols] = turned[: 2 * M].astype(BF)
        own = iota((HALF, GATES), 0) // LEAD == k
        zx_ref[:, cols] += jnp.where(own, turned[2 * M :], 0.0)
        j_ref[:, cols] += jnp.where(own, mm(g_turn, act_ref[k, :, cols]), 0.0)
        return carry

    lax.fori_loop(0, nb * chunks, backward, 0, unroll=UNROLL)

    back_fc = by_halves(mm(at_ref[...], g_low))
    lane_of = iota((2 * M, LANES), 1) % HALF // LEAD
    nothing = jnp.zeros((2 * M, LANES), F32)
    back_rows = jnp.concatenate(
        [jnp.where(lane_of == k, back_fc[: 2 * M].astype(F32), nothing) for k in range(nb)], axis=0
    ).astype(BF)
    cross = jnp.where(
        iota((HALF, LANES), 0) // LEAD == iota((HALF, LANES), 1) % HALF // LEAD,
        back_fc[2 * M :].astype(F32),
        0.0,
    ).astype(BF)
    v_all = v_ref[...]
    z_all = r_ref[:, : 2 * M, :].reshape(nb * 2 * M, FF)
    high, low = split(row_groups(zx_ref[...]))
    zx = jnp.concatenate([high, low], axis=0).astype(BF)
    w_up = w_ref[:, D : D + FF]
    back_block = mm(z_all, w_up, NT) + mm(back_rows, head_twice)
    turned = (scale * back_block).astype(BF)
    embed_grad = row_groups(mm(zx, w_up, NT)) + row_groups(mm(cross, head_twice))
    head_grad = row_groups(mm(back_rows, v_all, TN)) + row_groups(mm(cross, embed_all, TN))
    down_grad = row_groups(j_ref[...])

    turned_real = jnp.concatenate(
        [turned[2 * k * M : (2 * k + 1) * M] for k in range(nb)], axis=0
    )
    turned_imag = jnp.concatenate(
        [turned[(2 * k + 1) * M : (2 * k + 2) * M] for k in range(nb)], axis=0
    )
    p_real = mm(turned_real, wdup_ref[...], NT)
    p_imag = mm(turned_imag, wdup_ref[...], NT)
    real_lane = iota((modes, LANES), 1) < HALF
    lane = iota((LEAD, LANES), 1)
    for i in range(n_data):
        cols = slice(i * LANES, (i + 1) * LANES)
        for j in range(n_mode):
            d = i * n_mode + j
            pieces = []
            for k in range(nb):
                at = slice(k * M + j * modes, k * M + (j + 1) * modes)
                pieces.append(jnp.where(real_lane, p_real[at, cols], p_imag[at, cols]))
            send_ref[d, :nbm, :] = jnp.concatenate(pieces, axis=0).astype(BF)
            out = jnp.zeros((LEAD, LANES), F32)
            for source, width, place in (
                (down_grad, share, 0),
                (embed_grad, rows, HALF),
                (head_grad, rows, HALF + rows),
            ):
                first = d * width // LANES * LANES
                piece = source[:, first : first + LANES]
                shift = (place - (d * width - first)) % LANES
                piece = pltpu.roll(piece, shift, 1) if shift else piece
                out = jnp.where((lane >= place) & (lane < place + width), piece, out)
            high, low = split(out)
            send_ref[d, nbm:, :] = jnp.concatenate([high, low], axis=0).astype(BF)

    x_all = x_ref[...]
    real_lane = iota(x_all.shape, 1) % LANES < HALF
    x_real = jnp.where(real_lane, x_all, zero)
    x_imag = jnp.where(real_lane, zero, x_all)
    out_grad = mm(x_real, turned_real, TN) + mm(x_imag, turned_imag, TN)
    each = n_data // H
    for head in range(H):
        block = 0.0
        for i in range(head * each, (head + 1) * each):
            block += out_grad[2 * i * E : (2 * i + 1) * E] + out_grad[(2 * i + 1) * E : (2 * i + 2) * E]
        out = act_ref.at[1] if big_ref is None else big_ref
        out[head * E : (head + 1) * E, :D] = block.astype(BF)
    for c in range(FF // 512):
        cols = slice(c * 512, (c + 1) * 512)
        up_grad = mm(v_all, z_all[:, cols], TN) + mm(embed_twice, zx[:, cols], TN)
        if big_ref is None:
            act_ref[0, :D, cols] = up_grad.astype(BF)
        else:
            big_ref[:, D + c * 512 : D + (c + 1) * 512] = up_grad.astype(BF)


def block(count, me, weights, ins, sizes):
    n_data, n_mode, nb = sizes[:3]
    tiled = len(sizes) > 4
    whole = pl.BlockSpec(memory_space=pltpu.VMEM)
    far = pl.BlockSpec(memory_space=pl.ANY if tiled else pltpu.VMEM)
    big = [jax.ShapeDtypeStruct((D, D + FF), BF)]
    scratch = []
    if tiled:
        half = (4, n_data * n_mode // 8, D // n_data // n_mode, D + FF)
        big = [jax.ShapeDtypeStruct(half, BF)] * 2
        scratch = [
            pltpu.SemaphoreType.DMA((n_data * n_mode,)),
            pltpu.SemaphoreType.DMA((6,)),
            pltpu.VMEM((D, D + FF + LANES), BF),
        ]
        scratch += [pltpu.VMEM(x.shape, x.dtype) for x in ins[1:]]
    return pl.pallas_call(
        partial(block_kernel, sizes),
        out_shape=(
            jax.ShapeDtypeStruct(ins[0].shape, BF),
            jax.ShapeDtypeStruct((8, LANES), F32),
            *big,
        ),
        in_specs=[pl.BlockSpec(memory_space=pltpu.SMEM)] * 2
        + [far] * len(weights)
        + [whole]
        + [far] * (len(ins) - 1),
        out_specs=(whole,) * (2 + len(big)),
        scratch_shapes=scratch
        + [
            pltpu.VMEM((2 * n_data * E, D), BF),
            pltpu.VMEM((nb * M, n_data * LANES), BF),
            pltpu.VMEM((nb * 2 * M, D), BF),
            pltpu.VMEM((nb, 4 * M, FF), BF),
            pltpu.VMEM((LANES, FF), BF),
            pltpu.VMEM((nb, S, FF), BF),
            pltpu.VMEM((nb, S, FF), SLOPE),
            pltpu.VMEM((S, LANES), F32),
            pltpu.VMEM((HALF, FF), F32),
            pltpu.VMEM((HALF, FF), F32),
        ],
        compiler_params=pltpu.CompilerParams(vmem_limit_bytes=VMEM_BYTES),
        name="block",
    )(count, me, *weights, *ins)


def at_lane(x, first, width):
    x = pltpu.roll(x, first, 1) if first else x
    lane = iota(x.shape, 1)
    return jnp.where((lane >= first) & (lane < first + width), x, 0.0)


def from_lane(x, first, width):
    base = first // LANES * LANES
    x = x[:, base : base + LANES]
    shift = (LANES - (first - base)) % LANES
    x = pltpu.roll(x, shift, 1) if shift else x
    return jnp.where(iota(x.shape, 1) < width, x, 0.0)


def staged(kernel, ahead, *refs):
    sems = refs[-1]
    n_held = len(refs) - 1 - len(ahead)
    held = list(refs[:n_held])
    copies = []
    for at, (index, place) in enumerate(zip(ahead, refs[n_held:-1], strict=True)):
        copies.append(pltpu.make_async_copy(refs[index], place, sems.at[at]))
        copies[-1].start()
        held[index] = place

    def ready():
        for copy in copies:
            copy.wait()

    kernel(ready, *held)


def call(kernel, outs, ins, scratch=(), name=None, cost=0, ahead=()):
    whole = pl.BlockSpec(memory_space=pltpu.VMEM)
    in_specs = [whole] * len(ins)
    scratch = list(scratch)
    if ahead:
        kernel = partial(staged, kernel, ahead)
        for index in ahead:
            in_specs[index] = pl.BlockSpec(memory_space=pl.ANY)
            scratch.append(pltpu.VMEM(ins[index].shape, ins[index].dtype))
        scratch.append(pltpu.SemaphoreType.DMA((len(ahead),)))
    return pl.pallas_call(
        kernel,
        out_shape=outs,
        in_specs=in_specs,
        out_specs=jax.tree.map(lambda _: whole, outs),
        scratch_shapes=scratch,
        compiler_params=pltpu.CompilerParams(vmem_limit_bytes=FULL_BYTES if ahead else SMALL_BYTES),
        name=name,
        cost_estimate=pl.CostEstimate(flops=cost, bytes_accessed=cost // 10, transcendentals=0)
        if cost
        else None,
    )(*ins)


def thin_rows(dense_ref):
    thin = dense_ref[:, 2 * D + 2 * FF :]
    thin = jnp.concatenate([thin, jnp.zeros((thin.shape[0], LANES - 2 * C), F32)], axis=1)
    return at_lane(thin, 0, C) + at_lane(from_lane(thin, C, C), LEAD, C)


def pack_kernel(sizes, ready, series_ref, future_ref, mask_ref, dense_ref, send_ref, rows_ref, one_ref, two_ref):
    n_mode, nb = sizes[1:3]
    ready()
    one_ref[...] = series_ref[...].astype(F32)
    two_ref[...] = mask_ref[...].astype(F32)
    for j in range(n_mode):
        for k in range(nb):
            b = j * nb + k
            for c in range(C):
                send_ref[j, k * LEAD + c, :] = one_ref[c, b, :]
                send_ref[j, (nb + k) * LEAD + c, :] = future_ref[c, b, :]
            send_ref[j, k * LEAD + C, :] = two_ref[b, :]
            send_ref[j, (nb + k) * LEAD + C, :] = jnp.zeros_like(two_ref[b, :])
    rows_ref[:, : D + FF] = dense_ref[:, D : 2 * D + FF].astype(BF)
    rows_ref[:, D + FF :] = thin_rows(dense_ref).astype(BF)


def own_rows(got_ref, all_ref):
    steps = got_ref.shape[2]
    for j in range(got_ref.shape[0]):
        all_ref[:, j * steps : (j + 1) * steps] = got_ref[j]
    half = all_ref.shape[0] // 2
    inputs = all_ref[:half, :]
    mask = inputs
    inputs = jnp.where(iota(inputs.shape, 0) % LEAD == C, 0.0, inputs)
    return inputs, mask, all_ref[half:, :]


def spectra_kernel(sizes, got_ref, cos_ref, sin_ref, dense_ref, send_ref, all_ref):
    n_data, n_mode, nb, _ = sizes
    n_all = n_data * n_mode
    modes = M // n_mode
    wide = D // n_data
    share = FF // n_all
    x, mask, _ = own_rows(got_ref, all_ref)
    count = jnp.sum(jnp.where(iota(mask.shape, 0) % LEAD == C, mask, 0.0))
    low = cos_ref[...].astype(BF)
    inner = mm(low, rows_at(x, 0, LANES).astype(BF), NT)
    low = (-sin_ref[...]).astype(BF)
    inner += mm(low, rows_at(x, nb * LEAD, LANES).astype(BF), NT)
    thin = thin_rows(dense_ref).astype(BF)
    query = mm(thin, dense_ref[:, :D].astype(BF), TN)[:LEAD]
    down = mm(thin, dense_ref[:, 2 * D + FF : 2 * D + 2 * FF].astype(BF), TN)[LEAD : 2 * LEAD]
    row = iota((LEAD, LANES), 0)
    lane = iota((LEAD, LANES), 1)
    for i in range(n_data):
        ours = at_lane(from_lane(query, i * wide, wide), HALF, wide)
        ours = jnp.where((row == C) & (lane == HALF), count, ours)
        for j in range(n_mode):
            d = i * n_mode + j
            block = inner[j * modes : (j + 1) * modes]
            if modes < 16:
                block = jnp.concatenate([block, jnp.zeros((16 - modes, LANES), F32)], axis=0)
            theirs = at_lane(from_lane(down, d * share, share), HALF, share)
            send_ref[d] = block + jnp.concatenate([ours, theirs], axis=0)


def tables_kernel(
    got_ref, cos_ref, sin_ref, a_ref, at_ref, rest_ref, rest_t_ref, target_ref, keep_ref, all_ref
):
    x, mask, target = own_rows(got_ref, all_ref)
    count = x.shape[0]
    keep = [
        jnp.broadcast_to(mask[at + C : at + LEAD], (LEAD, S)) for at in range(0, count, LEAD)
    ]
    keep = jnp.concatenate(keep, axis=0)
    twice = lambda rows: jnp.concatenate([rows_at(rows, 0, HALF)] * 2, axis=0).T
    a_ref[:, 2 * M :] = twice(x).astype(BF)
    at_ref[2 * M :, :] = rows_at(x, 0, HALF).astype(BF)
    target_ref[...] = twice(target)
    keep_ref[...] = twice(keep)
    basis = jnp.concatenate([cos_ref[...], -sin_ref[...]], axis=0)
    low = basis.astype(BF)
    at_ref[: 2 * M, :] = low
    rest_ref[...] = (basis - low.astype(F32)).astype(BF)
    turned = basis.T
    low = turned.astype(BF)
    a_ref[:, : 2 * M] = low
    rest_t_ref[...] = (turned - low.astype(F32)).astype(BF)


def mix_kernel(sizes, got_ref, mixer_ref, send_ref, spec_ref, thin_ref, wide_ref, out_ref):
    n_data, n_mode, nb, _ = sizes
    n_all = n_data * n_mode
    modes = M // n_mode
    nbm = nb * modes
    wide = D // n_data
    share = FF // n_all
    got = got_ref[...]
    thin = jnp.sum(got, axis=0)
    thin_ref[...] = thin
    query = from_lane(thin[:LEAD], HALF, wide)
    query = jnp.where(iota(query.shape, 0) < C, query, 0.0)
    down = from_lane(thin[LEAD:], HALF, share)
    high, low = split(down)
    down = jnp.concatenate([high, low], axis=0).astype(BF)
    spread = []
    for part in range(2):
        block = at_lane(query, part * wide, wide)
        zero = jnp.zeros_like(block)
        for k in range(nb):
            blocks = [block if g == k else zero for g in range(nb)]
            spread.append(jnp.concatenate(blocks, axis=1))
    spread = jnp.concatenate(spread, axis=0)
    inner = got.reshape(n_all * 16, LANES)[:, : 2 * nb * LEAD]
    spec = lax.dot_general(
        inner, spread, NN, precision=lax.Precision.HIGHEST, preferred_element_type=F32
    )
    for k in range(nb):
        wide_ref[k] = spec[:, k * LANES : (k + 1) * LANES]
    for m in range(modes):
        spec = [wide_ref[k, pl.ds(m, n_all, stride=16), :][:, : 2 * wide] for k in range(nb)]
        spec = jnp.concatenate(spec, axis=0).astype(BF)
        spec_ref[m] = spec
        mixed = mm(spec, mixer_ref[m])
        for k in range(nb):
            out_ref[pl.ds(k * modes + m, n_all, stride=nbm), :] = mixed[
                k * n_all : (k + 1) * n_all
            ]
    for d in range(n_all):
        send_ref[d, :nbm, :] = out_ref[d * nbm : (d + 1) * nbm, :].astype(BF)
        send_ref[d, nbm:, :] = down


def mix_back_kernel(
    sizes, got_ref, mixer_ref, first_ref, stat_ref, send_ref, grad_ref, thin_ref, in_ref, wide_ref
):
    n_data, n_mode, nb, _ = sizes
    n_all = n_data * n_mode
    modes = M // n_mode
    nbm = nb * modes
    wide = D // n_data
    share = FF // n_all
    thin = jnp.zeros((16, LANES), F32)
    for d in range(n_all):
        in_ref[d * nbm : (d + 1) * nbm, :] = got_ref[d, :nbm, :].astype(F32)
        thin += got_ref[d, nbm:, :].astype(F32)
    thin = thin[:LEAD] + thin[LEAD:]
    thin_ref[...] = thin
    if modes < 16:
        wide_ref[...] = jnp.zeros_like(wide_ref)
    for m in range(modes):
        grad = [in_ref[pl.ds(k * modes + m, n_all, stride=nbm), :] for k in range(nb)]
        grad = jnp.concatenate(grad, axis=0).astype(BF)
        grad_ref[m] = grad
        back = mm(grad, mixer_ref[m], NT).astype(BF).astype(F32)
        if 2 * wide < LANES:
            back = jnp.concatenate(
                [back, jnp.zeros((back.shape[0], LANES - 2 * wide), F32)], axis=1
            )
        for k in range(nb):
            wide_ref[k, pl.ds(m, n_all, stride=16), :] = back[k * n_all : (k + 1) * n_all]
    inner = first_ref[...].reshape(n_all * 16, LANES)
    inner = jnp.where(iota(inner.shape, 1) < HALF, inner, 0.0)
    inner = by_halves(fold(inner))
    total = jnp.zeros((LEAD, LANES), F32)
    for k in range(nb):
        query = mm(inner, wide_ref[k].astype(BF), TN)
        query = query[:HALF] + query[HALF:]
        for part in range(2):
            at = (part * nb + k) * LEAD
            total += from_lane(query[at : at + LEAD], part * wide, wide)
    block = total + at_lane(from_lane(thin, 0, share), HALF, share)
    row, lane = iota(block.shape, 0), iota(block.shape, 1)
    stats = jnp.where(lane < HALF, stat_ref[:1, :], stat_ref[1:2, :])
    block = jnp.where(row == C, stats, block)
    for d in range(n_all):
        send_ref[d] = block


def spectral_kernel(
    modes,
    wide,
    ready,
    spec_ref,
    grad_ref,
    w_ref,
    m_ref,
    v_ref,
    ema_ref,
    w_out,
    m_out,
    v_out,
    ema_out,
    low_out,
    pair_ref,
    turn_ref,
):
    ready()
    lower = iota((wide, LANES), 1) < HALF
    half_lower = iota((wide // 2, LANES), 1) < HALF
    for m in range(modes):
        slopes = mm(spec_ref[m], grad_ref[m], TN)
        other = pltpu.roll(slopes[wide:], HALF, 1)
        pair_ref[m] = jnp.where(lower, slopes[:wide] + other, slopes[:wide] - other)
        even = pair_ref[m, pl.ds(0, wide // 2, stride=2), :]
        odd = pair_ref[m, pl.ds(1, wide // 2, stride=2), :]
        real = jnp.where(half_lower, even, pltpu.roll(odd, HALF, 1))
        imag = jnp.where(half_lower, pltpu.roll(even, HALF, 1), odd)
        turn_ref[0, pl.ds(m, wide // 2, stride=modes), :] = real
        turn_ref[1, pl.ds(m, wide // 2, stride=modes), :] = imag
    for part in range(2):
        for at in range(wide // 2):
            cols = slice(at * LANES, (at + 1) * LANES)
            grad = turn_ref[part, at * modes : (at + 1) * modes, :]
            new = adamw(
                w_ref[part, :, cols],
                grad,
                m_ref[part, :, cols],
                v_ref[part, :, cols],
                ema_ref[part, :, cols],
                RATE_SPEC,
            )
            for ref, value in zip((w_out, m_out, v_out, ema_out, low_out), new, strict=True):
                ref[part, :, cols] = value


def rows_kernel(
    sizes,
    n_big,
    got_ref,
    thin_ref,
    steps_ref,
    w_ref,
    m_ref,
    v_ref,
    ema_ref,
    *refs,
):
    big_refs, (loss_ref, w_out, m_out, v_out, ema_out, low_out) = refs[:n_big], refs[n_big:]
    n_data, n_mode, _, total = sizes
    n_all = n_data * n_mode
    wide = D // n_data
    share = FF // n_all
    rows = w_ref.shape[0]
    query = []
    for at in range(D // LANES):
        block = jnp.zeros((LEAD, LANES), F32)
        for i in range(at * LANES // wide, (at + 1) * LANES // wide):
            part = sum(got_ref[i * n_mode + j, :LEAD, :] for j in range(n_mode))
            block += at_lane(part, i * wide % LANES, wide)
        query.append(block)
    query = jnp.concatenate(query, axis=1)
    down = []
    for at in range(FF // LANES):
        block = jnp.zeros((LEAD, LANES), F32)
        for d in range(at * LANES // share, (at + 1) * LANES // share):
            block += at_lane(from_lane(got_ref[d, :LEAD, :], HALF, share), d * share % LANES, share)
        down.append(block)
    down = jnp.where(iota((LEAD, FF), 0) < C, jnp.concatenate(down, axis=1), 0.0)
    norm = SPECTRAL_WEIGHT / (total * M * S)
    stats = sum(got_ref[d, C : C + 1, :] for d in range(n_all))
    steps = steps_ref[C : C + 1, HALF : HALF + 1]
    loss_ref[...] = stats[:, :1] / steps + norm * stats[:, HALF : HALF + 1]

    keep = iota((LEAD, D), 0) < C
    query = jnp.where(keep, query, 0.0)
    query = jnp.concatenate(split(query), axis=0).astype(BF)
    down = jnp.concatenate(split(down), axis=0).astype(BF)
    thin = thin_rows(w_ref)
    embed = at_lane(thin, 0, C) + at_lane(from_lane(thin, 0, C), LEAD, C)
    head = from_lane(thin, LEAD, C)
    head = at_lane(head, 0, C) + at_lane(head, LEAD, C)

    def back(weights, sums):
        sums = jnp.concatenate([sums, jnp.zeros((LANES - 16, sums.shape[1]), BF)], axis=0)
        out = mm(weights.astype(BF), sums, NT)
        return from_lane(out, 0, LEAD) + from_lane(out, LEAD, LEAD)

    own = jnp.concatenate([thin_ref[...], jnp.zeros((LANES - LEAD, LANES), F32)], axis=0).T
    embed_grad = own[HALF : HALF + rows] + back(w_ref[:, :D], query)
    head_grad = own[HALF + rows : HALF + 2 * rows] + back(
        w_ref[:, 2 * D + FF : 2 * D + 2 * FF], down
    )
    last = at_lane(embed_grad, 0, C) + at_lane(head_grad, C, C)

    def update(grad, cols):
        new = adamw(w_ref[:, cols], grad, m_ref[:, cols], v_ref[:, cols], ema_ref[:, cols], RATE_DENSE)
        for ref, value in zip((w_out, m_out, v_out, ema_out, low_out), new, strict=True):
            ref[:, cols] = value

    update(mm(embed[:, :16].astype(BF), query), slice(0, D))
    update(sum(ref[...].astype(F32) for ref in big_refs), slice(D, 2 * D + FF))
    update(mm(head[:, :16].astype(BF), down), slice(2 * D + FF, 2 * D + 2 * FF))
    update(last[:, : 2 * C], slice(2 * D + 2 * FF, 2 * D + 2 * FF + 2 * C))


def per_device(
    series,
    future_values,
    step_mask,
    mode_index,
    dense,
    dense_m,
    dense_v,
    dense_ema,
    spectral,
    spec_m,
    fourier_variance_moment,
    spec_ema,
):
    n_mode = lax.axis_size("mode")
    n_data = lax.axis_size("dp")
    n_all = n_mode * n_data
    time_rows, batch, chans = series.shape
    nb = batch // n_mode
    total = batch * n_data
    modes = M // n_mode
    wide = D // n_data
    rows = dense.shape[0]
    shape = jax.ShapeDtypeStruct
    sizes = (n_data, n_mode, nb, total)
    tiled = rows % 16 == 0 and n_mode == 4 and n_data >= 4

    send, weights = call(
        partial(pack_kernel, sizes),
        (shape((n_mode, 2 * nb * LEAD, time_rows), F32), shape((rows, D + FF + LANES), BF)),
        (series.transpose(2, 1, 0), future_values.transpose(2, 1, 0), step_mask.T, dense),
        [pltpu.VMEM((chans, batch, time_rows), F32), pltpu.VMEM((batch, time_rows), F32)],
        name="pack",
        ahead=(0, 1, 2, 3),
    )
    me = jnp.stack([lax.axis_index("dp"), lax.axis_index("mode")]).astype(jnp.int32)
    own = exchange(send, "mode")
    cosv, sinv = tables(mode_index)
    weights = [gather_rows(weights)] if not tiled else gather_tiles_first(weights)
    if tiled:
        weights = gather_tiles_second(*weights)

    whole_rows = [pltpu.VMEM((2 * nb * LEAD, S), F32)]
    send = call(
        partial(spectra_kernel, sizes),
        shape((n_all, 16, LANES), F32),
        (own, cosv, sinv, dense),
        whole_rows,
        name="spectra",
    )
    first = exchange(send, AXES)
    ins = call(
        tables_kernel,
        (
            shape((S, 4 * M), BF),
            shape((3 * M, S), BF),
            shape((2 * M, S), BF),
            shape((S, 2 * M), BF),
            shape((S, LANES), F32),
            shape((S, LANES), F32),
        ),
        (own, cosv, sinv),
        whole_rows,
        name="tables",
        cost=10**10,
    )
    first, *ins = together(first, *ins)
    if tiled:
        weights = gather_tiles_third(*weights)

    w_low = spectral.astype(BF).reshape(2, modes, wide, E)
    mixer = jnp.concatenate(
        [
            jnp.concatenate([w_low[0], w_low[1]], axis=2),
            jnp.concatenate([-w_low[1], w_low[0]], axis=2),
        ],
        axis=1,
    )
    scratch = [
        pltpu.VMEM((nb, n_all * 16, LANES), F32),
        pltpu.VMEM((n_all * nb * modes, LANES), F32),
    ]
    send, spec, thin = call(
        partial(mix_kernel, sizes),
        (
            shape((n_all, nb * modes + 16, LANES), BF),
            shape((modes, total, 2 * wide), BF),
            shape((16, LANES), F32),
        ),
        (first, mixer),
        scratch,
        name="mix",
    )
    if tiled:
        send, *weights = together(send, *weights)
        weights = gather_tiles_last(weights)
    got = exchange(send, AXES)
    steps = thin

    send, stats, *big = block(
        steps[C, HALF].reshape(1),
        me,
        weights,
        (got, *ins),
        sizes + (True,) if tiled else sizes,
    )
    got = exchange(send, AXES)
    if tiled:
        big = scatter_tiles_first(*big)
        got, *big = together(got, *big)
        big = scatter_tiles_second(*big)
    send, grad_mixed, thin = call(
        partial(mix_back_kernel, sizes),
        (
            shape((n_all, LEAD, LANES), F32),
            shape((modes, total, LANES), BF),
            shape((LEAD, LANES), F32),
        ),
        (got, mixer, first, stats),
        scratch[::-1],
        name="mix_back",
        cost=10**10,
    )
    if tiled:
        grad_mixed, big = together(grad_mixed, big)
    spec_out = call(
        partial(spectral_kernel, modes, wide),
        (shape(spectral.shape, F32),) * 4 + (shape(spectral.shape, BF),),
        (spec, grad_mixed, spectral, spec_m, fourier_variance_moment, spec_ema),
        [
            pltpu.VMEM((modes, wide, LANES), F32),
            pltpu.VMEM((2, modes * wide // 2, LANES), F32),
        ],
        name="spectral",
        ahead=(0, 1, 2, 3, 4, 5),
        cost=10**10,
    )
    got = exchange(send, AXES)
    big = scatter_tiles_third(*big) if tiled else [scatter_rows(big[0], rows)]
    loss, *dense_out = call(
        partial(rows_kernel, sizes, len(big)),
        (shape((1, 1), F32),) + (shape(dense.shape, F32),) * 4 + (shape(dense.shape, BF),),
        (got, thin, steps, dense, dense_m, dense_v, dense_ema, *big),
        name="rows",
    )
    return (loss.reshape(()),) + tuple(dense_out) + tuple(spec_out)


def solution(mesh):
    rows = P(("dp", "mode"), None)
    mixing = P(None, "mode", "dp")
    return jax.shard_map(
        per_device,
        mesh=mesh,
        in_specs=(P("mode", "dp", None), P("mode", "dp", None), P("mode", "dp"), P())
        + (rows,) * 4
        + (mixing,) * 4,
        out_specs=(P(),) + (rows,) * 5 + (mixing,) * 5,
        check_vma=False,
    )
```

```python
import math
from functools import partial

import jax
import jax.numpy as jnp
from jax import lax
from jax.experimental import pallas as pl
from jax.experimental.pallas import tpu as pltpu
from jax.sharding import PartitionSpec as P

D = 512
H = 8
E = 64
FF = 2048
M = 64
C = 7
S = 768
LANES = 128

SPECTRAL_WEIGHT = 0.5
RATE_DENSE = 0.02
RATE_SPEC = 0.1
BF = jnp.bfloat16
F32 = jnp.float32
AXES = ("dp", "mode")
SLOPE = jnp.bfloat16
VMEM_BYTES = 60 * 1024 * 1024
FULL_BYTES = 60 * 1024 * 1024
SMALL_BYTES = 16 * 1024 * 1024


def plain(spec, left, right):
    return jnp.einsum(spec, left, right, preferred_element_type=F32)


def exact(spec, left, right):
    return jnp.einsum(
        spec, left, right, precision=lax.Precision.HIGHEST, preferred_element_type=F32
    )


def tables(mode_index):
    steps = jnp.arange(S, dtype=jnp.int32)
    phase = mode_index[:, None] * steps[None, :] % S
    angle = phase.astype(F32) * (2.0 * math.pi / S)
    return (jnp.cos(angle), jnp.sin(angle))


def unpack(whole):
    return (
        whole[:, :D],
        whole[:, D : 2 * D],
        whole[:, 2 * D : 2 * D + FF],
        whole[:, 2 * D + FF : 2 * D + 2 * FF],
        whole[:, 2 * D + 2 * FF : 2 * D + 2 * FF + C],
        whole[:, 2 * D + 2 * FF + C :],
    )


def adamw(weight, grad, first, second, average, rate):
    first_new = 0.5 * first + 0.5 * grad
    second_new = 0.5 * second + 0.5 * grad * grad
    weight_new = weight - rate * (first_new / (jnp.sqrt(second_new) + 1e-08) + 0.01 * weight)
    average_new = 0.9 * average + 0.1 * weight_new
    return (weight_new, first_new, second_new, average_new, weight_new.astype(BF))


def halves(x):
    high = x.astype(BF)
    return high, (x - high.astype(F32)).astype(BF)


def fill(x, size, axis):
    wanted = list(x.shape)
    wanted[axis] = size - x.shape[axis]
    return jnp.concatenate([x, jnp.zeros(wanted, x.dtype)], axis=axis) if wanted[axis] else x


def exchange(x, axes):
    return lax.all_to_all(x, axes, 0, 0, tiled=True)


def partners(step):
    count = lax.axis_size("mode")
    return [(index, index ^ step) for index in range(count)]


def bit_of(step):
    return lax.div(lax.axis_index("mode"), step) % 2


def steps_of_mode():
    return [1 << bit for bit in range(lax.axis_size("mode").bit_length() - 1)]


def by_xor(x, axis, step):
    count = lax.axis_size(axis)
    return lax.ppermute(x, axis, [(index, index ^ step) for index in range(count)])


def tile_offsets(n_data):
    cut = n_data // 4
    low = [2 * step for step in range(cut)]
    high = [2 * step for step in range(cut, 2 * cut)]
    ones = lambda data: [index + 1 for index in data]
    offsets = [
        (low + ones(low), [0] * 2 * cut),
        (low + ones(low), [2] * 2 * cut),
        (high + high, [0] * cut + [2] * cut),
        (ones(high) + ones(high), [0] * cut + [2] * cut),
    ]
    return offsets + [(data, [index + 1 for index in mode]) for data, mode in offsets]


def gather_tiles_first(x):
    n_data = lax.axis_size("dp")
    deep = [x] + [by_xor(x, "dp", 2 * step) for step in range(1, n_data // 2)]
    cut = len(deep) // 2
    return jnp.stack(deep[:cut]), jnp.stack(deep[cut:])


def gather_tiles_second(first, second):
    first = jnp.concatenate([first, by_xor(first, "dp", 1)])
    return first, jnp.concatenate([second, by_xor(second, "mode", 2)])


def gather_tiles_third(first, second):
    return [first, by_xor(first, "mode", 2), second, by_xor(second, "dp", 1)]


def gather_tiles_last(pieces):
    return pieces + [by_xor(piece, "mode", 1) for piece in pieces]


def tile_order(n_data):
    cut = n_data // 4
    low = [2 * step for step in range(cut)]
    high = [2 * step for step in range(cut, 2 * cut)]
    groups = [
        [(data + x, 2) for data in low for x in (0, 1)],
        [(data + x, 0) for data in low for x in (0, 1)],
        [(data + 1, 2 * y) for data in high for y in (0, 1)],
        [(data, 2 * y) for data in high for y in (0, 1)],
    ]
    return [[(data, mode + core) for data, mode in group] for core in (1, 0) for group in groups]


def together(*values):
    return lax.optimization_barrier(values)


def total_of(terms, pick):
    return sum(term[pick].astype(F32) for term in terms)


def scatter_tiles_first(away, stay):
    pairs = lambda terms: [x.reshape((x.shape[0] // 2, 2) + x.shape[1:]) for x in terms]
    come = by_xor(away, "mode", 1)
    first = by_xor(total_of([stay, come], 0).astype(BF), "mode", 2)
    second = by_xor(total_of([stay, come], 2).astype(BF), "dp", 1)
    first = pairs([stay[1], come[1], first])
    second = pairs([stay[3], come[3], second])
    away = [total_of(terms, (slice(None), 1)).astype(BF) for terms in (first, second)]
    return away + [[x[:, 0] for x in terms] for terms in (first, second)]


def scatter_tiles_second(first_away, second_away, first, second):
    return [first + [by_xor(first_away, "dp", 1)], second + [by_xor(second_away, "mode", 2)]]


def scatter_tiles_third(first, second):
    cut = first[0].shape[0]
    come = []
    for step in range(1, 2 * cut):
        terms, at = (first, step) if step < cut else (second, step - cut)
        come.append(by_xor(total_of(terms, at).astype(BF), "dp", 2 * step))
    return [total_of(first, 0)] + come


def gather_rows(x):
    n_data = lax.axis_size("dp")
    held = exchange(jnp.broadcast_to(x[None], (n_data,) + x.shape), "dp")[:, None]
    for step in reversed(steps_of_mode()):
        other = lax.ppermute(held, "mode", partners(step))
        first = bit_of(step) == 0
        pair = [jnp.where(first, held, other), jnp.where(first, other, held)]
        held = jnp.concatenate(pair, axis=1) if step > 1 else jnp.stack(pair, axis=2)
    return held.reshape(-1, x.shape[1])


def scatter_rows(x, rows):
    n_data, n_mode = lax.axis_size("dp"), lax.axis_size("mode")
    held = x.reshape(n_data, n_mode, rows, x.shape[1])
    for step in steps_of_mode():
        held = held.reshape(n_data, held.shape[1] // 2, 2, rows, x.shape[1])
        bit = bit_of(step)
        away = lax.dynamic_index_in_dim(held, 1 - bit, 2, keepdims=False)
        stay = lax.dynamic_index_in_dim(held, bit, 2, keepdims=False)
        other = lax.ppermute(away, "mode", partners(step))
        held = (stay.astype(F32) + other.astype(F32)).astype(BF)
    held = exchange(held.reshape(n_data, rows, x.shape[1]), "dp")
    return jnp.sum(held.astype(F32), axis=0)


NN = (((1,), (0,)), ((), ()))
NT = (((1,), (1,)), ((), ()))
TN = (((0,), (0,)), ((), ()))
FIRST = 2.0 * math.sqrt(2.0 / math.pi)
THIRD = FIRST * 0.044715
GATES = 1024
UNROLL = 4
LEAD = 8
HALF = 64


def mm(left, right, dims=NN):
    return lax.dot_general(left, right, dims, preferred_element_type=F32)


def iota(shape, axis):
    return lax.broadcasted_iota(jnp.int32, shape, axis)


def split(x):
    high = x.astype(BF).astype(F32)
    return high, x - high


def by_halves(x):
    high, low = split(x)
    return jnp.where(iota(x.shape, 1) < HALF, high, low).astype(BF)


def fold(x):
    return x + pltpu.roll(x, HALF, 1)


def rows_at(x, first, count):
    parts = []
    if first:
        parts.append(jnp.zeros((first, x.shape[1]), F32))
    parts.append(x)
    if count - first - x.shape[0]:
        parts.append(jnp.zeros((count - first - x.shape[0], x.shape[1]), F32))
    return jnp.concatenate(parts, axis=0)


def row_groups(x):
    return sum(x[at : at + LEAD] for at in range(0, x.shape[0], LEAD))


def block_kernel(sizes, count_ref, me_ref, *refs):
    if len(sizes) == 4:
        block_steps(sizes, lambda what: None, count_ref, *refs)
        return
    n_data, n_mode = sizes[:2]
    rows = D // n_data // n_mode
    offsets = tile_offsets(n_data)
    n_pieces = len(offsets)
    pieces, got_ref, sources, refs = refs[:n_pieces], refs[n_pieces], refs[n_pieces + 1 : n_pieces + 7], refs[n_pieces + 7 :]
    send_ref, stat_ref, away_ref, stay_ref, row_sems, sems, w_ref = refs[:7]
    places, scratch = refs[7:13], refs[13:]
    act_ref = scratch[5]

    def rows_of(data, mode):
        owner = (me_ref[0] ^ data) * n_mode + (me_ref[1] ^ mode)
        return pl.ds(pl.multiple_of(owner * rows, rows), rows)

    row_copies = []
    for ref, (data, mode) in zip(pieces, offsets, strict=True):
        for at, (one, two) in enumerate(zip(data, mode, strict=True)):
            place = w_ref.at[rows_of(one, two), :]
            row_copies.append(
                pltpu.make_async_copy(ref.at[at], place, row_sems.at[len(row_copies)])
            )
            row_copies[-1].start()
    copies = [
        pltpu.make_async_copy(source, place, sems.at[at])
        for at, (source, place) in enumerate(zip(sources, places, strict=True))
    ]
    for copy in copies:
        copy.start()
    waits = {"rows": row_copies, "a": copies[:1], "rest": copies[1:]}

    def ready(what):
        for copy in waits[what]:
            copy.wait()

    block_steps(sizes, ready, count_ref, w_ref, got_ref, *places, send_ref, stat_ref, None, *scratch)
    for at, group in enumerate(tile_order(n_data)):
        ref = away_ref if at < 4 else stay_ref
        for index, (data, mode) in enumerate(group):
            ref[at % 4, index, :, :D] = act_ref[1, rows_of(data, mode), :D]
            ref[at % 4, index, :, D:] = act_ref[0, rows_of(data, mode), :]


def block_steps(
    sizes,
    ready,
    count_ref,
    w_ref,
    got_ref,
    a_ref,
    at_ref,
    rest_ref,
    rest_t_ref,
    target_ref,
    keep_ref,
    send_ref,
    stat_ref,
    big_ref,
    wdup_ref,
    x_ref,
    v_ref,
    r_ref,
    wd_ref,
    act_ref,
    slope_ref,
    fc_ref,
    zx_ref,
    j_ref,
):
    n_data, n_mode, nb, total = sizes[:4]
    n_all = n_data * n_mode
    modes = M // n_mode
    nbm = nb * modes
    share = FF // n_all
    rows = D // n_all
    scale = 2.0 / S
    norm = SPECTRAL_WEIGHT / (total * M * S)
    chunks = FF // GATES

    for i in range(n_data):
        blocks = [got_ref[i * n_mode + j, :nbm, :].astype(F32) for j in range(n_mode)]
        for k in range(nb):
            column = [block[k * modes : (k + 1) * modes] for block in blocks]
            x_ref[k * M : (k + 1) * M, i * LANES : (i + 1) * LANES] = jnp.concatenate(
                column, axis=0
            ).astype(BF)

    per = LANES // share
    for at in range(FF // LANES):
        block = jnp.zeros((16, LANES), F32)
        for q in range(per):
            piece = got_ref[at * per + q, nbm : nbm + 16, :].astype(F32)
            piece = pltpu.roll(piece, q * share, 1) if q else piece
            block = jnp.where(iota(block.shape, 1) // share == q, piece, block)
        spread = [
            rows_at(jnp.concatenate([half] * nb, axis=0), 0, HALF)
            for half in (block[:LEAD], block[LEAD:])
        ]
        wd_ref[:, at * LANES : (at + 1) * LANES] = jnp.concatenate(spread, axis=0).astype(BF)
    ready("rows")
    for i in range(n_data):
        head = i * H // n_data
        block = w_ref[head * E : (head + 1) * E, :D]
        wdup_ref[2 * i * E : (2 * i + 1) * E, :] = block
        wdup_ref[(2 * i + 1) * E : (2 * i + 2) * E, :] = block
    x_all = x_ref[...]
    real_lane = iota(x_all.shape, 1) % LANES < HALF
    zero = jnp.zeros_like(x_all)
    x_real = jnp.where(real_lane, x_all, zero)
    x_imag = jnp.where(real_lane, zero, x_all)
    line_real = scale * mm(x_real, wdup_ref[...])
    line_imag = scale * mm(x_imag, wdup_ref[...])
    for k in range(nb):
        v_ref[2 * k * M : (2 * k + 1) * M, :] = line_real[k * M : (k + 1) * M].astype(BF)
        v_ref[(2 * k + 1) * M : (2 * k + 2) * M, :] = line_imag[k * M : (k + 1) * M].astype(BF)

    thin_t = w_ref[:, D + FF :].astype(F32).T
    embed_t = thin_t[:LEAD]
    head_t = thin_t[LEAD : 2 * LEAD]
    pad = [jnp.zeros((HALF - nb * LEAD, D), F32)] if nb * LEAD < HALF else []
    embed_all = jnp.concatenate([embed_t] * nb + pad, axis=0).astype(BF)
    head_all = jnp.concatenate([head_t] * nb + pad, axis=0).astype(BF)
    head_twice = jnp.concatenate([head_all, head_all], axis=0)
    embed_twice = jnp.concatenate([embed_t, embed_t], axis=0).astype(BF)

    for c in range(FF // 512):
        cols = slice(c * 512, (c + 1) * 512)
        w_up = w_ref[:, D + c * 512 : D + (c + 1) * 512]
        lifted = mm(v_ref[...], w_up)
        thin = mm(embed_twice, w_up)[:LEAD]
        high, low = split(thin)
        for k in range(nb):
            r_ref[k, : 2 * M, cols] = lifted[2 * k * M : 2 * (k + 1) * M].astype(BF)
            r_ref[k, 2 * M :, cols] = jnp.concatenate(
                [rows_at(high, k * LEAD, HALF), rows_at(low, k * LEAD, HALF)], axis=0
            ).astype(BF)

    parts = [mm(head_all[:16], v_ref[2 * k * M : 2 * (k + 1) * M, :], NT)[:LEAD] for k in range(nb)]
    by_head = rows_at(jnp.concatenate(parts, axis=0), 0, HALF)
    cross = mm(head_all, jnp.concatenate([embed_all, jnp.zeros_like(embed_all)], axis=0), NT)
    cross = jnp.where(iota(cross.shape, 0) // LEAD == iota(cross.shape, 1) // LEAD, cross, 0.0)
    high, low = split(jnp.concatenate([by_head, cross], axis=1))
    by_head = jnp.concatenate([high, low], axis=0).astype(BF)
    ready("a")
    fc_ref[...] = mm(a_ref[...], by_head, NT)

    own_lane = iota((S, LANES), 1) % HALF // LEAD

    def forward(step, carry):
        k = step // chunks
        cols = pl.ds(pl.multiple_of(step % chunks * GATES, GATES), GATES)
        gate = mm(a_ref[...], r_ref[k, :, cols])
        square = gate * gate
        sig = 0.5 * jnp.tanh(gate * (square * (0.5 * THIRD) + 0.5 * FIRST)) + 0.5
        act = gate * sig
        low = act.astype(BF)
        act_ref[k, :, cols] = low
        slope = sig + act * (1.0 - sig) * (square * (3.0 * THIRD) + FIRST)
        slope_ref[k, :, cols] = slope.astype(slope_ref.dtype)
        fc_ref[...] += jnp.where(own_lane == k, mm(low, wd_ref[:, cols], NT), 0.0)
        return carry

    lax.fori_loop(0, nb * chunks, forward, 0, unroll=UNROLL)

    ready("rest")
    keep = keep_ref[...]
    masked = keep * (fold(fc_ref[...]) - target_ref[...])
    two = by_halves(masked)
    err = fold(mm(at_ref[: 2 * M, :], two) + mm(rest_ref[...], two))
    stat_ref[...] = jnp.concatenate(
        [
            jnp.full((1, LANES), 0.5 * jnp.sum(masked * masked)),
            jnp.full((1, LANES), 0.5 * jnp.sum(err * err)),
            jnp.zeros((6, LANES), F32),
        ],
        axis=0,
    )
    two = by_halves(err)
    back = fold(mm(a_ref[:, : 2 * M], two) + mm(rest_t_ref[...], two))
    g_fc = keep * ((2.0 / count_ref[0]) * masked + (2.0 * norm) * back)
    g_low = g_fc.astype(BF)
    g_turn = g_fc.T[:HALF].astype(BF)
    zx_ref[...] = jnp.zeros_like(zx_ref)
    j_ref[...] = jnp.zeros_like(j_ref)

    def backward(step, carry):
        k = step // chunks
        cols = pl.ds(pl.multiple_of(step % chunks * GATES, GATES), GATES)
        fed = mm(jnp.where(own_lane == k, g_fc, 0.0).astype(BF), wd_ref[:, cols])
        g_gate = (fed * slope_ref[k, :, cols].astype(F32)).astype(BF)
        turned = mm(at_ref[...], g_gate)
        r_ref[k, : 2 * M, cols] = turned[: 2 * M].astype(BF)
        own = iota((HALF, GATES), 0) // LEAD == k
        zx_ref[:, cols] += jnp.where(own, turned[2 * M :], 0.0)
        j_ref[:, cols] += jnp.where(own, mm(g_turn, act_ref[k, :, cols]), 0.0)
        return carry

    lax.fori_loop(0, nb * chunks, backward, 0, unroll=UNROLL)

    back_fc = by_halves(mm(at_ref[...], g_low))
    lane_of = iota((2 * M, LANES), 1) % HALF // LEAD
    nothing = jnp.zeros((2 * M, LANES), F32)
    back_rows = jnp.concatenate(
        [jnp.where(lane_of == k, back_fc[: 2 * M].astype(F32), nothing) for k in range(nb)], axis=0
    ).astype(BF)
    cross = jnp.where(
        iota((HALF, LANES), 0) // LEAD == iota((HALF, LANES), 1) % HALF // LEAD,
        back_fc[2 * M :].astype(F32),
        0.0,
    ).astype(BF)
    v_all = v_ref[...]
    z_all = r_ref[:, : 2 * M, :].reshape(nb * 2 * M, FF)
    high, low = split(row_groups(zx_ref[...]))
    zx = jnp.concatenate([high, low], axis=0).astype(BF)
    w_up = w_ref[:, D : D + FF]
    back_block = mm(z_all, w_up, NT) + mm(back_rows, head_twice)
    turned = (scale * back_block).astype(BF)
    embed_grad = row_groups(mm(zx, w_up, NT)) + row_groups(mm(cross, head_twice))
    head_grad = row_groups(mm(back_rows, v_all, TN)) + row_groups(mm(cross, embed_all, TN))
    down_grad = row_groups(j_ref[...])

    turned_real = jnp.concatenate(
        [turned[2 * k * M : (2 * k + 1) * M] for k in range(nb)], axis=0
    )
    turned_imag = jnp.concatenate(
        [turned[(2 * k + 1) * M : (2 * k + 2) * M] for k in range(nb)], axis=0
    )
    p_real = mm(turned_real, wdup_ref[...], NT)
    p_imag = mm(turned_imag, wdup_ref[...], NT)
    real_lane = iota((modes, LANES), 1) < HALF
    lane = iota((LEAD, LANES), 1)
    for i in range(n_data):
        cols = slice(i * LANES, (i + 1) * LANES)
        for j in range(n_mode):
            d = i * n_mode + j
            pieces = []
            for k in range(nb):
                at = slice(k * M + j * modes, k * M + (j + 1) * modes)
                pieces.append(jnp.where(real_lane, p_real[at, cols], p_imag[at, cols]))
            send_ref[d, :nbm, :] = jnp.concatenate(pieces, axis=0).astype(BF)
            out = jnp.zeros((LEAD, LANES), F32)
            for source, width, place in (
                (down_grad, share, 0),
                (embed_grad, rows, HALF),
                (head_grad, rows, HALF + rows),
            ):
                first = d * width // LANES * LANES
                piece = source[:, first : first + LANES]
                shift = (place - (d * width - first)) % LANES
                piece = pltpu.roll(piece, shift, 1) if shift else piece
                out = jnp.where((lane >= place) & (lane < place + width), piece, out)
            high, low = split(out)
            send_ref[d, nbm:, :] = jnp.concatenate([high, low], axis=0).astype(BF)

    x_all = x_ref[...]
    real_lane = iota(x_all.shape, 1) % LANES < HALF
    x_real = jnp.where(real_lane, x_all, zero)
    x_imag = jnp.where(real_lane, zero, x_all)
    out_grad = mm(x_real, turned_real, TN) + mm(x_imag, turned_imag, TN)
    each = n_data // H
    for head in range(H):
        block = 0.0
        for i in range(head * each, (head + 1) * each):
            block += out_grad[2 * i * E : (2 * i + 1) * E] + out_grad[(2 * i + 1) * E : (2 * i + 2) * E]
        out = act_ref.at[1] if big_ref is None else big_ref
        out[head * E : (head + 1) * E, :D] = block.astype(BF)
    for c in range(FF // 512):
        cols = slice(c * 512, (c + 1) * 512)
        up_grad = mm(v_all, z_all[:, cols], TN) + mm(embed_twice, zx[:, cols], TN)
        if big_ref is None:
            act_ref[0, :D, cols] = up_grad.astype(BF)
        else:
            big_ref[:, D + c * 512 : D + (c + 1) * 512] = up_grad.astype(BF)


def block(count, me, weights, ins, sizes):
    n_data, n_mode, nb = sizes[:3]
    tiled = len(sizes) > 4
    whole = pl.BlockSpec(memory_space=pltpu.VMEM)
    far = pl.BlockSpec(memory_space=pl.ANY if tiled else pltpu.VMEM)
    big = [jax.ShapeDtypeStruct((D, D + FF), BF)]
    scratch = []
    if tiled:
        half = (4, n_data * n_mode // 8, D // n_data // n_mode, D + FF)
        big = [jax.ShapeDtypeStruct(half, BF)] * 2
        scratch = [
            pltpu.SemaphoreType.DMA((n_data * n_mode,)),
            pltpu.SemaphoreType.DMA((6,)),
            pltpu.VMEM((D, D + FF + LANES), BF),
        ]
        scratch += [pltpu.VMEM(x.shape, x.dtype) for x in ins[1:]]
    return pl.pallas_call(
        partial(block_kernel, sizes),
        out_shape=(
            jax.ShapeDtypeStruct(ins[0].shape, BF),
            jax.ShapeDtypeStruct((8, LANES), F32),
            *big,
        ),
        in_specs=[pl.BlockSpec(memory_space=pltpu.SMEM)] * 2
        + [far] * len(weights)
        + [whole]
        + [far] * (len(ins) - 1),
        out_specs=(whole,) * (2 + len(big)),
        scratch_shapes=scratch
        + [
            pltpu.VMEM((2 * n_data * E, D), BF),
            pltpu.VMEM((nb * M, n_data * LANES), BF),
            pltpu.VMEM((nb * 2 * M, D), BF),
            pltpu.VMEM((nb, 4 * M, FF), BF),
            pltpu.VMEM((LANES, FF), BF),
            pltpu.VMEM((nb, S, FF), BF),
            pltpu.VMEM((nb, S, FF), SLOPE),
            pltpu.VMEM((S, LANES), F32),
            pltpu.VMEM((HALF, FF), F32),
            pltpu.VMEM((HALF, FF), F32),
        ],
        compiler_params=pltpu.CompilerParams(vmem_limit_bytes=VMEM_BYTES),
        name="block",
    )(count, me, *weights, *ins)


def at_lane(x, first, width):
    x = pltpu.roll(x, first, 1) if first else x
    lane = iota(x.shape, 1)
    return jnp.where((lane >= first) & (lane < first + width), x, 0.0)


def from_lane(x, first, width):
    base = first // LANES * LANES
    x = x[:, base : base + LANES]
    shift = (LANES - (first - base)) % LANES
    x = pltpu.roll(x, shift, 1) if shift else x
    return jnp.where(iota(x.shape, 1) < width, x, 0.0)


def staged(kernel, ahead, *refs):
    sems = refs[-1]
    n_held = len(refs) - 1 - len(ahead)
    held = list(refs[:n_held])
    copies = []
    for at, (index, place) in enumerate(zip(ahead, refs[n_held:-1], strict=True)):
        copies.append(pltpu.make_async_copy(refs[index], place, sems.at[at]))
        copies[-1].start()
        held[index] = place

    def ready():
        for copy in copies:
            copy.wait()

    kernel(ready, *held)


def call(kernel, outs, ins, scratch=(), name=None, cost=0, ahead=()):
    whole = pl.BlockSpec(memory_space=pltpu.VMEM)
    in_specs = [whole] * len(ins)
    scratch = list(scratch)
    if ahead:
        kernel = partial(staged, kernel, ahead)
        for index in ahead:
            in_specs[index] = pl.BlockSpec(memory_space=pl.ANY)
            scratch.append(pltpu.VMEM(ins[index].shape, ins[index].dtype))
        scratch.append(pltpu.SemaphoreType.DMA((len(ahead),)))
    return pl.pallas_call(
        kernel,
        out_shape=outs,
        in_specs=in_specs,
        out_specs=jax.tree.map(lambda _: whole, outs),
        scratch_shapes=scratch,
        compiler_params=pltpu.CompilerParams(vmem_limit_bytes=FULL_BYTES if ahead else SMALL_BYTES),
        name=name,
        cost_estimate=pl.CostEstimate(flops=cost, bytes_accessed=cost // 10, transcendentals=0)
        if cost
        else None,
    )(*ins)


def thin_rows(dense_ref):
    thin = dense_ref[:, 2 * D + 2 * FF :]
    thin = jnp.concatenate([thin, jnp.zeros((thin.shape[0], LANES - 2 * C), F32)], axis=1)
    return at_lane(thin, 0, C) + at_lane(from_lane(thin, C, C), LEAD, C)


def pack_kernel(sizes, ready, series_ref, future_ref, mask_ref, dense_ref, send_ref, rows_ref, one_ref, two_ref):
    n_mode, nb = sizes[1:3]
    ready()
    one_ref[...] = series_ref[...].astype(F32)
    two_ref[...] = mask_ref[...].astype(F32)
    for j in range(n_mode):
        for k in range(nb):
            b = j * nb + k
            for c in range(C):
                send_ref[j, k * LEAD + c, :] = one_ref[c, b, :]
                send_ref[j, (nb + k) * LEAD + c, :] = future_ref[c, b, :]
            send_ref[j, k * LEAD + C, :] = two_ref[b, :]
            send_ref[j, (nb + k) * LEAD + C, :] = jnp.zeros_like(two_ref[b, :])
    rows_ref[:, : D + FF] = dense_ref[:, D : 2 * D + FF].astype(BF)
    rows_ref[:, D + FF :] = thin_rows(dense_ref).astype(BF)


def own_rows(got_ref, all_ref):
    steps = got_ref.shape[2]
    for j in range(got_ref.shape[0]):
        all_ref[:, j * steps : (j + 1) * steps] = got_ref[j]
    half = all_ref.shape[0] // 2
    inputs = all_ref[:half, :]
    mask = inputs
    inputs = jnp.where(iota(inputs.shape, 0) % LEAD == C, 0.0, inputs)
    return inputs, mask, all_ref[half:, :]


def spectra_kernel(sizes, got_ref, cos_ref, sin_ref, dense_ref, send_ref, all_ref):
    n_data, n_mode, nb, _ = sizes
    n_all = n_data * n_mode
    modes = M // n_mode
    wide = D // n_data
    share = FF // n_all
    x, mask, _ = own_rows(got_ref, all_ref)
    count = jnp.sum(jnp.where(iota(mask.shape, 0) % LEAD == C, mask, 0.0))
    low = cos_ref[...].astype(BF)
    inner = mm(low, rows_at(x, 0, LANES).astype(BF), NT)
    low = (-sin_ref[...]).astype(BF)
    inner += mm(low, rows_at(x, nb * LEAD, LANES).astype(BF), NT)
    thin = thin_rows(dense_ref).astype(BF)
    query = mm(thin, dense_ref[:, :D].astype(BF), TN)[:LEAD]
    down = mm(thin, dense_ref[:, 2 * D + FF : 2 * D + 2 * FF].astype(BF), TN)[LEAD : 2 * LEAD]
    row = iota((LEAD, LANES), 0)
    lane = iota((LEAD, LANES), 1)
    for i in range(n_data):
        ours = at_lane(from_lane(query, i * wide, wide), HALF, wide)
        ours = jnp.where((row == C) & (lane == HALF), count, ours)
        for j in range(n_mode):
            d = i * n_mode + j
            block = inner[j * modes : (j + 1) * modes]
            if modes < 16:
                block = jnp.concatenate([block, jnp.zeros((16 - modes, LANES), F32)], axis=0)
            theirs = at_lane(from_lane(down, d * share, share), HALF, share)
            send_ref[d] = block + jnp.concatenate([ours, theirs], axis=0)


def tables_kernel(
    got_ref, cos_ref, sin_ref, a_ref, at_ref, rest_ref, rest_t_ref, target_ref, keep_ref, all_ref
):
    x, mask, target = own_rows(got_ref, all_ref)
    count = x.shape[0]
    keep = [
        jnp.broadcast_to(mask[at + C : at + LEAD], (LEAD, S)) for at in range(0, count, LEAD)
    ]
    keep = jnp.concatenate(keep, axis=0)
    twice = lambda rows: jnp.concatenate([rows_at(rows, 0, HALF)] * 2, axis=0).T
    a_ref[:, 2 * M :] = twice(x).astype(BF)
    at_ref[2 * M :, :] = rows_at(x, 0, HALF).astype(BF)
    target_ref[...] = twice(target)
    keep_ref[...] = twice(keep)
    basis = jnp.concatenate([cos_ref[...], -sin_ref[...]], axis=0)
    low = basis.astype(BF)
    at_ref[: 2 * M, :] = low
    rest_ref[...] = (basis - low.astype(F32)).astype(BF)
    turned = basis.T
    low = turned.astype(BF)
    a_ref[:, : 2 * M] = low
    rest_t_ref[...] = (turned - low.astype(F32)).astype(BF)


def mix_kernel(sizes, got_ref, mixer_ref, send_ref, spec_ref, thin_ref, wide_ref, out_ref):
    n_data, n_mode, nb, _ = sizes
    n_all = n_data * n_mode
    modes = M // n_mode
    nbm = nb * modes
    wide = D // n_data
    share = FF // n_all
    got = got_ref[...]
    thin = jnp.sum(got, axis=0)
    thin_ref[...] = thin
    query = from_lane(thin[:LEAD], HALF, wide)
    query = jnp.where(iota(query.shape, 0) < C, query, 0.0)
    down = from_lane(thin[LEAD:], HALF, share)
    high, low = split(down)
    down = jnp.concatenate([high, low], axis=0).astype(BF)
    spread = []
    for part in range(2):
        block = at_lane(query, part * wide, wide)
        zero = jnp.zeros_like(block)
        for k in range(nb):
            blocks = [block if g == k else zero for g in range(nb)]
            spread.append(jnp.concatenate(blocks, axis=1))
    spread = jnp.concatenate(spread, axis=0)
    inner = got.reshape(n_all * 16, LANES)
    inner = by_halves(fold(jnp.where(iota(inner.shape, 1) < HALF, inner, 0.0)))
    high, low = split(rows_at(spread, 0, HALF))
    spec = mm(inner, jnp.concatenate([high, high], axis=0).astype(BF))
    spec += mm(inner, jnp.concatenate([low, jnp.zeros_like(low)], axis=0).astype(BF))
    for k in range(nb):
        wide_ref[k] = spec[:, k * LANES : (k + 1) * LANES]
    for m in range(modes):
        spec = [wide_ref[k, pl.ds(m, n_all, stride=16), :][:, : 2 * wide] for k in range(nb)]
        spec = jnp.concatenate(spec, axis=0).astype(BF)
        spec_ref[m] = spec
        mixed = mm(spec, mixer_ref[m])
        for k in range(nb):
            out_ref[pl.ds(k * modes + m, n_all, stride=nbm), :] = mixed[
                k * n_all : (k + 1) * n_all
            ]
    for d in range(n_all):
        send_ref[d, :nbm, :] = out_ref[d * nbm : (d + 1) * nbm, :].astype(BF)
        send_ref[d, nbm:, :] = down


def mix_back_kernel(
    sizes, got_ref, mixer_ref, first_ref, stat_ref, send_ref, grad_ref, thin_ref, in_ref, wide_ref
):
    n_data, n_mode, nb, _ = sizes
    n_all = n_data * n_mode
    modes = M // n_mode
    nbm = nb * modes
    wide = D // n_data
    share = FF // n_all
    thin = jnp.zeros((16, LANES), F32)
    for d in range(n_all):
        in_ref[d * nbm : (d + 1) * nbm, :] = got_ref[d, :nbm, :].astype(F32)
        thin += got_ref[d, nbm:, :].astype(F32)
    thin = thin[:LEAD] + thin[LEAD:]
    thin_ref[...] = thin
    if modes < 16:
        wide_ref[...] = jnp.zeros_like(wide_ref)
    for m in range(modes):
        grad = [in_ref[pl.ds(k * modes + m, n_all, stride=nbm), :] for k in range(nb)]
        grad = jnp.concatenate(grad, axis=0).astype(BF)
        grad_ref[m] = grad
        back = mm(grad, mixer_ref[m], NT).astype(BF).astype(F32)
        if 2 * wide < LANES:
            back = jnp.concatenate(
                [back, jnp.zeros((back.shape[0], LANES - 2 * wide), F32)], axis=1
            )
        for k in range(nb):
            wide_ref[k, pl.ds(m, n_all, stride=16), :] = back[k * n_all : (k + 1) * n_all]
    inner = first_ref[...].reshape(n_all * 16, LANES)
    inner = jnp.where(iota(inner.shape, 1) < HALF, inner, 0.0)
    inner = by_halves(fold(inner))
    total = jnp.zeros((LEAD, LANES), F32)
    for k in range(nb):
        query = mm(inner, wide_ref[k].astype(BF), TN)
        query = query[:HALF] + query[HALF:]
        for part in range(2):
            at = (part * nb + k) * LEAD
            total += from_lane(query[at : at + LEAD], part * wide, wide)
    block = total + at_lane(from_lane(thin, 0, share), HALF, share)
    row, lane = iota(block.shape, 0), iota(block.shape, 1)
    stats = jnp.where(lane < HALF, stat_ref[:1, :], stat_ref[1:2, :])
    block = jnp.where(row == C, stats, block)
    for d in range(n_all):
        send_ref[d] = block


def spectral_kernel(
    modes,
    wide,
    ready,
    spec_ref,
    grad_ref,
    w_ref,
    m_ref,
    v_ref,
    ema_ref,
    w_out,
    m_out,
    v_out,
    ema_out,
    low_out,
    pair_ref,
    turn_ref,
):
    ready()
    lower = iota((wide, LANES), 1) < HALF
    half_lower = iota((wide // 2, LANES), 1) < HALF
    for m in range(modes):
        slopes = mm(spec_ref[m], grad_ref[m], TN)
        other = pltpu.roll(slopes[wide:], HALF, 1)
        pair_ref[m] = jnp.where(lower, slopes[:wide] + other, slopes[:wide] - other)
        even = pair_ref[m, pl.ds(0, wide // 2, stride=2), :]
        odd = pair_ref[m, pl.ds(1, wide // 2, stride=2), :]
        real = jnp.where(half_lower, even, pltpu.roll(odd, HALF, 1))
        imag = jnp.where(half_lower, pltpu.roll(even, HALF, 1), odd)
        turn_ref[0, pl.ds(m, wide // 2, stride=modes), :] = real
        turn_ref[1, pl.ds(m, wide // 2, stride=modes), :] = imag
    for part in range(2):
        for at in range(wide // 2):
            cols = slice(at * LANES, (at + 1) * LANES)
            grad = turn_ref[part, at * modes : (at + 1) * modes, :]
            new = adamw(
                w_ref[part, :, cols],
                grad,
                m_ref[part, :, cols],
                v_ref[part, :, cols],
                ema_ref[part, :, cols],
                RATE_SPEC,
            )
            for ref, value in zip((w_out, m_out, v_out, ema_out, low_out), new, strict=True):
                ref[part, :, cols] = value


def rows_kernel(
    sizes,
    n_big,
    got_ref,
    thin_ref,
    steps_ref,
    w_ref,
    m_ref,
    v_ref,
    ema_ref,
    *refs,
):
    big_refs, (loss_ref, w_out, m_out, v_out, ema_out, low_out) = refs[:n_big], refs[n_big:]
    n_data, n_mode, _, total = sizes
    n_all = n_data * n_mode
    wide = D // n_data
    share = FF // n_all
    rows = w_ref.shape[0]
    query = []
    for at in range(D // LANES):
        block = jnp.zeros((LEAD, LANES), F32)
        for i in range(at * LANES // wide, (at + 1) * LANES // wide):
            part = sum(got_ref[i * n_mode + j, :LEAD, :] for j in range(n_mode))
            block += at_lane(part, i * wide % LANES, wide)
        query.append(block)
    query = jnp.concatenate(query, axis=1)
    down = []
    for at in range(FF // LANES):
        block = jnp.zeros((LEAD, LANES), F32)
        for d in range(at * LANES // share, (at + 1) * LANES // share):
            block += at_lane(from_lane(got_ref[d, :LEAD, :], HALF, share), d * share % LANES, share)
        down.append(block)
    down = jnp.where(iota((LEAD, FF), 0) < C, jnp.concatenate(down, axis=1), 0.0)
    norm = SPECTRAL_WEIGHT / (total * M * S)
    stats = sum(got_ref[d, C : C + 1, :] for d in range(n_all))
    steps = steps_ref[C : C + 1, HALF : HALF + 1]
    loss_ref[...] = stats[:, :1] / steps + norm * stats[:, HALF : HALF + 1]

    keep = iota((LEAD, D), 0) < C
    query = jnp.where(keep, query, 0.0)
    query = jnp.concatenate(split(query), axis=0).astype(BF)
    down = jnp.concatenate(split(down), axis=0).astype(BF)
    thin = thin_rows(w_ref)
    embed = at_lane(thin, 0, C) + at_lane(from_lane(thin, 0, C), LEAD, C)
    head = from_lane(thin, LEAD, C)
    head = at_lane(head, 0, C) + at_lane(head, LEAD, C)

    def back(weights, sums):
        sums = jnp.concatenate([sums, jnp.zeros((LANES - 16, sums.shape[1]), BF)], axis=0)
        out = mm(weights.astype(BF), sums, NT)
        return from_lane(out, 0, LEAD) + from_lane(out, LEAD, LEAD)

    own = jnp.concatenate([thin_ref[...], jnp.zeros((LANES - LEAD, LANES), F32)], axis=0).T
    embed_grad = own[HALF : HALF + rows] + back(w_ref[:, :D], query)
    head_grad = own[HALF + rows : HALF + 2 * rows] + back(
        w_ref[:, 2 * D + FF : 2 * D + 2 * FF], down
    )
    last = at_lane(embed_grad, 0, C) + at_lane(head_grad, C, C)

    def update(grad, cols):
        new = adamw(w_ref[:, cols], grad, m_ref[:, cols], v_ref[:, cols], ema_ref[:, cols], RATE_DENSE)
        for ref, value in zip((w_out, m_out, v_out, ema_out, low_out), new, strict=True):
            ref[:, cols] = value

    update(mm(embed[:, :16].astype(BF), query), slice(0, D))
    update(sum(ref[...].astype(F32) for ref in big_refs), slice(D, 2 * D + FF))
    update(mm(head[:, :16].astype(BF), down), slice(2 * D + FF, 2 * D + 2 * FF))
    update(last[:, : 2 * C], slice(2 * D + 2 * FF, 2 * D + 2 * FF + 2 * C))


def per_device(
    series,
    future_values,
    step_mask,
    mode_index,
    dense,
    dense_m,
    dense_v,
    dense_ema,
    spectral,
    spec_m,
    fourier_variance_moment,
    spec_ema,
):
    n_mode = lax.axis_size("mode")
    n_data = lax.axis_size("dp")
    n_all = n_mode * n_data
    time_rows, batch, chans = series.shape
    nb = batch // n_mode
    total = batch * n_data
    modes = M // n_mode
    wide = D // n_data
    rows = dense.shape[0]
    shape = jax.ShapeDtypeStruct
    sizes = (n_data, n_mode, nb, total)
    tiled = rows % 16 == 0 and n_mode == 4 and n_data >= 4

    send, weights = call(
        partial(pack_kernel, sizes),
        (shape((n_mode, 2 * nb * LEAD, time_rows), F32), shape((rows, D + FF + LANES), BF)),
        (series.transpose(2, 1, 0), future_values.transpose(2, 1, 0), step_mask.T, dense),
        [pltpu.VMEM((chans, batch, time_rows), F32), pltpu.VMEM((batch, time_rows), F32)],
        name="pack",
        ahead=(0, 1, 2, 3),
    )
    me = jnp.stack([lax.axis_index("dp"), lax.axis_index("mode")]).astype(jnp.int32)
    own = exchange(send, "mode")
    cosv, sinv = tables(mode_index)
    weights = [gather_rows(weights)] if not tiled else gather_tiles_first(weights)
    if tiled:
        weights = gather_tiles_second(*weights)

    whole_rows = [pltpu.VMEM((2 * nb * LEAD, S), F32)]
    send = call(
        partial(spectra_kernel, sizes),
        shape((n_all, 16, LANES), F32),
        (own, cosv, sinv, dense),
        whole_rows,
        name="spectra",
    )
    first = exchange(send, AXES)
    ins = call(
        tables_kernel,
        (
            shape((S, 4 * M), BF),
            shape((3 * M, S), BF),
            shape((2 * M, S), BF),
            shape((S, 2 * M), BF),
            shape((S, LANES), F32),
            shape((S, LANES), F32),
        ),
        (own, cosv, sinv),
        whole_rows,
        name="tables",
        cost=10**10,
    )
    first, *ins = together(first, *ins)
    if tiled:
        weights = gather_tiles_third(*weights)

    w_low = spectral.astype(BF).reshape(2, modes, wide, E)
    mixer = jnp.concatenate(
        [
            jnp.concatenate([w_low[0], w_low[1]], axis=2),
            jnp.concatenate([-w_low[1], w_low[0]], axis=2),
        ],
        axis=1,
    )
    scratch = [
        pltpu.VMEM((nb, n_all * 16, LANES), F32),
        pltpu.VMEM((n_all * nb * modes, LANES), F32),
    ]
    send, spec, thin = call(
        partial(mix_kernel, sizes),
        (
            shape((n_all, nb * modes + 16, LANES), BF),
            shape((modes, total, 2 * wide), BF),
            shape((16, LANES), F32),
        ),
        (first, mixer),
        scratch,
        name="mix",
    )
    if tiled:
        send, *weights = together(send, *weights)
        weights = gather_tiles_last(weights)
    got = exchange(send, AXES)
    steps = thin

    send, stats, *big = block(
        steps[C, HALF].reshape(1),
        me,
        weights,
        (got, *ins),
        sizes + (True,) if tiled else sizes,
    )
    got = exchange(send, AXES)
    if tiled:
        big = scatter_tiles_first(*big)
        got, *big = together(got, *big)
        big = scatter_tiles_second(*big)
    send, grad_mixed, thin = call(
        partial(mix_back_kernel, sizes),
        (
            shape((n_all, LEAD, LANES), F32),
            shape((modes, total, LANES), BF),
            shape((LEAD, LANES), F32),
        ),
        (got, mixer, first, stats),
        scratch[::-1],
        name="mix_back",
        cost=10**10,
    )
    if tiled:
        grad_mixed, big = together(grad_mixed, big)
    spec_out = call(
        partial(spectral_kernel, modes, wide),
        (shape(spectral.shape, F32),) * 4 + (shape(spectral.shape, BF),),
        (spec, grad_mixed, spectral, spec_m, fourier_variance_moment, spec_ema),
        [
            pltpu.VMEM((modes, wide, LANES), F32),
            pltpu.VMEM((2, modes * wide // 2, LANES), F32),
        ],
        name="spectral",
        ahead=(0, 1, 2, 3, 4, 5),
        cost=10**10,
    )
    got = exchange(send, AXES)
    big = scatter_tiles_third(*big) if tiled else [scatter_rows(big[0], rows)]
    loss, *dense_out = call(
        partial(rows_kernel, sizes, len(big)),
        (shape((1, 1), F32),) + (shape(dense.shape, F32),) * 4 + (shape(dense.shape, BF),),
        (got, thin, steps, dense, dense_m, dense_v, dense_ema, *big),
        name="rows",
    )
    return (loss.reshape(()),) + tuple(dense_out) + tuple(spec_out)


def solution(mesh):
    rows = P(("dp", "mode"), None)
    mixing = P(None, "mode", "dp")
    return jax.shard_map(
        per_device,
        mesh=mesh,
        in_specs=(P("mode", "dp", None), P("mode", "dp", None), P("mode", "dp"), P())
        + (rows,) * 4
        + (mixing,) * 4,
        out_specs=(P(),) + (rows,) * 5 + (mixing,) * 5,
        check_vma=False,
    )
```

```python
import math
from functools import partial

import jax
import jax.numpy as jnp
from jax import lax
from jax.experimental import pallas as pl
from jax.experimental.pallas import tpu as pltpu
from jax.sharding import PartitionSpec as P

D = 512
H = 8
E = 64
FF = 2048
M = 64
C = 7
S = 768
LANES = 128

SPECTRAL_WEIGHT = 0.5
RATE_DENSE = 0.02
RATE_SPEC = 0.1
BF = jnp.bfloat16
F32 = jnp.float32
AXES = ("dp", "mode")
SLOPE = jnp.bfloat16
VMEM_BYTES = 60 * 1024 * 1024
FULL_BYTES = 60 * 1024 * 1024
SMALL_BYTES = 16 * 1024 * 1024


def plain(spec, left, right):
    return jnp.einsum(spec, left, right, preferred_element_type=F32)


def exact(spec, left, right):
    return jnp.einsum(
        spec, left, right, precision=lax.Precision.HIGHEST, preferred_element_type=F32
    )


def tables(mode_index):
    steps = jnp.arange(S, dtype=jnp.int32)
    phase = mode_index[:, None] * steps[None, :] % S
    angle = phase.astype(F32) * (2.0 * math.pi / S)
    return (jnp.cos(angle), jnp.sin(angle))


def unpack(whole):
    return (
        whole[:, :D],
        whole[:, D : 2 * D],
        whole[:, 2 * D : 2 * D + FF],
        whole[:, 2 * D + FF : 2 * D + 2 * FF],
        whole[:, 2 * D + 2 * FF : 2 * D + 2 * FF + C],
        whole[:, 2 * D + 2 * FF + C :],
    )


def adamw(weight, grad, first, second, average, rate):
    first_new = 0.5 * first + 0.5 * grad
    second_new = 0.5 * second + 0.5 * grad * grad
    weight_new = weight - rate * (first_new / (jnp.sqrt(second_new) + 1e-08) + 0.01 * weight)
    average_new = 0.9 * average + 0.1 * weight_new
    return (weight_new, first_new, second_new, average_new, weight_new.astype(BF))


def halves(x):
    high = x.astype(BF)
    return high, (x - high.astype(F32)).astype(BF)


def fill(x, size, axis):
    wanted = list(x.shape)
    wanted[axis] = size - x.shape[axis]
    return jnp.concatenate([x, jnp.zeros(wanted, x.dtype)], axis=axis) if wanted[axis] else x


def exchange(x, axes):
    return lax.all_to_all(x, axes, 0, 0, tiled=True)


def partners(step):
    count = lax.axis_size("mode")
    return [(index, index ^ step) for index in range(count)]


def bit_of(step):
    return lax.div(lax.axis_index("mode"), step) % 2


def steps_of_mode():
    return [1 << bit for bit in range(lax.axis_size("mode").bit_length() - 1)]


def by_xor(x, axis, step):
    count = lax.axis_size(axis)
    return lax.ppermute(x, axis, [(index, index ^ step) for index in range(count)])


def tile_offsets(n_data):
    cut = n_data // 4
    low = [2 * step for step in range(cut)]
    high = [2 * step for step in range(cut, 2 * cut)]
    ones = lambda data: [index + 1 for index in data]
    offsets = [
        (low + ones(low), [0] * 2 * cut),
        (low + ones(low), [2] * 2 * cut),
        (high + high, [0] * cut + [2] * cut),
        (ones(high) + ones(high), [0] * cut + [2] * cut),
    ]
    return offsets + [(data, [index + 1 for index in mode]) for data, mode in offsets]


def gather_tiles_first(x):
    n_data = lax.axis_size("dp")
    deep = [x] + [by_xor(x, "dp", 2 * step) for step in range(1, n_data // 2)]
    cut = len(deep) // 2
    return jnp.stack(deep[:cut]), jnp.stack(deep[cut:])


def gather_tiles_second(first, second):
    first = jnp.concatenate([first, by_xor(first, "dp", 1)])
    return first, jnp.concatenate([second, by_xor(second, "mode", 2)])


def gather_tiles_third(first, second):
    return [first, by_xor(first, "mode", 2), second, by_xor(second, "dp", 1)]


def gather_tiles_last(pieces):
    return pieces + [by_xor(piece, "mode", 1) for piece in pieces]


def tile_order(n_data):
    cut = n_data // 4
    low = [2 * step for step in range(cut)]
    high = [2 * step for step in range(cut, 2 * cut)]
    groups = [
        [(data + x, 2) for data in low for x in (0, 1)],
        [(data + x, 0) for data in low for x in (0, 1)],
        [(data + 1, 2 * y) for data in high for y in (0, 1)],
        [(data, 2 * y) for data in high for y in (0, 1)],
    ]
    return [[(data, mode + core) for data, mode in group] for core in (1, 0) for group in groups]


def together(*values):
    return lax.optimization_barrier(values)


def total_of(terms, pick):
    return sum(term[pick].astype(F32) for term in terms)


def scatter_tiles_first(away, stay):
    pairs = lambda terms: [x.reshape((x.shape[0] // 2, 2) + x.shape[1:]) for x in terms]
    come = by_xor(away, "mode", 1)
    first = by_xor(total_of([stay, come], 0).astype(BF), "mode", 2)
    second = by_xor(total_of([stay, come], 2).astype(BF), "dp", 1)
    first = pairs([stay[1], come[1], first])
    second = pairs([stay[3], come[3], second])
    away = [total_of(terms, (slice(None), 1)).astype(BF) for terms in (first, second)]
    return away + [[x[:, 0] for x in terms] for terms in (first, second)]


def scatter_tiles_second(first_away, second_away, first, second):
    return [first + [by_xor(first_away, "dp", 1)], second + [by_xor(second_away, "mode", 2)]]


def scatter_tiles_third(first, second):
    cut = first[0].shape[0]
    come = []
    for step in range(1, 2 * cut):
        terms, at = (first, step) if step < cut else (second, step - cut)
        come.append(by_xor(total_of(terms, at).astype(BF), "dp", 2 * step))
    return [total_of(first, 0)] + come


def gather_rows(x):
    n_data = lax.axis_size("dp")
    held = exchange(jnp.broadcast_to(x[None], (n_data,) + x.shape), "dp")[:, None]
    for step in reversed(steps_of_mode()):
        other = lax.ppermute(held, "mode", partners(step))
        first = bit_of(step) == 0
        pair = [jnp.where(first, held, other), jnp.where(first, other, held)]
        held = jnp.concatenate(pair, axis=1) if step > 1 else jnp.stack(pair, axis=2)
    return held.reshape(-1, x.shape[1])


def scatter_rows(x, rows):
    n_data, n_mode = lax.axis_size("dp"), lax.axis_size("mode")
    held = x.reshape(n_data, n_mode, rows, x.shape[1])
    for step in steps_of_mode():
        held = held.reshape(n_data, held.shape[1] // 2, 2, rows, x.shape[1])
        bit = bit_of(step)
        away = lax.dynamic_index_in_dim(held, 1 - bit, 2, keepdims=False)
        stay = lax.dynamic_index_in_dim(held, bit, 2, keepdims=False)
        other = lax.ppermute(away, "mode", partners(step))
        held = (stay.astype(F32) + other.astype(F32)).astype(BF)
    held = exchange(held.reshape(n_data, rows, x.shape[1]), "dp")
    return jnp.sum(held.astype(F32), axis=0)


NN = (((1,), (0,)), ((), ()))
NT = (((1,), (1,)), ((), ()))
TN = (((0,), (0,)), ((), ()))
FIRST = 2.0 * math.sqrt(2.0 / math.pi)
THIRD = FIRST * 0.044715
GATES = 1024
LEAD = 8
HALF = 64


def mm(left, right, dims=NN):
    return lax.dot_general(left, right, dims, preferred_element_type=F32)


def iota(shape, axis):
    return lax.broadcasted_iota(jnp.int32, shape, axis)


def split(x):
    high = x.astype(BF).astype(F32)
    return high, x - high


def by_halves(x):
    high, low = split(x)
    return jnp.where(iota(x.shape, 1) < HALF, high, low).astype(BF)


def fold(x):
    return x + pltpu.roll(x, HALF, 1)


def rows_at(x, first, count):
    parts = []
    if first:
        parts.append(jnp.zeros((first, x.shape[1]), F32))
    parts.append(x)
    if count - first - x.shape[0]:
        parts.append(jnp.zeros((count - first - x.shape[0], x.shape[1]), F32))
    return jnp.concatenate(parts, axis=0)


def row_groups(x):
    return sum(x[at : at + LEAD] for at in range(0, x.shape[0], LEAD))


def block_kernel(sizes, count_ref, me_ref, *refs):
    if len(sizes) == 4:
        block_steps(sizes, lambda what: None, count_ref, *refs)
        return
    n_data, n_mode = sizes[:2]
    rows = D // n_data // n_mode
    offsets = tile_offsets(n_data)
    n_pieces = len(offsets)
    pieces, got_ref, sources, refs = refs[:n_pieces], refs[n_pieces], refs[n_pieces + 1 : n_pieces + 7], refs[n_pieces + 7 :]
    send_ref, stat_ref, away_ref, stay_ref, row_sems, sems, w_ref = refs[:7]
    places, scratch = refs[7:13], refs[13:]
    act_ref = scratch[5]

    def rows_of(data, mode):
        owner = (me_ref[0] ^ data) * n_mode + (me_ref[1] ^ mode)
        return pl.ds(pl.multiple_of(owner * rows, rows), rows)

    row_copies = []
    for ref, (data, mode) in zip(pieces, offsets, strict=True):
        for at, (one, two) in enumerate(zip(data, mode, strict=True)):
            place = w_ref.at[rows_of(one, two), :]
            row_copies.append(
                pltpu.make_async_copy(ref.at[at], place, row_sems.at[len(row_copies)])
            )
            row_copies[-1].start()
    copies = [
        pltpu.make_async_copy(source, place, sems.at[at])
        for at, (source, place) in enumerate(zip(sources, places, strict=True))
    ]
    for copy in copies:
        copy.start()
    waits = {"rows": row_copies, "a": copies[:1], "rest": copies[1:]}

    def ready(what):
        for copy in waits[what]:
            copy.wait()

    block_steps(sizes, ready, count_ref, w_ref, got_ref, *places, send_ref, stat_ref, None, *scratch)
    for at, group in enumerate(tile_order(n_data)):
        ref = away_ref if at < 4 else stay_ref
        for index, (data, mode) in enumerate(group):
            ref[at % 4, index, :, :D] = act_ref[1, rows_of(data, mode), :D]
            ref[at % 4, index, :, D:] = act_ref[0, rows_of(data, mode), :]


def block_steps(
    sizes,
    ready,
    count_ref,
    w_ref,
    got_ref,
    a_ref,
    at_ref,
    rest_ref,
    rest_t_ref,
    target_ref,
    keep_ref,
    send_ref,
    stat_ref,
    big_ref,
    wdup_ref,
    x_ref,
    v_ref,
    r_ref,
    wd_ref,
    act_ref,
    slope_ref,
    fc_ref,
    zx_ref,
    j_ref,
):
    n_data, n_mode, nb, total = sizes[:4]
    n_all = n_data * n_mode
    modes = M // n_mode
    nbm = nb * modes
    share = FF // n_all
    rows = D // n_all
    scale = 2.0 / S
    norm = SPECTRAL_WEIGHT / (total * M * S)
    chunks = FF // GATES

    for i in range(n_data):
        blocks = [got_ref[i * n_mode + j, :nbm, :].astype(F32) for j in range(n_mode)]
        for k in range(nb):
            column = [block[k * modes : (k + 1) * modes] for block in blocks]
            x_ref[k * M : (k + 1) * M, i * LANES : (i + 1) * LANES] = jnp.concatenate(
                column, axis=0
            ).astype(BF)

    per = LANES // share
    for at in range(FF // LANES):
        block = jnp.zeros((16, LANES), F32)
        for q in range(per):
            piece = got_ref[at * per + q, nbm : nbm + 16, :].astype(F32)
            piece = pltpu.roll(piece, q * share, 1) if q else piece
            block = jnp.where(iota(block.shape, 1) // share == q, piece, block)
        spread = [
            rows_at(jnp.concatenate([half] * nb, axis=0), 0, HALF)
            for half in (block[:LEAD], block[LEAD:])
        ]
        wd_ref[:, at * LANES : (at + 1) * LANES] = jnp.concatenate(spread, axis=0).astype(BF)
    ready("rows")
    for i in range(n_data):
        head = i * H // n_data
        block = w_ref[head * E : (head + 1) * E, :D]
        wdup_ref[2 * i * E : (2 * i + 1) * E, :] = block
        wdup_ref[(2 * i + 1) * E : (2 * i + 2) * E, :] = block
    x_all = x_ref[...]
    real_lane = iota(x_all.shape, 1) % LANES < HALF
    zero = jnp.zeros_like(x_all)
    x_real = jnp.where(real_lane, x_all, zero)
    x_imag = jnp.where(real_lane, zero, x_all)
    line_real = scale * mm(x_real, wdup_ref[...])
    line_imag = scale * mm(x_imag, wdup_ref[...])
    for k in range(nb):
        v_ref[2 * k * M : (2 * k + 1) * M, :] = line_real[k * M : (k + 1) * M].astype(BF)
        v_ref[(2 * k + 1) * M : (2 * k + 2) * M, :] = line_imag[k * M : (k + 1) * M].astype(BF)

    thin_t = w_ref[:, D + FF :].astype(F32).T
    embed_t = thin_t[:LEAD]
    head_t = thin_t[LEAD : 2 * LEAD]
    pad = [jnp.zeros((HALF - nb * LEAD, D), F32)] if nb * LEAD < HALF else []
    embed_all = jnp.concatenate([embed_t] * nb + pad, axis=0).astype(BF)
    head_all = jnp.concatenate([head_t] * nb + pad, axis=0).astype(BF)
    head_twice = jnp.concatenate([head_all, head_all], axis=0)
    embed_twice = jnp.concatenate([embed_t, embed_t], axis=0).astype(BF)

    for c in range(FF // 512):
        cols = slice(c * 512, (c + 1) * 512)
        w_up = w_ref[:, D + c * 512 : D + (c + 1) * 512]
        lifted = mm(v_ref[...], w_up)
        thin = mm(embed_twice, w_up)[:LEAD]
        high, low = split(thin)
        for k in range(nb):
            r_ref[k, : 2 * M, cols] = lifted[2 * k * M : 2 * (k + 1) * M].astype(BF)
            r_ref[k, 2 * M :, cols] = jnp.concatenate(
                [rows_at(high, k * LEAD, HALF), rows_at(low, k * LEAD, HALF)], axis=0
            ).astype(BF)

    parts = [mm(head_all[:16], v_ref[2 * k * M : 2 * (k + 1) * M, :], NT)[:LEAD] for k in range(nb)]
    by_head = rows_at(jnp.concatenate(parts, axis=0), 0, HALF)
    cross = mm(head_all, jnp.concatenate([embed_all, jnp.zeros_like(embed_all)], axis=0), NT)
    cross = jnp.where(iota(cross.shape, 0) // LEAD == iota(cross.shape, 1) // LEAD, cross, 0.0)
    high, low = split(jnp.concatenate([by_head, cross], axis=1))
    by_head = jnp.concatenate([high, low], axis=0).astype(BF)
    ready("a")
    fc_ref[...] = mm(a_ref[...], by_head, NT)

    own_lane = iota((S, LANES), 1) % HALF // LEAD

    def forward(step, carry):
        k = step // chunks
        cols = pl.ds(pl.multiple_of(step % chunks * GATES, GATES), GATES)
        gate = mm(a_ref[...], r_ref[k, :, cols])
        square = gate * gate
        sig = 0.5 * jnp.tanh(gate * (square * (0.5 * THIRD) + 0.5 * FIRST)) + 0.5
        act = gate * sig
        low = act.astype(BF)
        act_ref[k, :, cols] = low
        slope = sig + act * (1.0 - sig) * (square * (3.0 * THIRD) + FIRST)
        slope_ref[k, :, cols] = slope.astype(slope_ref.dtype)
        fc_ref[...] += jnp.where(own_lane == k, mm(low, wd_ref[:, cols], NT), 0.0)
        return carry

    lax.fori_loop(0, nb * chunks, forward, 0, unroll=nb * chunks)

    ready("rest")
    keep = keep_ref[...]
    masked = keep * (fold(fc_ref[...]) - target_ref[...])
    two = by_halves(masked)
    err = fold(mm(at_ref[: 2 * M, :], two) + mm(rest_ref[...], two))
    stat_ref[...] = jnp.concatenate(
        [
            jnp.full((1, LANES), 0.5 * jnp.sum(masked * masked)),
            jnp.full((1, LANES), 0.5 * jnp.sum(err * err)),
            jnp.zeros((6, LANES), F32),
        ],
        axis=0,
    )
    two = by_halves(err)
    back = fold(mm(a_ref[:, : 2 * M], two) + mm(rest_t_ref[...], two))
    g_fc = keep * ((2.0 / count_ref[0]) * masked + (2.0 * norm) * back)
    g_low = g_fc.astype(BF)
    g_turn = g_fc.T[:HALF].astype(BF)
    zx_ref[...] = jnp.zeros_like(zx_ref)
    j_ref[...] = jnp.zeros_like(j_ref)

    def backward(step, carry):
        k = step // chunks
        cols = pl.ds(pl.multiple_of(step % chunks * GATES, GATES), GATES)
        fed = mm(jnp.where(own_lane == k, g_fc, 0.0).astype(BF), wd_ref[:, cols])
        g_gate = (fed * slope_ref[k, :, cols].astype(F32)).astype(BF)
        turned = mm(at_ref[...], g_gate)
        r_ref[k, : 2 * M, cols] = turned[: 2 * M].astype(BF)
        own = iota((HALF, GATES), 0) // LEAD == k
        zx_ref[:, cols] += jnp.where(own, turned[2 * M :], 0.0)
        j_ref[:, cols] += jnp.where(own, mm(g_turn, act_ref[k, :, cols]), 0.0)
        return carry

    lax.fori_loop(0, nb * chunks, backward, 0, unroll=nb * chunks)

    back_fc = by_halves(mm(at_ref[...], g_low))
    lane_of = iota((2 * M, LANES), 1) % HALF // LEAD
    nothing = jnp.zeros((2 * M, LANES), F32)
    back_rows = jnp.concatenate(
        [jnp.where(lane_of == k, back_fc[: 2 * M].astype(F32), nothing) for k in range(nb)], axis=0
    ).astype(BF)
    cross = jnp.where(
        iota((HALF, LANES), 0) // LEAD == iota((HALF, LANES), 1) % HALF // LEAD,
        back_fc[2 * M :].astype(F32),
        0.0,
    ).astype(BF)
    v_all = v_ref[...]
    z_all = r_ref[:, : 2 * M, :].reshape(nb * 2 * M, FF)
    high, low = split(row_groups(zx_ref[...]))
    zx = jnp.concatenate([high, low], axis=0).astype(BF)
    w_up = w_ref[:, D : D + FF]
    back_block = mm(z_all, w_up, NT) + mm(back_rows, head_twice)
    turned = (scale * back_block).astype(BF)
    embed_grad = row_groups(mm(zx, w_up, NT)) + row_groups(mm(cross, head_twice))
    head_grad = row_groups(mm(back_rows, v_all, TN)) + row_groups(mm(cross, embed_all, TN))
    down_grad = row_groups(j_ref[...])

    turned_real = jnp.concatenate(
        [turned[2 * k * M : (2 * k + 1) * M] for k in range(nb)], axis=0
    )
    turned_imag = jnp.concatenate(
        [turned[(2 * k + 1) * M : (2 * k + 2) * M] for k in range(nb)], axis=0
    )
    p_real = mm(turned_real, wdup_ref[...], NT)
    p_imag = mm(turned_imag, wdup_ref[...], NT)
    real_lane = iota((modes, LANES), 1) < HALF
    lane = iota((LEAD, LANES), 1)
    for i in range(n_data):
        cols = slice(i * LANES, (i + 1) * LANES)
        for j in range(n_mode):
            d = i * n_mode + j
            pieces = []
            for k in range(nb):
                at = slice(k * M + j * modes, k * M + (j + 1) * modes)
                pieces.append(jnp.where(real_lane, p_real[at, cols], p_imag[at, cols]))
            send_ref[d, :nbm, :] = jnp.concatenate(pieces, axis=0).astype(BF)
            out = jnp.zeros((LEAD, LANES), F32)
            for source, width, place in (
                (down_grad, share, 0),
                (embed_grad, rows, HALF),
                (head_grad, rows, HALF + rows),
            ):
                first = d * width // LANES * LANES
                piece = source[:, first : first + LANES]
                shift = (place - (d * width - first)) % LANES
                piece = pltpu.roll(piece, shift, 1) if shift else piece
                out = jnp.where((lane >= place) & (lane < place + width), piece, out)
            high, low = split(out)
            send_ref[d, nbm:, :] = jnp.concatenate([high, low], axis=0).astype(BF)

    x_all = x_ref[...]
    real_lane = iota(x_all.shape, 1) % LANES < HALF
    x_real = jnp.where(real_lane, x_all, zero)
    x_imag = jnp.where(real_lane, zero, x_all)
    out_grad = mm(x_real, turned_real, TN) + mm(x_imag, turned_imag, TN)
    each = n_data // H
    for head in range(H):
        block = 0.0
        for i in range(head * each, (head + 1) * each):
            block += out_grad[2 * i * E : (2 * i + 1) * E] + out_grad[(2 * i + 1) * E : (2 * i + 2) * E]
        out = act_ref.at[1] if big_ref is None else big_ref
        out[head * E : (head + 1) * E, :D] = block.astype(BF)
    for c in range(FF // 512):
        cols = slice(c * 512, (c + 1) * 512)
        up_grad = mm(v_all, z_all[:, cols], TN) + mm(embed_twice, zx[:, cols], TN)
        if big_ref is None:
            act_ref[0, :D, cols] = up_grad.astype(BF)
        else:
            big_ref[:, D + c * 512 : D + (c + 1) * 512] = up_grad.astype(BF)


def block(count, me, weights, ins, sizes):
    n_data, n_mode, nb = sizes[:3]
    tiled = len(sizes) > 4
    whole = pl.BlockSpec(memory_space=pltpu.VMEM)
    far = pl.BlockSpec(memory_space=pl.ANY if tiled else pltpu.VMEM)
    big = [jax.ShapeDtypeStruct((D, D + FF), BF)]
    scratch = []
    if tiled:
        half = (4, n_data * n_mode // 8, D // n_data // n_mode, D + FF)
        big = [jax.ShapeDtypeStruct(half, BF)] * 2
        scratch = [
            pltpu.SemaphoreType.DMA((n_data * n_mode,)),
            pltpu.SemaphoreType.DMA((6,)),
            pltpu.VMEM((D, D + FF + LANES), BF),
        ]
        scratch += [pltpu.VMEM(x.shape, x.dtype) for x in ins[1:]]
    return pl.pallas_call(
        partial(block_kernel, sizes),
        out_shape=(
            jax.ShapeDtypeStruct(ins[0].shape, BF),
            jax.ShapeDtypeStruct((8, LANES), F32),
            *big,
        ),
        in_specs=[pl.BlockSpec(memory_space=pltpu.SMEM)] * 2
        + [far] * len(weights)
        + [whole]
        + [far] * (len(ins) - 1),
        out_specs=(whole,) * (2 + len(big)),
        scratch_shapes=scratch
        + [
            pltpu.VMEM((2 * n_data * E, D), BF),
            pltpu.VMEM((nb * M, n_data * LANES), BF),
            pltpu.VMEM((nb * 2 * M, D), BF),
            pltpu.VMEM((nb, 4 * M, FF), BF),
            pltpu.VMEM((LANES, FF), BF),
            pltpu.VMEM((nb, S, FF), BF),
            pltpu.VMEM((nb, S, FF), SLOPE),
            pltpu.VMEM((S, LANES), F32),
            pltpu.VMEM((HALF, FF), F32),
            pltpu.VMEM((HALF, FF), F32),
        ],
        compiler_params=pltpu.CompilerParams(vmem_limit_bytes=VMEM_BYTES),
        name="block",
    )(count, me, *weights, *ins)


def at_lane(x, first, width):
    x = pltpu.roll(x, first, 1) if first else x
    lane = iota(x.shape, 1)
    return jnp.where((lane >= first) & (lane < first + width), x, 0.0)


def from_lane(x, first, width):
    base = first // LANES * LANES
    x = x[:, base : base + LANES]
    shift = (LANES - (first - base)) % LANES
    x = pltpu.roll(x, shift, 1) if shift else x
    return jnp.where(iota(x.shape, 1) < width, x, 0.0)


def staged(kernel, ahead, *refs):
    sems = refs[-1]
    n_held = len(refs) - 1 - len(ahead)
    held = list(refs[:n_held])
    copies = []
    for at, (index, place) in enumerate(zip(ahead, refs[n_held:-1], strict=True)):
        copies.append(pltpu.make_async_copy(refs[index], place, sems.at[at]))
        copies[-1].start()
        held[index] = place

    def ready():
        for copy in copies:
            copy.wait()

    kernel(ready, *held)


def call(kernel, outs, ins, scratch=(), name=None, cost=0, ahead=()):
    whole = pl.BlockSpec(memory_space=pltpu.VMEM)
    in_specs = [whole] * len(ins)
    scratch = list(scratch)
    if ahead:
        kernel = partial(staged, kernel, ahead)
        for index in ahead:
            in_specs[index] = pl.BlockSpec(memory_space=pl.ANY)
            scratch.append(pltpu.VMEM(ins[index].shape, ins[index].dtype))
        scratch.append(pltpu.SemaphoreType.DMA((len(ahead),)))
    return pl.pallas_call(
        kernel,
        out_shape=outs,
        in_specs=in_specs,
        out_specs=jax.tree.map(lambda _: whole, outs),
        scratch_shapes=scratch,
        compiler_params=pltpu.CompilerParams(vmem_limit_bytes=FULL_BYTES if ahead else SMALL_BYTES),
        name=name,
        cost_estimate=pl.CostEstimate(flops=cost, bytes_accessed=cost // 10, transcendentals=0)
        if cost
        else None,
    )(*ins)


def thin_rows(dense_ref):
    thin = dense_ref[:, 2 * D + 2 * FF :]
    thin = jnp.concatenate([thin, jnp.zeros((thin.shape[0], LANES - 2 * C), F32)], axis=1)
    return at_lane(thin, 0, C) + at_lane(from_lane(thin, C, C), LEAD, C)


def pack_kernel(sizes, ready, series_ref, future_ref, mask_ref, dense_ref, send_ref, rows_ref, one_ref, two_ref):
    n_mode, nb = sizes[1:3]
    ready()
    one_ref[...] = series_ref[...].astype(F32)
    two_ref[...] = mask_ref[...].astype(F32)
    for j in range(n_mode):
        for k in range(nb):
            b = j * nb + k
            for c in range(C):
                send_ref[j, k * LEAD + c, :] = one_ref[c, b, :]
                send_ref[j, (nb + k) * LEAD + c, :] = future_ref[c, b, :]
            send_ref[j, k * LEAD + C, :] = two_ref[b, :]
            send_ref[j, (nb + k) * LEAD + C, :] = jnp.zeros_like(two_ref[b, :])
    rows_ref[:, : D + FF] = dense_ref[:, D : 2 * D + FF].astype(BF)
    rows_ref[:, D + FF :] = thin_rows(dense_ref).astype(BF)


def own_rows(got_ref, all_ref):
    steps = got_ref.shape[2]
    for j in range(got_ref.shape[0]):
        all_ref[:, j * steps : (j + 1) * steps] = got_ref[j]
    half = all_ref.shape[0] // 2
    inputs = all_ref[:half, :]
    mask = inputs
    inputs = jnp.where(iota(inputs.shape, 0) % LEAD == C, 0.0, inputs)
    return inputs, mask, all_ref[half:, :]


def spectra_kernel(sizes, got_ref, cos_ref, sin_ref, dense_ref, send_ref, all_ref):
    n_data, n_mode, nb, _ = sizes
    n_all = n_data * n_mode
    modes = M // n_mode
    wide = D // n_data
    share = FF // n_all
    x, mask, _ = own_rows(got_ref, all_ref)
    count = jnp.sum(jnp.where(iota(mask.shape, 0) % LEAD == C, mask, 0.0))
    low = cos_ref[...].astype(BF)
    inner = mm(low, rows_at(x, 0, LANES).astype(BF), NT)
    low = (-sin_ref[...]).astype(BF)
    inner += mm(low, rows_at(x, nb * LEAD, LANES).astype(BF), NT)
    thin = thin_rows(dense_ref).astype(BF)
    query = mm(thin, dense_ref[:, :D].astype(BF), TN)[:LEAD]
    down = mm(thin, dense_ref[:, 2 * D + FF : 2 * D + 2 * FF].astype(BF), TN)[LEAD : 2 * LEAD]
    row = iota((LEAD, LANES), 0)
    lane = iota((LEAD, LANES), 1)
    for i in range(n_data):
        ours = at_lane(from_lane(query, i * wide, wide), HALF, wide)
        ours = jnp.where((row == C) & (lane == HALF), count, ours)
        for j in range(n_mode):
            d = i * n_mode + j
            block = inner[j * modes : (j + 1) * modes]
            if modes < 16:
                block = jnp.concatenate([block, jnp.zeros((16 - modes, LANES), F32)], axis=0)
            theirs = at_lane(from_lane(down, d * share, share), HALF, share)
            send_ref[d] = block + jnp.concatenate([ours, theirs], axis=0)


def tables_kernel(
    got_ref, cos_ref, sin_ref, a_ref, at_ref, rest_ref, rest_t_ref, target_ref, keep_ref, all_ref
):
    x, mask, target = own_rows(got_ref, all_ref)
    count = x.shape[0]
    keep = [
        jnp.broadcast_to(mask[at + C : at + LEAD], (LEAD, S)) for at in range(0, count, LEAD)
    ]
    keep = jnp.concatenate(keep, axis=0)
    twice = lambda rows: jnp.concatenate([rows_at(rows, 0, HALF)] * 2, axis=0).T
    a_ref[:, 2 * M :] = twice(x).astype(BF)
    at_ref[2 * M :, :] = rows_at(x, 0, HALF).astype(BF)
    target_ref[...] = twice(target)
    keep_ref[...] = twice(keep)
    basis = jnp.concatenate([cos_ref[...], -sin_ref[...]], axis=0)
    low = basis.astype(BF)
    at_ref[: 2 * M, :] = low
    rest_ref[...] = (basis - low.astype(F32)).astype(BF)
    turned = basis.T
    low = turned.astype(BF)
    a_ref[:, : 2 * M] = low
    rest_t_ref[...] = (turned - low.astype(F32)).astype(BF)


def mix_kernel(sizes, got_ref, mixer_ref, send_ref, spec_ref, thin_ref, wide_ref, out_ref):
    n_data, n_mode, nb, _ = sizes
    n_all = n_data * n_mode
    modes = M // n_mode
    nbm = nb * modes
    wide = D // n_data
    share = FF // n_all
    got = got_ref[...]
    thin = jnp.sum(got, axis=0)
    thin_ref[...] = thin
    query = from_lane(thin[:LEAD], HALF, wide)
    query = jnp.where(iota(query.shape, 0) < C, query, 0.0)
    down = from_lane(thin[LEAD:], HALF, share)
    high, low = split(down)
    down = jnp.concatenate([high, low], axis=0).astype(BF)
    spread = []
    for part in range(2):
        block = at_lane(query, part * wide, wide)
        zero = jnp.zeros_like(block)
        for k in range(nb):
            blocks = [block if g == k else zero for g in range(nb)]
            spread.append(jnp.concatenate(blocks, axis=1))
    spread = jnp.concatenate(spread, axis=0)
    inner = got.reshape(n_all * 16, LANES)
    inner = by_halves(fold(jnp.where(iota(inner.shape, 1) < HALF, inner, 0.0)))
    high, low = split(rows_at(spread, 0, HALF))
    spec = mm(inner, jnp.concatenate([high, high], axis=0).astype(BF))
    spec += mm(inner, jnp.concatenate([low, jnp.zeros_like(low)], axis=0).astype(BF))
    for k in range(nb):
        wide_ref[k] = spec[:, k * LANES : (k + 1) * LANES]
    for m in range(modes):
        spec = [wide_ref[k, pl.ds(m, n_all, stride=16), :][:, : 2 * wide] for k in range(nb)]
        spec = jnp.concatenate(spec, axis=0).astype(BF)
        spec_ref[m] = spec
        mixed = mm(spec, mixer_ref[m])
        for k in range(nb):
            out_ref[pl.ds(k * modes + m, n_all, stride=nbm), :] = mixed[
                k * n_all : (k + 1) * n_all
            ]
    for d in range(n_all):
        send_ref[d, :nbm, :] = out_ref[d * nbm : (d + 1) * nbm, :].astype(BF)
        send_ref[d, nbm:, :] = down


def mix_back_kernel(
    sizes, got_ref, mixer_ref, first_ref, stat_ref, send_ref, grad_ref, thin_ref, in_ref, wide_ref
):
    n_data, n_mode, nb, _ = sizes
    n_all = n_data * n_mode
    modes = M // n_mode
    nbm = nb * modes
    wide = D // n_data
    share = FF // n_all
    thin = jnp.zeros((16, LANES), F32)
    for d in range(n_all):
        in_ref[d * nbm : (d + 1) * nbm, :] = got_ref[d, :nbm, :].astype(F32)
        thin += got_ref[d, nbm:, :].astype(F32)
    thin = thin[:LEAD] + thin[LEAD:]
    thin_ref[...] = thin
    if modes < 16:
        wide_ref[...] = jnp.zeros_like(wide_ref)
    for m in range(modes):
        grad = [in_ref[pl.ds(k * modes + m, n_all, stride=nbm), :] for k in range(nb)]
        grad = jnp.concatenate(grad, axis=0).astype(BF)
        grad_ref[m] = grad
        back = mm(grad, mixer_ref[m], NT).astype(BF).astype(F32)
        if 2 * wide < LANES:
            back = jnp.concatenate(
                [back, jnp.zeros((back.shape[0], LANES - 2 * wide), F32)], axis=1
            )
        for k in range(nb):
            wide_ref[k, pl.ds(m, n_all, stride=16), :] = back[k * n_all : (k + 1) * n_all]
    inner = first_ref[...].reshape(n_all * 16, LANES)
    inner = jnp.where(iota(inner.shape, 1) < HALF, inner, 0.0)
    inner = by_halves(fold(inner))
    total = jnp.zeros((LEAD, LANES), F32)
    for k in range(nb):
        query = mm(inner, wide_ref[k].astype(BF), TN)
        query = query[:HALF] + query[HALF:]
        for part in range(2):
            at = (part * nb + k) * LEAD
            total += from_lane(query[at : at + LEAD], part * wide, wide)
    block = total + at_lane(from_lane(thin, 0, share), HALF, share)
    row, lane = iota(block.shape, 0), iota(block.shape, 1)
    stats = jnp.where(lane < HALF, stat_ref[:1, :], stat_ref[1:2, :])
    block = jnp.where(row == C, stats, block)
    for d in range(n_all):
        send_ref[d] = block


def spectral_kernel(
    modes,
    wide,
    ready,
    spec_ref,
    grad_ref,
    w_ref,
    m_ref,
    v_ref,
    ema_ref,
    w_out,
    m_out,
    v_out,
    ema_out,
    low_out,
    pair_ref,
    turn_ref,
):
    ready()
    lower = iota((wide, LANES), 1) < HALF
    half_lower = iota((wide // 2, LANES), 1) < HALF
    for m in range(modes):
        slopes = mm(spec_ref[m], grad_ref[m], TN)
        other = pltpu.roll(slopes[wide:], HALF, 1)
        pair_ref[m] = jnp.where(lower, slopes[:wide] + other, slopes[:wide] - other)
        even = pair_ref[m, pl.ds(0, wide // 2, stride=2), :]
        odd = pair_ref[m, pl.ds(1, wide // 2, stride=2), :]
        real = jnp.where(half_lower, even, pltpu.roll(odd, HALF, 1))
        imag = jnp.where(half_lower, pltpu.roll(even, HALF, 1), odd)
        turn_ref[0, pl.ds(m, wide // 2, stride=modes), :] = real
        turn_ref[1, pl.ds(m, wide // 2, stride=modes), :] = imag
    for part in range(2):
        for at in range(wide // 2):
            cols = slice(at * LANES, (at + 1) * LANES)
            grad = turn_ref[part, at * modes : (at + 1) * modes, :]
            new = adamw(
                w_ref[part, :, cols],
                grad,
                m_ref[part, :, cols],
                v_ref[part, :, cols],
                ema_ref[part, :, cols],
                RATE_SPEC,
            )
            for ref, value in zip((w_out, m_out, v_out, ema_out, low_out), new, strict=True):
                ref[part, :, cols] = value


def rows_kernel(
    sizes,
    n_big,
    got_ref,
    thin_ref,
    steps_ref,
    w_ref,
    m_ref,
    v_ref,
    ema_ref,
    *refs,
):
    big_refs, (loss_ref, w_out, m_out, v_out, ema_out, low_out) = refs[:n_big], refs[n_big:]
    n_data, n_mode, _, total = sizes
    n_all = n_data * n_mode
    wide = D // n_data
    share = FF // n_all
    rows = w_ref.shape[0]
    query = []
    for at in range(D // LANES):
        block = jnp.zeros((LEAD, LANES), F32)
        for i in range(at * LANES // wide, (at + 1) * LANES // wide):
            part = sum(got_ref[i * n_mode + j, :LEAD, :] for j in range(n_mode))
            block += at_lane(part, i * wide % LANES, wide)
        query.append(block)
    query = jnp.concatenate(query, axis=1)
    down = []
    for at in range(FF // LANES):
        block = jnp.zeros((LEAD, LANES), F32)
        for d in range(at * LANES // share, (at + 1) * LANES // share):
            block += at_lane(from_lane(got_ref[d, :LEAD, :], HALF, share), d * share % LANES, share)
        down.append(block)
    down = jnp.where(iota((LEAD, FF), 0) < C, jnp.concatenate(down, axis=1), 0.0)
    norm = SPECTRAL_WEIGHT / (total * M * S)
    stats = sum(got_ref[d, C : C + 1, :] for d in range(n_all))
    steps = steps_ref[C : C + 1, HALF : HALF + 1]
    loss_ref[...] = stats[:, :1] / steps + norm * stats[:, HALF : HALF + 1]

    keep = iota((LEAD, D), 0) < C
    query = jnp.where(keep, query, 0.0)
    query = jnp.concatenate(split(query), axis=0).astype(BF)
    down = jnp.concatenate(split(down), axis=0).astype(BF)
    thin = thin_rows(w_ref)
    embed = at_lane(thin, 0, C) + at_lane(from_lane(thin, 0, C), LEAD, C)
    head = from_lane(thin, LEAD, C)
    head = at_lane(head, 0, C) + at_lane(head, LEAD, C)

    def back(weights, sums):
        sums = jnp.concatenate([sums, jnp.zeros((LANES - 16, sums.shape[1]), BF)], axis=0)
        out = mm(weights.astype(BF), sums, NT)
        return from_lane(out, 0, LEAD) + from_lane(out, LEAD, LEAD)

    own = jnp.concatenate([thin_ref[...], jnp.zeros((LANES - LEAD, LANES), F32)], axis=0).T
    embed_grad = own[HALF : HALF + rows] + back(w_ref[:, :D], query)
    head_grad = own[HALF + rows : HALF + 2 * rows] + back(
        w_ref[:, 2 * D + FF : 2 * D + 2 * FF], down
    )
    last = at_lane(embed_grad, 0, C) + at_lane(head_grad, C, C)

    def update(grad, cols):
        new = adamw(w_ref[:, cols], grad, m_ref[:, cols], v_ref[:, cols], ema_ref[:, cols], RATE_DENSE)
        for ref, value in zip((w_out, m_out, v_out, ema_out, low_out), new, strict=True):
            ref[:, cols] = value

    update(mm(embed[:, :16].astype(BF), query), slice(0, D))
    update(sum(ref[...].astype(F32) for ref in big_refs), slice(D, 2 * D + FF))
    update(mm(head[:, :16].astype(BF), down), slice(2 * D + FF, 2 * D + 2 * FF))
    update(last[:, : 2 * C], slice(2 * D + 2 * FF, 2 * D + 2 * FF + 2 * C))


def per_device(
    series,
    future_values,
    step_mask,
    mode_index,
    dense,
    dense_m,
    dense_v,
    dense_ema,
    spectral,
    spec_m,
    fourier_variance_moment,
    spec_ema,
):
    n_mode = lax.axis_size("mode")
    n_data = lax.axis_size("dp")
    n_all = n_mode * n_data
    time_rows, batch, chans = series.shape
    nb = batch // n_mode
    total = batch * n_data
    modes = M // n_mode
    wide = D // n_data
    rows = dense.shape[0]
    shape = jax.ShapeDtypeStruct
    sizes = (n_data, n_mode, nb, total)
    tiled = rows % 16 == 0 and n_mode == 4 and n_data >= 4

    send, weights = call(
        partial(pack_kernel, sizes),
        (shape((n_mode, 2 * nb * LEAD, time_rows), F32), shape((rows, D + FF + LANES), BF)),
        (series.transpose(2, 1, 0), future_values.transpose(2, 1, 0), step_mask.T, dense),
        [pltpu.VMEM((chans, batch, time_rows), F32), pltpu.VMEM((batch, time_rows), F32)],
        name="pack",
        ahead=(0, 1, 2, 3),
    )
    me = jnp.stack([lax.axis_index("dp"), lax.axis_index("mode")]).astype(jnp.int32)
    own = exchange(send, "mode")
    cosv, sinv = tables(mode_index)
    weights = [gather_rows(weights)] if not tiled else gather_tiles_first(weights)
    if tiled:
        weights = gather_tiles_second(*weights)

    whole_rows = [pltpu.VMEM((2 * nb * LEAD, S), F32)]
    send = call(
        partial(spectra_kernel, sizes),
        shape((n_all, 16, LANES), F32),
        (own, cosv, sinv, dense),
        whole_rows,
        name="spectra",
    )
    first = exchange(send, AXES)
    ins = call(
        tables_kernel,
        (
            shape((S, 4 * M), BF),
            shape((3 * M, S), BF),
            shape((2 * M, S), BF),
            shape((S, 2 * M), BF),
            shape((S, LANES), F32),
            shape((S, LANES), F32),
        ),
        (own, cosv, sinv),
        whole_rows,
        name="tables",
        cost=10**10,
    )
    first, *ins = together(first, *ins)
    if tiled:
        weights = gather_tiles_third(*weights)

    w_low = spectral.astype(BF).reshape(2, modes, wide, E)
    mixer = jnp.concatenate(
        [
            jnp.concatenate([w_low[0], w_low[1]], axis=2),
            jnp.concatenate([-w_low[1], w_low[0]], axis=2),
        ],
        axis=1,
    )
    scratch = [
        pltpu.VMEM((nb, n_all * 16, LANES), F32),
        pltpu.VMEM((n_all * nb * modes, LANES), F32),
    ]
    send, spec, thin = call(
        partial(mix_kernel, sizes),
        (
            shape((n_all, nb * modes + 16, LANES), BF),
            shape((modes, total, 2 * wide), BF),
            shape((16, LANES), F32),
        ),
        (first, mixer),
        scratch,
        name="mix",
    )
    if tiled:
        send, *weights = together(send, *weights)
        weights = gather_tiles_last(weights)
    got = exchange(send, AXES)
    steps = thin

    send, stats, *big = block(
        steps[C, HALF].reshape(1),
        me,
        weights,
        (got, *ins),
        sizes + (True,) if tiled else sizes,
    )
    got = exchange(send, AXES)
    if tiled:
        big = scatter_tiles_first(*big)
        got, *big = together(got, *big)
        big = scatter_tiles_second(*big)
    send, grad_mixed, thin = call(
        partial(mix_back_kernel, sizes),
        (
            shape((n_all, LEAD, LANES), F32),
            shape((modes, total, LANES), BF),
            shape((LEAD, LANES), F32),
        ),
        (got, mixer, first, stats),
        scratch[::-1],
        name="mix_back",
        cost=10**10,
    )
    if tiled:
        grad_mixed, big = together(grad_mixed, big)
    spec_out = call(
        partial(spectral_kernel, modes, wide),
        (shape(spectral.shape, F32),) * 4 + (shape(spectral.shape, BF),),
        (spec, grad_mixed, spectral, spec_m, fourier_variance_moment, spec_ema),
        [
            pltpu.VMEM((modes, wide, LANES), F32),
            pltpu.VMEM((2, modes * wide // 2, LANES), F32),
        ],
        name="spectral",
        ahead=(0, 1, 2, 3, 4, 5),
        cost=10**10,
    )
    got = exchange(send, AXES)
    big = scatter_tiles_third(*big) if tiled else [scatter_rows(big[0], rows)]
    loss, *dense_out = call(
        partial(rows_kernel, sizes, len(big)),
        (shape((1, 1), F32),) + (shape(dense.shape, F32),) * 4 + (shape(dense.shape, BF),),
        (got, thin, steps, dense, dense_m, dense_v, dense_ema, *big),
        name="rows",
    )
    return (loss.reshape(()),) + tuple(dense_out) + tuple(spec_out)


def solution(mesh):
    rows = P(("dp", "mode"), None)
    mixing = P(None, "mode", "dp")
    return jax.shard_map(
        per_device,
        mesh=mesh,
        in_specs=(P("mode", "dp", None), P("mode", "dp", None), P("mode", "dp"), P())
        + (rows,) * 4
        + (mixing,) * 4,
        out_specs=(P(),) + (rows,) * 5 + (mixing,) * 5,
        check_vma=False,
    )
```

```python
import math
from functools import partial

import jax
import jax.numpy as jnp
from jax import lax
from jax.experimental import pallas as pl
from jax.experimental.pallas import tpu as pltpu
from jax.sharding import PartitionSpec as P

D = 512
H = 8
E = 64
FF = 2048
M = 64
C = 7
S = 768
LANES = 128

SPECTRAL_WEIGHT = 0.5
RATE_DENSE = 0.02
RATE_SPEC = 0.1
BF = jnp.bfloat16
F32 = jnp.float32
AXES = ("dp", "mode")
SLOPE = jnp.bfloat16
VMEM_BYTES = 60 * 1024 * 1024
FULL_BYTES = 60 * 1024 * 1024
SMALL_BYTES = 16 * 1024 * 1024


def plain(spec, left, right):
    return jnp.einsum(spec, left, right, preferred_element_type=F32)


def exact(spec, left, right):
    return jnp.einsum(
        spec, left, right, precision=lax.Precision.HIGHEST, preferred_element_type=F32
    )


def tables(mode_index):
    steps = jnp.arange(S, dtype=jnp.int32)
    phase = mode_index[:, None] * steps[None, :] % S
    angle = phase.astype(F32) * (2.0 * math.pi / S)
    return (jnp.cos(angle), jnp.sin(angle))


def unpack(whole):
    return (
        whole[:, :D],
        whole[:, D : 2 * D],
        whole[:, 2 * D : 2 * D + FF],
        whole[:, 2 * D + FF : 2 * D + 2 * FF],
        whole[:, 2 * D + 2 * FF : 2 * D + 2 * FF + C],
        whole[:, 2 * D + 2 * FF + C :],
    )


def adamw(weight, grad, first, second, average, rate):
    first_new = 0.5 * first + 0.5 * grad
    second_new = 0.5 * second + 0.5 * grad * grad
    weight_new = weight - rate * (first_new / (jnp.sqrt(second_new) + 1e-08) + 0.01 * weight)
    average_new = 0.9 * average + 0.1 * weight_new
    return (weight_new, first_new, second_new, average_new, weight_new.astype(BF))


def halves(x):
    high = x.astype(BF)
    return high, (x - high.astype(F32)).astype(BF)


def fill(x, size, axis):
    wanted = list(x.shape)
    wanted[axis] = size - x.shape[axis]
    return jnp.concatenate([x, jnp.zeros(wanted, x.dtype)], axis=axis) if wanted[axis] else x


def exchange(x, axes):
    return lax.all_to_all(x, axes, 0, 0, tiled=True)


def partners(step):
    count = lax.axis_size("mode")
    return [(index, index ^ step) for index in range(count)]


def bit_of(step):
    return lax.div(lax.axis_index("mode"), step) % 2


def steps_of_mode():
    return [1 << bit for bit in range(lax.axis_size("mode").bit_length() - 1)]


def by_xor(x, axis, step):
    count = lax.axis_size(axis)
    return lax.ppermute(x, axis, [(index, index ^ step) for index in range(count)])


def tile_offsets(n_data):
    cut = n_data // 4
    low = [2 * step for step in range(cut)]
    high = [2 * step for step in range(cut, 2 * cut)]
    ones = lambda data: [index + 1 for index in data]
    offsets = [
        (low + ones(low), [0] * 2 * cut),
        (low + ones(low), [2] * 2 * cut),
        (high + high, [0] * cut + [2] * cut),
        (ones(high) + ones(high), [0] * cut + [2] * cut),
    ]
    return offsets + [(data, [index + 1 for index in mode]) for data, mode in offsets]


def gather_tiles_first(x):
    n_data = lax.axis_size("dp")
    deep = [x] + [by_xor(x, "dp", 2 * step) for step in range(1, n_data // 2)]
    cut = len(deep) // 2
    return jnp.stack(deep[:cut]), jnp.stack(deep[cut:])


def gather_tiles_second(first, second):
    first = jnp.concatenate([first, by_xor(first, "dp", 1)])
    return first, jnp.concatenate([second, by_xor(second, "mode", 2)])


def gather_tiles_third(first, second):
    return [first, by_xor(first, "mode", 2), second, by_xor(second, "dp", 1)]


def gather_tiles_last(pieces):
    return pieces + [by_xor(piece, "mode", 1) for piece in pieces]


def tile_order(n_data):
    cut = n_data // 4
    low = [2 * step for step in range(cut)]
    high = [2 * step for step in range(cut, 2 * cut)]
    groups = [
        [(data + x, 2) for data in low for x in (0, 1)],
        [(data + x, 0) for data in low for x in (0, 1)],
        [(data + 1, 2 * y) for data in high for y in (0, 1)],
        [(data, 2 * y) for data in high for y in (0, 1)],
    ]
    return [[(data, mode + core) for data, mode in group] for core in (1, 0) for group in groups]


def together(*values):
    return lax.optimization_barrier(values)


def total_of(terms, pick):
    return sum(term[pick].astype(F32) for term in terms)


def scatter_tiles_first(away, stay):
    pairs = lambda terms: [x.reshape((x.shape[0] // 2, 2) + x.shape[1:]) for x in terms]
    come = by_xor(away, "mode", 1)
    first = by_xor(total_of([stay, come], 0).astype(BF), "mode", 2)
    second = by_xor(total_of([stay, come], 2).astype(BF), "dp", 1)
    first = pairs([stay[1], come[1], first])
    second = pairs([stay[3], come[3], second])
    away = [total_of(terms, (slice(None), 1)).astype(BF) for terms in (first, second)]
    return away + [[x[:, 0] for x in terms] for terms in (first, second)]


def scatter_tiles_second(first_away, second_away, first, second):
    return [first + [by_xor(first_away, "dp", 1)], second + [by_xor(second_away, "mode", 2)]]


def scatter_tiles_third(first, second):
    cut = first[0].shape[0]
    come = []
    for step in range(1, 2 * cut):
        terms, at = (first, step) if step < cut else (second, step - cut)
        come.append(by_xor(total_of(terms, at).astype(BF), "dp", 2 * step))
    return [total_of(first, 0)] + come


def gather_rows(x):
    n_data = lax.axis_size("dp")
    held = exchange(jnp.broadcast_to(x[None], (n_data,) + x.shape), "dp")[:, None]
    for step in reversed(steps_of_mode()):
        other = lax.ppermute(held, "mode", partners(step))
        first = bit_of(step) == 0
        pair = [jnp.where(first, held, other), jnp.where(first, other, held)]
        held = jnp.stack(pair, axis=2).reshape(n_data, -1, *x.shape)
    return held.reshape(-1, x.shape[1])


def scatter_rows(x, rows):
    n_data, n_mode = lax.axis_size("dp"), lax.axis_size("mode")
    held = x.reshape(n_data, n_mode, rows, x.shape[1])
    for step in steps_of_mode():
        held = held.reshape(n_data, held.shape[1] // 2, 2, rows, x.shape[1])
        bit = bit_of(step)
        away = lax.dynamic_index_in_dim(held, 1 - bit, 2, keepdims=False)
        stay = lax.dynamic_index_in_dim(held, bit, 2, keepdims=False)
        other = lax.ppermute(away, "mode", partners(step))
        held = (stay.astype(F32) + other.astype(F32)).astype(BF)
    held = exchange(held.reshape(n_data, rows, x.shape[1]), "dp")
    return jnp.sum(held.astype(F32), axis=0)


NN = (((1,), (0,)), ((), ()))
NT = (((1,), (1,)), ((), ()))
TN = (((0,), (0,)), ((), ()))
FIRST = 2.0 * math.sqrt(2.0 / math.pi)
THIRD = FIRST * 0.044715
GATES = 1024
UNROLL = 4
LEAD = 8
HALF = 64


def mm(left, right, dims=NN):
    return lax.dot_general(left, right, dims, preferred_element_type=F32)


def iota(shape, axis):
    return lax.broadcasted_iota(jnp.int32, shape, axis)


def split(x):
    high = x.astype(BF).astype(F32)
    return high, x - high


def by_halves(x):
    high, low = split(x)
    return jnp.where(iota(x.shape, 1) < HALF, high, low).astype(BF)


def fold(x):
    return x + pltpu.roll(x, HALF, 1)


def rows_at(x, first, count):
    parts = []
    if first:
        parts.append(jnp.zeros((first, x.shape[1]), F32))
    parts.append(x)
    if count - first - x.shape[0]:
        parts.append(jnp.zeros((count - first - x.shape[0], x.shape[1]), F32))
    return jnp.concatenate(parts, axis=0)


def row_groups(x):
    return sum(x[at : at + LEAD] for at in range(0, x.shape[0], LEAD))


def block_kernel(sizes, count_ref, me_ref, *refs):
    if len(sizes) == 4:
        block_steps(sizes, lambda what: None, count_ref, *refs)
        return
    n_data, n_mode = sizes[:2]
    rows = D // n_data // n_mode
    offsets = tile_offsets(n_data)
    n_pieces = len(offsets)
    pieces, got_ref, sources, refs = refs[:n_pieces], refs[n_pieces], refs[n_pieces + 1 : n_pieces + 7], refs[n_pieces + 7 :]
    send_ref, stat_ref, away_ref, stay_ref, row_sems, sems, w_ref = refs[:7]
    places, scratch = refs[7:13], refs[13:]
    act_ref = scratch[5]

    def rows_of(data, mode):
        owner = (me_ref[0] ^ data) * n_mode + (me_ref[1] ^ mode)
        return pl.ds(pl.multiple_of(owner * rows, rows), rows)

    row_copies = []
    for ref, (data, mode) in zip(pieces, offsets, strict=True):
        for at, (one, two) in enumerate(zip(data, mode, strict=True)):
            place = w_ref.at[rows_of(one, two), :]
            row_copies.append(
                pltpu.make_async_copy(ref.at[at], place, row_sems.at[len(row_copies)])
            )
            row_copies[-1].start()
    copies = [
        pltpu.make_async_copy(source, place, sems.at[at])
        for at, (source, place) in enumerate(zip(sources, places, strict=True))
    ]
    for copy in copies:
        copy.start()
    waits = {"rows": row_copies, "a": copies[:1], "rest": copies[1:]}

    def ready(what):
        for copy in waits[what]:
            copy.wait()

    block_steps(sizes, ready, count_ref, w_ref, got_ref, *places, send_ref, stat_ref, None, *scratch)
    for at, group in enumerate(tile_order(n_data)):
        ref = away_ref if at < 4 else stay_ref
        for index, (data, mode) in enumerate(group):
            ref[at % 4, index, :, :D] = act_ref[1, rows_of(data, mode), :D]
            ref[at % 4, index, :, D:] = act_ref[0, rows_of(data, mode), :]


def block_steps(
    sizes,
    ready,
    count_ref,
    w_ref,
    got_ref,
    a_ref,
    at_ref,
    rest_ref,
    rest_t_ref,
    target_ref,
    keep_ref,
    send_ref,
    stat_ref,
    big_ref,
    wdup_ref,
    x_ref,
    v_ref,
    r_ref,
    wd_ref,
    act_ref,
    slope_ref,
    fc_ref,
    zx_ref,
    j_ref,
):
    n_data, n_mode, nb, total = sizes[:4]
    n_all = n_data * n_mode
    modes = M // n_mode
    nbm = nb * modes
    share = FF // n_all
    rows = D // n_all
    scale = 2.0 / S
    norm = SPECTRAL_WEIGHT / (total * M * S)
    chunks = FF // GATES

    for i in range(n_data):
        blocks = [got_ref[i * n_mode + j, :nbm, :].astype(F32) for j in range(n_mode)]
        for k in range(nb):
            column = [block[k * modes : (k + 1) * modes] for block in blocks]
            x_ref[k * M : (k + 1) * M, i * LANES : (i + 1) * LANES] = jnp.concatenate(
                column, axis=0
            ).astype(BF)

    per = LANES // share
    for at in range(FF // LANES):
        block = jnp.zeros((16, LANES), F32)
        for q in range(per):
            piece = got_ref[at * per + q, nbm : nbm + 16, :].astype(F32)
            piece = pltpu.roll(piece, q * share, 1) if q else piece
            block = jnp.where(iota(block.shape, 1) // share == q, piece, block)
        spread = [
            rows_at(jnp.concatenate([half] * nb, axis=0), 0, HALF)
            for half in (block[:LEAD], block[LEAD:])
        ]
        wd_ref[:, at * LANES : (at + 1) * LANES] = jnp.concatenate(spread, axis=0).astype(BF)
    ready("rows")
    for i in range(n_data):
        head = i * H // n_data
        block = w_ref[head * E : (head + 1) * E, :D]
        wdup_ref[2 * i * E : (2 * i + 1) * E, :] = block
        wdup_ref[(2 * i + 1) * E : (2 * i + 2) * E, :] = block
    x_all = x_ref[...]
    real_lane = iota(x_all.shape, 1) % LANES < HALF
    zero = jnp.zeros_like(x_all)
    x_real = jnp.where(real_lane, x_all, zero)
    x_imag = jnp.where(real_lane, zero, x_all)
    line_real = scale * mm(x_real, wdup_ref[...])
    line_imag = scale * mm(x_imag, wdup_ref[...])
    for k in range(nb):
        v_ref[2 * k * M : (2 * k + 1) * M, :] = line_real[k * M : (k + 1) * M].astype(BF)
        v_ref[(2 * k + 1) * M : (2 * k + 2) * M, :] = line_imag[k * M : (k + 1) * M].astype(BF)

    thin_t = w_ref[:, D + FF :].astype(F32).T
    embed_t = thin_t[:LEAD]
    head_t = thin_t[LEAD : 2 * LEAD]
    pad = [jnp.zeros((HALF - nb * LEAD, D), F32)] if nb * LEAD < HALF else []
    embed_all = jnp.concatenate([embed_t] * nb + pad, axis=0).astype(BF)
    head_all = jnp.concatenate([head_t] * nb + pad, axis=0).astype(BF)
    head_twice = jnp.concatenate([head_all, head_all], axis=0)
    embed_twice = jnp.concatenate([embed_t, embed_t], axis=0).astype(BF)

    for c in range(FF // 512):
        cols = slice(c * 512, (c + 1) * 512)
        w_up = w_ref[:, D + c * 512 : D + (c + 1) * 512]
        lifted = mm(v_ref[...], w_up)
        thin = mm(embed_twice, w_up)[:LEAD]
        high, low = split(thin)
        for k in range(nb):
            r_ref[k, : 2 * M, cols] = lifted[2 * k * M : 2 * (k + 1) * M].astype(BF)
            r_ref[k, 2 * M :, cols] = jnp.concatenate(
                [rows_at(high, k * LEAD, HALF), rows_at(low, k * LEAD, HALF)], axis=0
            ).astype(BF)

    parts = [mm(head_all[:16], v_ref[2 * k * M : 2 * (k + 1) * M, :], NT)[:LEAD] for k in range(nb)]
    by_head = rows_at(jnp.concatenate(parts, axis=0), 0, HALF)
    cross = mm(head_all, jnp.concatenate([embed_all, jnp.zeros_like(embed_all)], axis=0), NT)
    cross = jnp.where(iota(cross.shape, 0) // LEAD == iota(cross.shape, 1) // LEAD, cross, 0.0)
    high, low = split(jnp.concatenate([by_head, cross], axis=1))
    by_head = jnp.concatenate([high, low], axis=0).astype(BF)
    ready("a")
    fc_ref[...] = mm(a_ref[...], by_head, NT)

    own_lane = iota((S, LANES), 1) % HALF // LEAD

    def forward(step, carry):
        k = step // chunks
        cols = pl.ds(pl.multiple_of(step % chunks * GATES, GATES), GATES)
        gate = mm(a_ref[...], r_ref[k, :, cols])
        square = gate * gate
        sig = 0.5 * jnp.tanh(gate * (square * (0.5 * THIRD) + 0.5 * FIRST)) + 0.5
        act = gate * sig
        low = act.astype(BF)
        act_ref[k, :, cols] = low
        slope = sig + act * (1.0 - sig) * (square * (3.0 * THIRD) + FIRST)
        slope_ref[k, :, cols] = slope.astype(slope_ref.dtype)
        fc_ref[...] += jnp.where(own_lane == k, mm(low, wd_ref[:, cols], NT), 0.0)
        return carry

    lax.fori_loop(0, nb * chunks, forward, 0, unroll=UNROLL)

    ready("rest")
    keep = keep_ref[...]
    masked = keep * (fold(fc_ref[...]) - target_ref[...])
    two = by_halves(masked)
    err = fold(mm(at_ref[: 2 * M, :], two) + mm(rest_ref[...], two))
    stat_ref[...] = jnp.concatenate(
        [
            jnp.full((1, LANES), 0.5 * jnp.sum(masked * masked)),
            jnp.full((1, LANES), 0.5 * jnp.sum(err * err)),
            jnp.zeros((6, LANES), F32),
        ],
        axis=0,
    )
    two = by_halves(err)
    back = fold(mm(a_ref[:, : 2 * M], two) + mm(rest_t_ref[...], two))
    g_fc = keep * ((2.0 / count_ref[0]) * masked + (2.0 * norm) * back)
    g_low = g_fc.astype(BF)
    g_turn = g_fc.T[:HALF].astype(BF)
    zx_ref[...] = jnp.zeros_like(zx_ref)
    j_ref[...] = jnp.zeros_like(j_ref)

    def backward(step, carry):
        k = step // chunks
        cols = pl.ds(pl.multiple_of(step % chunks * GATES, GATES), GATES)
        fed = mm(jnp.where(own_lane == k, g_fc, 0.0).astype(BF), wd_ref[:, cols])
        g_gate = (fed * slope_ref[k, :, cols].astype(F32)).astype(BF)
        turned = mm(at_ref[...], g_gate)
        r_ref[k, : 2 * M, cols] = turned[: 2 * M].astype(BF)
        own = iota((HALF, GATES), 0) // LEAD == k
        zx_ref[:, cols] += jnp.where(own, turned[2 * M :], 0.0)
        j_ref[:, cols] += jnp.where(own, mm(g_turn, act_ref[k, :, cols]), 0.0)
        return carry

    lax.fori_loop(0, nb * chunks, backward, 0, unroll=UNROLL)

    back_fc = by_halves(mm(at_ref[...], g_low))
    lane_of = iota((2 * M, LANES), 1) % HALF // LEAD
    nothing = jnp.zeros((2 * M, LANES), F32)
    back_rows = jnp.concatenate(
        [jnp.where(lane_of == k, back_fc[: 2 * M].astype(F32), nothing) for k in range(nb)], axis=0
    ).astype(BF)
    cross = jnp.where(
        iota((HALF, LANES), 0) // LEAD == iota((HALF, LANES), 1) % HALF // LEAD,
        back_fc[2 * M :].astype(F32),
        0.0,
    ).astype(BF)
    v_all = v_ref[...]
    z_all = r_ref[:, : 2 * M, :].reshape(nb * 2 * M, FF)
    high, low = split(row_groups(zx_ref[...]))
    zx = jnp.concatenate([high, low], axis=0).astype(BF)
    w_up = w_ref[:, D : D + FF]
    back_block = mm(z_all, w_up, NT) + mm(back_rows, head_twice)
    turned = (scale * back_block).astype(BF)
    embed_grad = row_groups(mm(zx, w_up, NT)) + row_groups(mm(cross, head_twice))
    head_grad = row_groups(mm(back_rows, v_all, TN)) + row_groups(mm(cross, embed_all, TN))
    down_grad = row_groups(j_ref[...])

    turned_real = jnp.concatenate(
        [turned[2 * k * M : (2 * k + 1) * M] for k in range(nb)], axis=0
    )
    turned_imag = jnp.concatenate(
        [turned[(2 * k + 1) * M : (2 * k + 2) * M] for k in range(nb)], axis=0
    )
    p_real = mm(turned_real, wdup_ref[...], NT)
    p_imag = mm(turned_imag, wdup_ref[...], NT)
    real_lane = iota((modes, LANES), 1) < HALF
    lane = iota((LEAD, LANES), 1)
    for i in range(n_data):
        cols = slice(i * LANES, (i + 1) * LANES)
        for j in range(n_mode):
            d = i * n_mode + j
            pieces = []
            for k in range(nb):
                at = slice(k * M + j * modes, k * M + (j + 1) * modes)
                pieces.append(jnp.where(real_lane, p_real[at, cols], p_imag[at, cols]))
            send_ref[d, :nbm, :] = jnp.concatenate(pieces, axis=0).astype(BF)
            out = jnp.zeros((LEAD, LANES), F32)
            for source, width, place in (
                (down_grad, share, 0),
                (embed_grad, rows, HALF),
                (head_grad, rows, HALF + rows),
            ):
                first = d * width // LANES * LANES
                piece = source[:, first : first + LANES]
                shift = (place - (d * width - first)) % LANES
                piece = pltpu.roll(piece, shift, 1) if shift else piece
                out = jnp.where((lane >= place) & (lane < place + width), piece, out)
            high, low = split(out)
            send_ref[d, nbm:, :] = jnp.concatenate([high, low], axis=0).astype(BF)

    x_all = x_ref[...]
    real_lane = iota(x_all.shape, 1) % LANES < HALF
    x_real = jnp.where(real_lane, x_all, zero)
    x_imag = jnp.where(real_lane, zero, x_all)
    out_grad = mm(x_real, turned_real, TN) + mm(x_imag, turned_imag, TN)
    each = n_data // H
    for head in range(H):
        block = 0.0
        for i in range(head * each, (head + 1) * each):
            block += out_grad[2 * i * E : (2 * i + 1) * E] + out_grad[(2 * i + 1) * E : (2 * i + 2) * E]
        out = act_ref.at[1] if big_ref is None else big_ref
        out[head * E : (head + 1) * E, :D] = block.astype(BF)
    for c in range(FF // 512):
        cols = slice(c * 512, (c + 1) * 512)
        up_grad = mm(v_all, z_all[:, cols], TN) + mm(embed_twice, zx[:, cols], TN)
        if big_ref is None:
            act_ref[0, :D, cols] = up_grad.astype(BF)
        else:
            big_ref[:, D + c * 512 : D + (c + 1) * 512] = up_grad.astype(BF)


def block(count, me, weights, ins, sizes):
    n_data, n_mode, nb = sizes[:3]
    tiled = len(sizes) > 4
    whole = pl.BlockSpec(memory_space=pltpu.VMEM)
    far = pl.BlockSpec(memory_space=pl.ANY if tiled else pltpu.VMEM)
    big = [jax.ShapeDtypeStruct((D, D + FF), BF)]
    scratch = []
    if tiled:
        half = (4, n_data * n_mode // 8, D // n_data // n_mode, D + FF)
        big = [jax.ShapeDtypeStruct(half, BF)] * 2
        scratch = [
            pltpu.SemaphoreType.DMA((n_data * n_mode,)),
            pltpu.SemaphoreType.DMA((6,)),
            pltpu.VMEM((D, D + FF + LANES), BF),
        ]
        scratch += [pltpu.VMEM(x.shape, x.dtype) for x in ins[1:]]
    return pl.pallas_call(
        partial(block_kernel, sizes),
        out_shape=(
            jax.ShapeDtypeStruct(ins[0].shape, BF),
            jax.ShapeDtypeStruct((8, LANES), F32),
            *big,
        ),
        in_specs=[pl.BlockSpec(memory_space=pltpu.SMEM)] * 2
        + [far] * len(weights)
        + [whole]
        + [far] * (len(ins) - 1),
        out_specs=(whole,) * (2 + len(big)),
        scratch_shapes=scratch
        + [
            pltpu.VMEM((2 * n_data * E, D), BF),
            pltpu.VMEM((nb * M, n_data * LANES), BF),
            pltpu.VMEM((nb * 2 * M, D), BF),
            pltpu.VMEM((nb, 4 * M, FF), BF),
            pltpu.VMEM((LANES, FF), BF),
            pltpu.VMEM((nb, S, FF), BF),
            pltpu.VMEM((nb, S, FF), SLOPE),
            pltpu.VMEM((S, LANES), F32),
            pltpu.VMEM((HALF, FF), F32),
            pltpu.VMEM((HALF, FF), F32),
        ],
        compiler_params=pltpu.CompilerParams(vmem_limit_bytes=VMEM_BYTES),
        name="block",
    )(count, me, *weights, *ins)


def at_lane(x, first, width):
    x = pltpu.roll(x, first, 1) if first else x
    lane = iota(x.shape, 1)
    return jnp.where((lane >= first) & (lane < first + width), x, 0.0)


def from_lane(x, first, width):
    base = first // LANES * LANES
    x = x[:, base : base + LANES]
    shift = (LANES - (first - base)) % LANES
    x = pltpu.roll(x, shift, 1) if shift else x
    return jnp.where(iota(x.shape, 1) < width, x, 0.0)


def staged(kernel, ahead, *refs):
    sems = refs[-1]
    n_held = len(refs) - 1 - len(ahead)
    held = list(refs[:n_held])
    copies = []
    for at, (index, place) in enumerate(zip(ahead, refs[n_held:-1], strict=True)):
        copies.append(pltpu.make_async_copy(refs[index], place, sems.at[at]))
        copies[-1].start()
        held[index] = place

    def ready():
        for copy in copies:
            copy.wait()

    kernel(ready, *held)


def call(kernel, outs, ins, scratch=(), name=None, cost=0, ahead=()):
    whole = pl.BlockSpec(memory_space=pltpu.VMEM)
    in_specs = [whole] * len(ins)
    scratch = list(scratch)
    if ahead:
        kernel = partial(staged, kernel, ahead)
        for index in ahead:
            in_specs[index] = pl.BlockSpec(memory_space=pl.ANY)
            scratch.append(pltpu.VMEM(ins[index].shape, ins[index].dtype))
        scratch.append(pltpu.SemaphoreType.DMA((len(ahead),)))
    return pl.pallas_call(
        kernel,
        out_shape=outs,
        in_specs=in_specs,
        out_specs=jax.tree.map(lambda _: whole, outs),
        scratch_shapes=scratch,
        compiler_params=pltpu.CompilerParams(vmem_limit_bytes=FULL_BYTES if ahead else SMALL_BYTES),
        name=name,
        cost_estimate=pl.CostEstimate(flops=cost, bytes_accessed=cost // 10, transcendentals=0)
        if cost
        else None,
    )(*ins)


def thin_rows(dense_ref):
    thin = dense_ref[:, 2 * D + 2 * FF :]
    thin = jnp.concatenate([thin, jnp.zeros((thin.shape[0], LANES - 2 * C), F32)], axis=1)
    return at_lane(thin, 0, C) + at_lane(from_lane(thin, C, C), LEAD, C)


def pack_kernel(sizes, ready, series_ref, future_ref, mask_ref, dense_ref, send_ref, rows_ref, one_ref, two_ref):
    n_mode, nb = sizes[1:3]
    ready()
    one_ref[...] = series_ref[...].astype(F32)
    two_ref[...] = mask_ref[...].astype(F32)
    for j in range(n_mode):
        for k in range(nb):
            b = j * nb + k
            for c in range(C):
                send_ref[j, k * LEAD + c, :] = one_ref[c, b, :]
                send_ref[j, (nb + k) * LEAD + c, :] = future_ref[c, b, :]
            send_ref[j, k * LEAD + C, :] = two_ref[b, :]
            send_ref[j, (nb + k) * LEAD + C, :] = jnp.zeros_like(two_ref[b, :])
    rows_ref[:, : D + FF] = dense_ref[:, D : 2 * D + FF].astype(BF)
    rows_ref[:, D + FF :] = thin_rows(dense_ref).astype(BF)


def own_rows(got_ref, all_ref):
    steps = got_ref.shape[2]
    for j in range(got_ref.shape[0]):
        all_ref[:, j * steps : (j + 1) * steps] = got_ref[j]
    half = all_ref.shape[0] // 2
    inputs = all_ref[:half, :]
    mask = inputs
    inputs = jnp.where(iota(inputs.shape, 0) % LEAD == C, 0.0, inputs)
    return inputs, mask, all_ref[half:, :]


def spectra_kernel(sizes, got_ref, cos_ref, sin_ref, dense_ref, send_ref, all_ref):
    n_data, n_mode, nb, _ = sizes
    n_all = n_data * n_mode
    modes = M // n_mode
    wide = D // n_data
    share = FF // n_all
    x, mask, _ = own_rows(got_ref, all_ref)
    count = jnp.sum(jnp.where(iota(mask.shape, 0) % LEAD == C, mask, 0.0))
    low = cos_ref[...].astype(BF)
    inner = mm(low, rows_at(x, 0, LANES).astype(BF), NT)
    low = (-sin_ref[...]).astype(BF)
    inner += mm(low, rows_at(x, nb * LEAD, LANES).astype(BF), NT)
    thin = thin_rows(dense_ref).astype(BF)
    query = mm(thin, dense_ref[:, :D].astype(BF), TN)[:LEAD]
    down = mm(thin, dense_ref[:, 2 * D + FF : 2 * D + 2 * FF].astype(BF), TN)[LEAD : 2 * LEAD]
    row = iota((LEAD, LANES), 0)
    lane = iota((LEAD, LANES), 1)
    for i in range(n_data):
        ours = at_lane(from_lane(query, i * wide, wide), HALF, wide)
        ours = jnp.where((row == C) & (lane == HALF), count, ours)
        for j in range(n_mode):
            d = i * n_mode + j
            block = inner[j * modes : (j + 1) * modes]
            if modes < 16:
                block = jnp.concatenate([block, jnp.zeros((16 - modes, LANES), F32)], axis=0)
            theirs = at_lane(from_lane(down, d * share, share), HALF, share)
            send_ref[d] = block + jnp.concatenate([ours, theirs], axis=0)


def tables_kernel(
    got_ref, cos_ref, sin_ref, a_ref, at_ref, rest_ref, rest_t_ref, target_ref, keep_ref, all_ref
):
    x, mask, target = own_rows(got_ref, all_ref)
    count = x.shape[0]
    keep = [
        jnp.broadcast_to(mask[at + C : at + LEAD], (LEAD, S)) for at in range(0, count, LEAD)
    ]
    keep = jnp.concatenate(keep, axis=0)
    twice = lambda rows: jnp.concatenate([rows_at(rows, 0, HALF)] * 2, axis=0).T
    a_ref[:, 2 * M :] = twice(x).astype(BF)
    at_ref[2 * M :, :] = rows_at(x, 0, HALF).astype(BF)
    target_ref[...] = twice(target)
    keep_ref[...] = twice(keep)
    basis = jnp.concatenate([cos_ref[...], -sin_ref[...]], axis=0)
    low = basis.astype(BF)
    at_ref[: 2 * M, :] = low
    rest_ref[...] = (basis - low.astype(F32)).astype(BF)
    turned = basis.T
    low = turned.astype(BF)
    a_ref[:, : 2 * M] = low
    rest_t_ref[...] = (turned - low.astype(F32)).astype(BF)


def mix_kernel(sizes, got_ref, mixer_ref, send_ref, spec_ref, thin_ref, wide_ref, out_ref):
    n_data, n_mode, nb, _ = sizes
    n_all = n_data * n_mode
    modes = M // n_mode
    nbm = nb * modes
    wide = D // n_data
    share = FF // n_all
    got = got_ref[...]
    thin = jnp.sum(got, axis=0)
    thin_ref[...] = thin
    query = from_lane(thin[:LEAD], HALF, wide)
    query = jnp.where(iota(query.shape, 0) < C, query, 0.0)
    down = from_lane(thin[LEAD:], HALF, share)
    high, low = split(down)
    down = jnp.concatenate([high, low], axis=0).astype(BF)
    spread = []
    for part in range(2):
        block = at_lane(query, part * wide, wide)
        zero = jnp.zeros_like(block)
        for k in range(nb):
            blocks = [block if g == k else zero for g in range(nb)]
            spread.append(jnp.concatenate(blocks, axis=1))
    spread = jnp.concatenate(spread, axis=0)
    inner = got.reshape(n_all * 16, LANES)
    inner = by_halves(fold(jnp.where(iota(inner.shape, 1) < HALF, inner, 0.0)))
    high, low = split(rows_at(spread, 0, HALF))
    spec = mm(inner, jnp.concatenate([high, high], axis=0).astype(BF))
    spec += mm(inner, jnp.concatenate([low, jnp.zeros_like(low)], axis=0).astype(BF))
    for k in range(nb):
        wide_ref[k] = spec[:, k * LANES : (k + 1) * LANES]
    for m in range(modes):
        spec = [wide_ref[k, pl.ds(m, n_all, stride=16), :][:, : 2 * wide] for k in range(nb)]
        spec = jnp.concatenate(spec, axis=0).astype(BF)
        spec_ref[m] = spec
        mixed = mm(spec, mixer_ref[m])
        for k in range(nb):
            out_ref[pl.ds(k * modes + m, n_all, stride=nbm), :] = mixed[
                k * n_all : (k + 1) * n_all
            ]
    for d in range(n_all):
        send_ref[d, :nbm, :] = out_ref[d * nbm : (d + 1) * nbm, :].astype(BF)
        send_ref[d, nbm:, :] = down


def mix_back_kernel(
    sizes, got_ref, mixer_ref, first_ref, stat_ref, send_ref, grad_ref, thin_ref, in_ref, wide_ref
):
    n_data, n_mode, nb, _ = sizes
    n_all = n_data * n_mode
    modes = M // n_mode
    nbm = nb * modes
    wide = D // n_data
    share = FF // n_all
    thin = jnp.zeros((16, LANES), F32)
    for d in range(n_all):
        in_ref[d * nbm : (d + 1) * nbm, :] = got_ref[d, :nbm, :].astype(F32)
        thin += got_ref[d, nbm:, :].astype(F32)
    thin = thin[:LEAD] + thin[LEAD:]
    thin_ref[...] = thin
    if modes < 16:
        wide_ref[...] = jnp.zeros_like(wide_ref)
    for m in range(modes):
        grad = [in_ref[pl.ds(k * modes + m, n_all, stride=nbm), :] for k in range(nb)]
        grad = jnp.concatenate(grad, axis=0).astype(BF)
        grad_ref[m] = grad
        back = mm(grad, mixer_ref[m], NT).astype(BF).astype(F32)
        if 2 * wide < LANES:
            back = jnp.concatenate(
                [back, jnp.zeros((back.shape[0], LANES - 2 * wide), F32)], axis=1
            )
        for k in range(nb):
            wide_ref[k, pl.ds(m, n_all, stride=16), :] = back[k * n_all : (k + 1) * n_all]
    inner = first_ref[...].reshape(n_all * 16, LANES)
    inner = jnp.where(iota(inner.shape, 1) < HALF, inner, 0.0)
    inner = by_halves(fold(inner))
    total = jnp.zeros((LEAD, LANES), F32)
    for k in range(nb):
        query = mm(inner, wide_ref[k].astype(BF), TN)
        query = query[:HALF] + query[HALF:]
        for part in range(2):
            at = (part * nb + k) * LEAD
            total += from_lane(query[at : at + LEAD], part * wide, wide)
    block = total + at_lane(from_lane(thin, 0, share), HALF, share)
    row, lane = iota(block.shape, 0), iota(block.shape, 1)
    stats = jnp.where(lane < HALF, stat_ref[:1, :], stat_ref[1:2, :])
    block = jnp.where(row == C, stats, block)
    for d in range(n_all):
        send_ref[d] = block


def spectral_kernel(
    modes,
    wide,
    ready,
    spec_ref,
    grad_ref,
    w_ref,
    m_ref,
    v_ref,
    ema_ref,
    w_out,
    m_out,
    v_out,
    ema_out,
    low_out,
    pair_ref,
    turn_ref,
):
    ready()
    lower = iota((wide, LANES), 1) < HALF
    half_lower = iota((wide // 2, LANES), 1) < HALF
    for m in range(modes):
        slopes = mm(spec_ref[m], grad_ref[m], TN)
        other = pltpu.roll(slopes[wide:], HALF, 1)
        pair_ref[m] = jnp.where(lower, slopes[:wide] + other, slopes[:wide] - other)
        even = pair_ref[m, pl.ds(0, wide // 2, stride=2), :]
        odd = pair_ref[m, pl.ds(1, wide // 2, stride=2), :]
        real = jnp.where(half_lower, even, pltpu.roll(odd, HALF, 1))
        imag = jnp.where(half_lower, pltpu.roll(even, HALF, 1), odd)
        turn_ref[0, pl.ds(m, wide // 2, stride=modes), :] = real
        turn_ref[1, pl.ds(m, wide // 2, stride=modes), :] = imag
    for part in range(2):
        for at in range(wide // 2):
            cols = slice(at * LANES, (at + 1) * LANES)
            grad = turn_ref[part, at * modes : (at + 1) * modes, :]
            new = adamw(
                w_ref[part, :, cols],
                grad,
                m_ref[part, :, cols],
                v_ref[part, :, cols],
                ema_ref[part, :, cols],
                RATE_SPEC,
            )
            for ref, value in zip((w_out, m_out, v_out, ema_out, low_out), new, strict=True):
                ref[part, :, cols] = value


def rows_kernel(
    sizes,
    n_big,
    got_ref,
    thin_ref,
    steps_ref,
    w_ref,
    m_ref,
    v_ref,
    ema_ref,
    *refs,
):
    big_refs, (loss_ref, w_out, m_out, v_out, ema_out, low_out) = refs[:n_big], refs[n_big:]
    n_data, n_mode, _, total = sizes
    n_all = n_data * n_mode
    wide = D // n_data
    share = FF // n_all
    rows = w_ref.shape[0]
    query = []
    for at in range(D // LANES):
        block = jnp.zeros((LEAD, LANES), F32)
        for i in range(at * LANES // wide, (at + 1) * LANES // wide):
            part = sum(got_ref[i * n_mode + j, :LEAD, :] for j in range(n_mode))
            block += at_lane(part, i * wide % LANES, wide)
        query.append(block)
    query = jnp.concatenate(query, axis=1)
    down = []
    for at in range(FF // LANES):
        block = jnp.zeros((LEAD, LANES), F32)
        for d in range(at * LANES // share, (at + 1) * LANES // share):
            block += at_lane(from_lane(got_ref[d, :LEAD, :], HALF, share), d * share % LANES, share)
        down.append(block)
    down = jnp.where(iota((LEAD, FF), 0) < C, jnp.concatenate(down, axis=1), 0.0)
    norm = SPECTRAL_WEIGHT / (total * M * S)
    stats = sum(got_ref[d, C : C + 1, :] for d in range(n_all))
    steps = steps_ref[C : C + 1, HALF : HALF + 1]
    loss_ref[...] = stats[:, :1] / steps + norm * stats[:, HALF : HALF + 1]

    keep = iota((LEAD, D), 0) < C
    query = jnp.where(keep, query, 0.0)
    query = jnp.concatenate(split(query), axis=0).astype(BF)
    down = jnp.concatenate(split(down), axis=0).astype(BF)
    thin = thin_rows(w_ref)
    embed = at_lane(thin, 0, C) + at_lane(from_lane(thin, 0, C), LEAD, C)
    head = from_lane(thin, LEAD, C)
    head = at_lane(head, 0, C) + at_lane(head, LEAD, C)

    def back(weights, sums):
        sums = jnp.concatenate([sums, jnp.zeros((LANES - 16, sums.shape[1]), BF)], axis=0)
        out = mm(weights.astype(BF), sums, NT)
        return from_lane(out, 0, LEAD) + from_lane(out, LEAD, LEAD)

    own = jnp.concatenate([thin_ref[...], jnp.zeros((LANES - LEAD, LANES), F32)], axis=0).T
    embed_grad = own[HALF : HALF + rows] + back(w_ref[:, :D], query)
    head_grad = own[HALF + rows : HALF + 2 * rows] + back(
        w_ref[:, 2 * D + FF : 2 * D + 2 * FF], down
    )
    last = at_lane(embed_grad, 0, C) + at_lane(head_grad, C, C)

    def update(grad, cols):
        new = adamw(w_ref[:, cols], grad, m_ref[:, cols], v_ref[:, cols], ema_ref[:, cols], RATE_DENSE)
        for ref, value in zip((w_out, m_out, v_out, ema_out, low_out), new, strict=True):
            ref[:, cols] = value

    update(mm(embed[:, :16].astype(BF), query), slice(0, D))
    update(sum(ref[...].astype(F32) for ref in big_refs), slice(D, 2 * D + FF))
    update(mm(head[:, :16].astype(BF), down), slice(2 * D + FF, 2 * D + 2 * FF))
    update(last[:, : 2 * C], slice(2 * D + 2 * FF, 2 * D + 2 * FF + 2 * C))


def per_device(
    series,
    future_values,
    step_mask,
    mode_index,
    dense,
    dense_m,
    dense_v,
    dense_ema,
    spectral,
    spec_m,
    fourier_variance_moment,
    spec_ema,
):
    n_mode = lax.axis_size("mode")
    n_data = lax.axis_size("dp")
    n_all = n_mode * n_data
    time_rows, batch, chans = series.shape
    nb = batch // n_mode
    total = batch * n_data
    modes = M // n_mode
    wide = D // n_data
    rows = dense.shape[0]
    shape = jax.ShapeDtypeStruct
    sizes = (n_data, n_mode, nb, total)
    tiled = rows % 16 == 0 and n_mode == 4 and n_data >= 4

    send, weights = call(
        partial(pack_kernel, sizes),
        (shape((n_mode, 2 * nb * LEAD, time_rows), F32), shape((rows, D + FF + LANES), BF)),
        (series.transpose(2, 1, 0), future_values.transpose(2, 1, 0), step_mask.T, dense),
        [pltpu.VMEM((chans, batch, time_rows), F32), pltpu.VMEM((batch, time_rows), F32)],
        name="pack",
        ahead=(0, 1, 2, 3),
    )
    me = jnp.stack([lax.axis_index("dp"), lax.axis_index("mode")]).astype(jnp.int32)
    own = exchange(send, "mode")
    cosv, sinv = tables(mode_index)
    weights = [gather_rows(weights)] if not tiled else gather_tiles_first(weights)
    if tiled:
        weights = gather_tiles_second(*weights)

    whole_rows = [pltpu.VMEM((2 * nb * LEAD, S), F32)]
    send = call(
        partial(spectra_kernel, sizes),
        shape((n_all, 16, LANES), F32),
        (own, cosv, sinv, dense),
        whole_rows,
        name="spectra",
    )
    first = exchange(send, AXES)
    ins = call(
        tables_kernel,
        (
            shape((S, 4 * M), BF),
            shape((3 * M, S), BF),
            shape((2 * M, S), BF),
            shape((S, 2 * M), BF),
            shape((S, LANES), F32),
            shape((S, LANES), F32),
        ),
        (own, cosv, sinv),
        whole_rows,
        name="tables",
        cost=10**10,
    )
    first, *ins = together(first, *ins)
    if tiled:
        weights = gather_tiles_third(*weights)

    w_low = spectral.astype(BF).reshape(2, modes, wide, E)
    mixer = jnp.concatenate(
        [
            jnp.concatenate([w_low[0], w_low[1]], axis=2),
            jnp.concatenate([-w_low[1], w_low[0]], axis=2),
        ],
        axis=1,
    )
    scratch = [
        pltpu.VMEM((nb, n_all * 16, LANES), F32),
        pltpu.VMEM((n_all * nb * modes, LANES), F32),
    ]
    send, spec, thin = call(
        partial(mix_kernel, sizes),
        (
            shape((n_all, nb * modes + 16, LANES), BF),
            shape((modes, total, 2 * wide), BF),
            shape((16, LANES), F32),
        ),
        (first, mixer),
        scratch,
        name="mix",
    )
    if tiled:
        send, *weights = together(send, *weights)
        weights = gather_tiles_last(weights)
    got = exchange(send, AXES)
    steps = thin

    send, stats, *big = block(
        steps[C, HALF].reshape(1),
        me,
        weights,
        (got, *ins),
        sizes + (True,) if tiled else sizes,
    )
    got = exchange(send, AXES)
    if tiled:
        big = scatter_tiles_first(*big)
        got, *big = together(got, *big)
        big = scatter_tiles_second(*big)
    send, grad_mixed, thin = call(
        partial(mix_back_kernel, sizes),
        (
            shape((n_all, LEAD, LANES), F32),
            shape((modes, total, LANES), BF),
            shape((LEAD, LANES), F32),
        ),
        (got, mixer, first, stats),
        scratch[::-1],
        name="mix_back",
        cost=10**10,
    )
    if tiled:
        grad_mixed, big = together(grad_mixed, big)
    spec_out = call(
        partial(spectral_kernel, modes, wide),
        (shape(spectral.shape, F32),) * 4 + (shape(spectral.shape, BF),),
        (spec, grad_mixed, spectral, spec_m, fourier_variance_moment, spec_ema),
        [
            pltpu.VMEM((modes, wide, LANES), F32),
            pltpu.VMEM((2, modes * wide // 2, LANES), F32),
        ],
        name="spectral",
        ahead=(0, 1, 2, 3, 4, 5),
        cost=10**10,
    )
    got = exchange(send, AXES)
    big = scatter_tiles_third(*big) if tiled else [scatter_rows(big[0], rows)]
    loss, *dense_out = call(
        partial(rows_kernel, sizes, len(big)),
        (shape((1, 1), F32),) + (shape(dense.shape, F32),) * 4 + (shape(dense.shape, BF),),
        (got, thin, steps, dense, dense_m, dense_v, dense_ema, *big),
        name="rows",
    )
    return (loss.reshape(()),) + tuple(dense_out) + tuple(spec_out)


def solution(mesh):
    rows = P(("dp", "mode"), None)
    mixing = P(None, "mode", "dp")
    return jax.shard_map(
        per_device,
        mesh=mesh,
        in_specs=(P("mode", "dp", None), P("mode", "dp", None), P("mode", "dp"), P())
        + (rows,) * 4
        + (mixing,) * 4,
        out_specs=(P(),) + (rows,) * 5 + (mixing,) * 5,
        check_vma=False,
    )
```

```python
import math
from functools import partial

import jax
import jax.numpy as jnp
from jax import lax
from jax.experimental import pallas as pl
from jax.experimental.pallas import tpu as pltpu
from jax.sharding import PartitionSpec as P

D = 512
H = 8
E = 64
FF = 2048
M = 64
C = 7
S = 768
LANES = 128

SPECTRAL_WEIGHT = 0.5
RATE_DENSE = 0.02
RATE_SPEC = 0.1
BF = jnp.bfloat16
F32 = jnp.float32
AXES = ("dp", "mode")
SLOPE = jnp.bfloat16
VMEM_BYTES = 60 * 1024 * 1024
FULL_BYTES = 60 * 1024 * 1024
SMALL_BYTES = 16 * 1024 * 1024


def plain(spec, left, right):
    return jnp.einsum(spec, left, right, preferred_element_type=F32)


def exact(spec, left, right):
    return jnp.einsum(
        spec, left, right, precision=lax.Precision.HIGHEST, preferred_element_type=F32
    )


def tables(mode_index):
    steps = jnp.arange(S, dtype=jnp.int32)
    phase = mode_index[:, None] * steps[None, :] % S
    angle = phase.astype(F32) * (2.0 * math.pi / S)
    return (jnp.cos(angle), jnp.sin(angle))


def unpack(whole):
    return (
        whole[:, :D],
        whole[:, D : 2 * D],
        whole[:, 2 * D : 2 * D + FF],
        whole[:, 2 * D + FF : 2 * D + 2 * FF],
        whole[:, 2 * D + 2 * FF : 2 * D + 2 * FF + C],
        whole[:, 2 * D + 2 * FF + C :],
    )


def adamw(weight, grad, first, second, average, rate):
    first_new = 0.5 * first + 0.5 * grad
    second_new = 0.5 * second + 0.5 * grad * grad
    weight_new = weight - rate * (first_new / (jnp.sqrt(second_new) + 1e-08) + 0.01 * weight)
    average_new = 0.9 * average + 0.1 * weight_new
    return (weight_new, first_new, second_new, average_new, weight_new.astype(BF))


def halves(x):
    high = x.astype(BF)
    return high, (x - high.astype(F32)).astype(BF)


def fill(x, size, axis):
    wanted = list(x.shape)
    wanted[axis] = size - x.shape[axis]
    return jnp.concatenate([x, jnp.zeros(wanted, x.dtype)], axis=axis) if wanted[axis] else x


def exchange(x, axes):
    return lax.all_to_all(x, axes, 0, 0, tiled=True)


def partners(step):
    count = lax.axis_size("mode")
    return [(index, index ^ step) for index in range(count)]


def bit_of(step):
    return lax.div(lax.axis_index("mode"), step) % 2


def steps_of_mode():
    return [1 << bit for bit in range(lax.axis_size("mode").bit_length() - 1)]


def by_xor(x, axis, step):
    count = lax.axis_size(axis)
    return lax.ppermute(x, axis, [(index, index ^ step) for index in range(count)])


def tile_offsets(n_data):
    cut = n_data // 4
    low = [2 * step for step in range(cut)]
    high = [2 * step for step in range(cut, 2 * cut)]
    ones = lambda data: [index + 1 for index in data]
    offsets = [
        (low + ones(low), [0] * 2 * cut),
        (low + ones(low), [2] * 2 * cut),
        (high + high, [0] * cut + [2] * cut),
        (ones(high) + ones(high), [0] * cut + [2] * cut),
    ]
    return offsets + [(data, [index + 1 for index in mode]) for data, mode in offsets]


def gather_tiles_first(x):
    n_data = lax.axis_size("dp")
    deep = [x] + [by_xor(x, "dp", 2 * step) for step in range(1, n_data // 2)]
    cut = len(deep) // 2
    return jnp.stack(deep[:cut]), jnp.stack(deep[cut:])


def gather_tiles_second(first, second):
    first = jnp.concatenate([first, by_xor(first, "dp", 1)])
    return first, jnp.concatenate([second, by_xor(second, "mode", 2)])


def gather_tiles_third(first, second):
    return [first, by_xor(first, "mode", 2), second, by_xor(second, "dp", 1)]


def gather_tiles_last(pieces):
    return pieces + [by_xor(piece, "mode", 1) for piece in pieces]


def tile_order(n_data):
    cut = n_data // 4
    low = [2 * step for step in range(cut)]
    high = [2 * step for step in range(cut, 2 * cut)]
    groups = [
        [(data + x, 2) for data in low for x in (0, 1)],
        [(data + x, 0) for data in low for x in (0, 1)],
        [(data + 1, 2 * y) for data in high for y in (0, 1)],
        [(data, 2 * y) for data in high for y in (0, 1)],
    ]
    return [[(data, mode + core) for data, mode in group] for core in (1, 0) for group in groups]


def together(*values):
    return lax.optimization_barrier(values)


def total_of(terms, pick):
    return sum(term[pick].astype(F32) for term in terms)


def scatter_tiles_first(away, stay):
    pairs = lambda terms: [x.reshape((x.shape[0] // 2, 2) + x.shape[1:]) for x in terms]
    come = by_xor(away, "mode", 1)
    first = by_xor(total_of([stay, come], 0).astype(BF), "mode", 2)
    second = by_xor(total_of([stay, come], 2).astype(BF), "dp", 1)
    first = pairs([stay[1], come[1], first])
    second = pairs([stay[3], come[3], second])
    away = [total_of(terms, (slice(None), 1)).astype(BF) for terms in (first, second)]
    return away + [[x[:, 0] for x in terms] for terms in (first, second)]


def scatter_tiles_second(first_away, second_away, first, second):
    return [first + [by_xor(first_away, "dp", 1)], second + [by_xor(second_away, "mode", 2)]]


def scatter_tiles_third(first, second):
    cut = first[0].shape[0]
    come = []
    for step in range(1, 2 * cut):
        terms, at = (first, step) if step < cut else (second, step - cut)
        come.append(by_xor(total_of(terms, at).astype(BF), "dp", 2 * step))
    return [total_of(first, 0)] + come


def gather_rows(x):
    n_data = lax.axis_size("dp")
    held = exchange(jnp.broadcast_to(x[None], (n_data,) + x.shape), "dp")[:, None]
    for step in reversed(steps_of_mode()):
        other = lax.ppermute(held, "mode", partners(step))
        first = bit_of(step) == 0
        pair = [jnp.where(first, held, other), jnp.where(first, other, held)]
        held = jnp.stack(pair, axis=2).reshape(n_data, -1, *x.shape)
    return held.reshape(-1, x.shape[1])


def scatter_rows(x, rows):
    n_data, n_mode = lax.axis_size("dp"), lax.axis_size("mode")
    held = x.reshape(n_data, n_mode, rows, x.shape[1])
    for step in steps_of_mode():
        held = held.reshape(n_data, held.shape[1] // 2, 2, rows, x.shape[1])
        bit = bit_of(step)
        away = lax.dynamic_index_in_dim(held, 1 - bit, 2, keepdims=False)
        stay = lax.dynamic_index_in_dim(held, bit, 2, keepdims=False)
        other = lax.ppermute(away, "mode", partners(step))
        held = (stay.astype(F32) + other.astype(F32)).astype(BF)
    held = exchange(held.reshape(n_data, rows, x.shape[1]), "dp")
    return jnp.sum(held.astype(F32), axis=0)


NN = (((1,), (0,)), ((), ()))
NT = (((1,), (1,)), ((), ()))
TN = (((0,), (0,)), ((), ()))
FIRST = 2.0 * math.sqrt(2.0 / math.pi)
THIRD = FIRST * 0.044715
GATES = 1024
UNROLL = 2
LEAD = 8
HALF = 64


def mm(left, right, dims=NN):
    return lax.dot_general(left, right, dims, preferred_element_type=F32)


def iota(shape, axis):
    return lax.broadcasted_iota(jnp.int32, shape, axis)


def split(x):
    high = x.astype(BF).astype(F32)
    return high, x - high


def by_halves(x):
    high, low = split(x)
    return jnp.where(iota(x.shape, 1) < HALF, high, low).astype(BF)


def fold(x):
    return x + pltpu.roll(x, HALF, 1)


def rows_at(x, first, count):
    parts = []
    if first:
        parts.append(jnp.zeros((first, x.shape[1]), F32))
    parts.append(x)
    if count - first - x.shape[0]:
        parts.append(jnp.zeros((count - first - x.shape[0], x.shape[1]), F32))
    return jnp.concatenate(parts, axis=0)


def row_groups(x):
    return sum(x[at : at + LEAD] for at in range(0, x.shape[0], LEAD))


def block_kernel(sizes, count_ref, me_ref, *refs):
    if len(sizes) == 4:
        block_steps(sizes, lambda what: None, count_ref, *refs)
        return
    n_data, n_mode = sizes[:2]
    rows = D // n_data // n_mode
    offsets = tile_offsets(n_data)
    n_pieces = len(offsets)
    pieces, got_ref, sources, refs = refs[:n_pieces], refs[n_pieces], refs[n_pieces + 1 : n_pieces + 7], refs[n_pieces + 7 :]
    send_ref, stat_ref, away_ref, stay_ref, row_sems, sems, w_ref = refs[:7]
    places, scratch = refs[7:13], refs[13:]
    act_ref = scratch[5]

    def rows_of(data, mode):
        owner = (me_ref[0] ^ data) * n_mode + (me_ref[1] ^ mode)
        return pl.ds(pl.multiple_of(owner * rows, rows), rows)

    row_copies = []
    for ref, (data, mode) in zip(pieces, offsets, strict=True):
        for at, (one, two) in enumerate(zip(data, mode, strict=True)):
            place = w_ref.at[rows_of(one, two), :]
            row_copies.append(
                pltpu.make_async_copy(ref.at[at], place, row_sems.at[len(row_copies)])
            )
            row_copies[-1].start()
    copies = [
        pltpu.make_async_copy(source, place, sems.at[at])
        for at, (source, place) in enumerate(zip(sources, places, strict=True))
    ]
    for copy in copies:
        copy.start()
    waits = {"rows": row_copies, "a": copies[:1], "rest": copies[1:]}

    def ready(what):
        for copy in waits[what]:
            copy.wait()

    block_steps(sizes, ready, count_ref, w_ref, got_ref, *places, send_ref, stat_ref, None, *scratch)
    for at, group in enumerate(tile_order(n_data)):
        ref = away_ref if at < 4 else stay_ref
        for index, (data, mode) in enumerate(group):
            ref[at % 4, index, :, :D] = act_ref[1, rows_of(data, mode), :D]
            ref[at % 4, index, :, D:] = act_ref[0, rows_of(data, mode), :]


def block_steps(
    sizes,
    ready,
    count_ref,
    w_ref,
    got_ref,
    a_ref,
    at_ref,
    rest_ref,
    rest_t_ref,
    target_ref,
    keep_ref,
    send_ref,
    stat_ref,
    big_ref,
    wdup_ref,
    x_ref,
    v_ref,
    r_ref,
    wd_ref,
    act_ref,
    slope_ref,
    fc_ref,
    zx_ref,
    j_ref,
):
    n_data, n_mode, nb, total = sizes[:4]
    n_all = n_data * n_mode
    modes = M // n_mode
    nbm = nb * modes
    share = FF // n_all
    rows = D // n_all
    scale = 2.0 / S
    norm = SPECTRAL_WEIGHT / (total * M * S)
    chunks = FF // GATES

    for i in range(n_data):
        blocks = [got_ref[i * n_mode + j, :nbm, :].astype(F32) for j in range(n_mode)]
        for k in range(nb):
            column = [block[k * modes : (k + 1) * modes] for block in blocks]
            x_ref[k * M : (k + 1) * M, i * LANES : (i + 1) * LANES] = jnp.concatenate(
                column, axis=0
            ).astype(BF)

    per = LANES // share
    for at in range(FF // LANES):
        block = jnp.zeros((16, LANES), F32)
        for q in range(per):
            piece = got_ref[at * per + q, nbm : nbm + 16, :].astype(F32)
            piece = pltpu.roll(piece, q * share, 1) if q else piece
            block = jnp.where(iota(block.shape, 1) // share == q, piece, block)
        spread = [
            rows_at(jnp.concatenate([half] * nb, axis=0), 0, HALF)
            for half in (block[:LEAD], block[LEAD:])
        ]
        wd_ref[:, at * LANES : (at + 1) * LANES] = jnp.concatenate(spread, axis=0).astype(BF)
    ready("rows")
    for i in range(n_data):
        head = i * H // n_data
        block = w_ref[head * E : (head + 1) * E, :D]
        wdup_ref[2 * i * E : (2 * i + 1) * E, :] = block
        wdup_ref[(2 * i + 1) * E : (2 * i + 2) * E, :] = block
    x_all = x_ref[...]
    real_lane = iota(x_all.shape, 1) % LANES < HALF
    zero = jnp.zeros_like(x_all)
    x_real = jnp.where(real_lane, x_all, zero)
    x_imag = jnp.where(real_lane, zero, x_all)
    line_real = scale * mm(x_real, wdup_ref[...])
    line_imag = scale * mm(x_imag, wdup_ref[...])
    for k in range(nb):
        v_ref[2 * k * M : (2 * k + 1) * M, :] = line_real[k * M : (k + 1) * M].astype(BF)
        v_ref[(2 * k + 1) * M : (2 * k + 2) * M, :] = line_imag[k * M : (k + 1) * M].astype(BF)

    thin_t = w_ref[:, D + FF :].astype(F32).T
    embed_t = thin_t[:LEAD]
    head_t = thin_t[LEAD : 2 * LEAD]
    pad = [jnp.zeros((HALF - nb * LEAD, D), F32)] if nb * LEAD < HALF else []
    embed_all = jnp.concatenate([embed_t] * nb + pad, axis=0).astype(BF)
    head_all = jnp.concatenate([head_t] * nb + pad, axis=0).astype(BF)
    head_twice = jnp.concatenate([head_all, head_all], axis=0)
    embed_twice = jnp.concatenate([embed_t, embed_t], axis=0).astype(BF)

    for c in range(FF // 512):
        cols = slice(c * 512, (c + 1) * 512)
        w_up = w_ref[:, D + c * 512 : D + (c + 1) * 512]
        lifted = mm(v_ref[...], w_up)
        thin = mm(embed_twice, w_up)[:LEAD]
        high, low = split(thin)
        for k in range(nb):
            r_ref[k, : 2 * M, cols] = lifted[2 * k * M : 2 * (k + 1) * M].astype(BF)
            r_ref[k, 2 * M :, cols] = jnp.concatenate(
                [rows_at(high, k * LEAD, HALF), rows_at(low, k * LEAD, HALF)], axis=0
            ).astype(BF)

    parts = [mm(head_all[:16], v_ref[2 * k * M : 2 * (k + 1) * M, :], NT)[:LEAD] for k in range(nb)]
    by_head = rows_at(jnp.concatenate(parts, axis=0), 0, HALF)
    cross = mm(head_all, jnp.concatenate([embed_all, jnp.zeros_like(embed_all)], axis=0), NT)
    cross = jnp.where(iota(cross.shape, 0) // LEAD == iota(cross.shape, 1) // LEAD, cross, 0.0)
    high, low = split(jnp.concatenate([by_head, cross], axis=1))
    by_head = jnp.concatenate([high, low], axis=0).astype(BF)
    ready("a")
    fc_ref[...] = mm(a_ref[...], by_head, NT)

    own_lane = iota((S, LANES), 1) % HALF // LEAD

    def forward(step, carry):
        k = step // chunks
        cols = pl.ds(pl.multiple_of(step % chunks * GATES, GATES), GATES)
        gate = mm(a_ref[...], r_ref[k, :, cols])
        square = gate * gate
        sig = 0.5 * jnp.tanh(gate * (square * (0.5 * THIRD) + 0.5 * FIRST)) + 0.5
        act = gate * sig
        low = act.astype(BF)
        act_ref[k, :, cols] = low
        slope = sig + act * (1.0 - sig) * (square * (3.0 * THIRD) + FIRST)
        slope_ref[k, :, cols] = slope.astype(slope_ref.dtype)
        fc_ref[...] += jnp.where(own_lane == k, mm(low, wd_ref[:, cols], NT), 0.0)
        return carry

    lax.fori_loop(0, nb * chunks, forward, 0, unroll=UNROLL)

    ready("rest")
    keep = keep_ref[...]
    masked = keep * (fold(fc_ref[...]) - target_ref[...])
    two = by_halves(masked)
    err = fold(mm(at_ref[: 2 * M, :], two) + mm(rest_ref[...], two))
    stat_ref[...] = jnp.concatenate(
        [
            jnp.full((1, LANES), 0.5 * jnp.sum(masked * masked)),
            jnp.full((1, LANES), 0.5 * jnp.sum(err * err)),
            jnp.zeros((6, LANES), F32),
        ],
        axis=0,
    )
    two = by_halves(err)
    back = fold(mm(a_ref[:, : 2 * M], two) + mm(rest_t_ref[...], two))
    g_fc = keep * ((2.0 / count_ref[0]) * masked + (2.0 * norm) * back)
    g_low = g_fc.astype(BF)
    g_turn = g_fc.T[:HALF].astype(BF)
    zx_ref[...] = jnp.zeros_like(zx_ref)
    j_ref[...] = jnp.zeros_like(j_ref)

    def backward(step, carry):
        k = step // chunks
        cols = pl.ds(pl.multiple_of(step % chunks * GATES, GATES), GATES)
        fed = mm(jnp.where(own_lane == k, g_fc, 0.0).astype(BF), wd_ref[:, cols])
        g_gate = (fed * slope_ref[k, :, cols].astype(F32)).astype(BF)
        turned = mm(at_ref[...], g_gate)
        r_ref[k, : 2 * M, cols] = turned[: 2 * M].astype(BF)
        own = iota((HALF, GATES), 0) // LEAD == k
        zx_ref[:, cols] += jnp.where(own, turned[2 * M :], 0.0)
        j_ref[:, cols] += jnp.where(own, mm(g_turn, act_ref[k, :, cols]), 0.0)
        return carry

    lax.fori_loop(0, nb * chunks, backward, 0, unroll=UNROLL)

    back_fc = by_halves(mm(at_ref[...], g_low))
    lane_of = iota((2 * M, LANES), 1) % HALF // LEAD
    nothing = jnp.zeros((2 * M, LANES), F32)
    back_rows = jnp.concatenate(
        [jnp.where(lane_of == k, back_fc[: 2 * M].astype(F32), nothing) for k in range(nb)], axis=0
    ).astype(BF)
    cross = jnp.where(
        iota((HALF, LANES), 0) // LEAD == iota((HALF, LANES), 1) % HALF // LEAD,
        back_fc[2 * M :].astype(F32),
        0.0,
    ).astype(BF)
    v_all = v_ref[...]
    z_all = r_ref[:, : 2 * M, :].reshape(nb * 2 * M, FF)
    high, low = split(row_groups(zx_ref[...]))
    zx = jnp.concatenate([high, low], axis=0).astype(BF)
    w_up = w_ref[:, D : D + FF]
    back_block = mm(z_all, w_up, NT) + mm(back_rows, head_twice)
    turned = (scale * back_block).astype(BF)
    embed_grad = row_groups(mm(zx, w_up, NT)) + row_groups(mm(cross, head_twice))
    head_grad = row_groups(mm(back_rows, v_all, TN)) + row_groups(mm(cross, embed_all, TN))
    down_grad = row_groups(j_ref[...])

    turned_real = jnp.concatenate(
        [turned[2 * k * M : (2 * k + 1) * M] for k in range(nb)], axis=0
    )
    turned_imag = jnp.concatenate(
        [turned[(2 * k + 1) * M : (2 * k + 2) * M] for k in range(nb)], axis=0
    )
    p_real = mm(turned_real, wdup_ref[...], NT)
    p_imag = mm(turned_imag, wdup_ref[...], NT)
    real_lane = iota((modes, LANES), 1) < HALF
    lane = iota((LEAD, LANES), 1)
    for i in range(n_data):
        cols = slice(i * LANES, (i + 1) * LANES)
        for j in range(n_mode):
            d = i * n_mode + j
            pieces = []
            for k in range(nb):
                at = slice(k * M + j * modes, k * M + (j + 1) * modes)
                pieces.append(jnp.where(real_lane, p_real[at, cols], p_imag[at, cols]))
            send_ref[d, :nbm, :] = jnp.concatenate(pieces, axis=0).astype(BF)
            out = jnp.zeros((LEAD, LANES), F32)
            for source, width, place in (
                (down_grad, share, 0),
                (embed_grad, rows, HALF),
                (head_grad, rows, HALF + rows),
            ):
                first = d * width // LANES * LANES
                piece = source[:, first : first + LANES]
                shift = (place - (d * width - first)) % LANES
                piece = pltpu.roll(piece, shift, 1) if shift else piece
                out = jnp.where((lane >= place) & (lane < place + width), piece, out)
            high, low = split(out)
            send_ref[d, nbm:, :] = jnp.concatenate([high, low], axis=0).astype(BF)

    x_all = x_ref[...]
    real_lane = iota(x_all.shape, 1) % LANES < HALF
    x_real = jnp.where(real_lane, x_all, zero)
    x_imag = jnp.where(real_lane, zero, x_all)
    out_grad = mm(x_real, turned_real, TN) + mm(x_imag, turned_imag, TN)
    each = n_data // H
    for head in range(H):
        block = 0.0
        for i in range(head * each, (head + 1) * each):
            block += out_grad[2 * i * E : (2 * i + 1) * E] + out_grad[(2 * i + 1) * E : (2 * i + 2) * E]
        out = act_ref.at[1] if big_ref is None else big_ref
        out[head * E : (head + 1) * E, :D] = block.astype(BF)
    for c in range(FF // 512):
        cols = slice(c * 512, (c + 1) * 512)
        up_grad = mm(v_all, z_all[:, cols], TN) + mm(embed_twice, zx[:, cols], TN)
        if big_ref is None:
            act_ref[0, :D, cols] = up_grad.astype(BF)
        else:
            big_ref[:, D + c * 512 : D + (c + 1) * 512] = up_grad.astype(BF)


def block(count, me, weights, ins, sizes):
    n_data, n_mode, nb = sizes[:3]
    tiled = len(sizes) > 4
    whole = pl.BlockSpec(memory_space=pltpu.VMEM)
    far = pl.BlockSpec(memory_space=pl.ANY if tiled else pltpu.VMEM)
    big = [jax.ShapeDtypeStruct((D, D + FF), BF)]
    scratch = []
    if tiled:
        half = (4, n_data * n_mode // 8, D // n_data // n_mode, D + FF)
        big = [jax.ShapeDtypeStruct(half, BF)] * 2
        scratch = [
            pltpu.SemaphoreType.DMA((n_data * n_mode,)),
            pltpu.SemaphoreType.DMA((6,)),
            pltpu.VMEM((D, D + FF + LANES), BF),
        ]
        scratch += [pltpu.VMEM(x.shape, x.dtype) for x in ins[1:]]
    return pl.pallas_call(
        partial(block_kernel, sizes),
        out_shape=(
            jax.ShapeDtypeStruct(ins[0].shape, BF),
            jax.ShapeDtypeStruct((8, LANES), F32),
            *big,
        ),
        in_specs=[pl.BlockSpec(memory_space=pltpu.SMEM)] * 2
        + [far] * len(weights)
        + [whole]
        + [far] * (len(ins) - 1),
        out_specs=(whole,) * (2 + len(big)),
        scratch_shapes=scratch
        + [
            pltpu.VMEM((2 * n_data * E, D), BF),
            pltpu.VMEM((nb * M, n_data * LANES), BF),
            pltpu.VMEM((nb * 2 * M, D), BF),
            pltpu.VMEM((nb, 4 * M, FF), BF),
            pltpu.VMEM((LANES, FF), BF),
            pltpu.VMEM((nb, S, FF), BF),
            pltpu.VMEM((nb, S, FF), SLOPE),
            pltpu.VMEM((S, LANES), F32),
            pltpu.VMEM((HALF, FF), F32),
            pltpu.VMEM((HALF, FF), F32),
        ],
        compiler_params=pltpu.CompilerParams(vmem_limit_bytes=VMEM_BYTES),
        name="block",
    )(count, me, *weights, *ins)


def at_lane(x, first, width):
    x = pltpu.roll(x, first, 1) if first else x
    lane = iota(x.shape, 1)
    return jnp.where((lane >= first) & (lane < first + width), x, 0.0)


def from_lane(x, first, width):
    base = first // LANES * LANES
    x = x[:, base : base + LANES]
    shift = (LANES - (first - base)) % LANES
    x = pltpu.roll(x, shift, 1) if shift else x
    return jnp.where(iota(x.shape, 1) < width, x, 0.0)


def staged(kernel, ahead, *refs):
    sems = refs[-1]
    n_held = len(refs) - 1 - len(ahead)
    held = list(refs[:n_held])
    copies = []
    for at, (index, place) in enumerate(zip(ahead, refs[n_held:-1], strict=True)):
        copies.append(pltpu.make_async_copy(refs[index], place, sems.at[at]))
        copies[-1].start()
        held[index] = place

    def ready():
        for copy in copies:
            copy.wait()

    kernel(ready, *held)


def call(kernel, outs, ins, scratch=(), name=None, cost=0, ahead=()):
    whole = pl.BlockSpec(memory_space=pltpu.VMEM)
    in_specs = [whole] * len(ins)
    scratch = list(scratch)
    if ahead:
        kernel = partial(staged, kernel, ahead)
        for index in ahead:
            in_specs[index] = pl.BlockSpec(memory_space=pl.ANY)
            scratch.append(pltpu.VMEM(ins[index].shape, ins[index].dtype))
        scratch.append(pltpu.SemaphoreType.DMA((len(ahead),)))
    return pl.pallas_call(
        kernel,
        out_shape=outs,
        in_specs=in_specs,
        out_specs=jax.tree.map(lambda _: whole, outs),
        scratch_shapes=scratch,
        compiler_params=pltpu.CompilerParams(vmem_limit_bytes=FULL_BYTES if ahead else SMALL_BYTES),
        name=name,
        cost_estimate=pl.CostEstimate(flops=cost, bytes_accessed=cost // 10, transcendentals=0)
        if cost
        else None,
    )(*ins)


def thin_rows(dense_ref):
    thin = dense_ref[:, 2 * D + 2 * FF :]
    thin = jnp.concatenate([thin, jnp.zeros((thin.shape[0], LANES - 2 * C), F32)], axis=1)
    return at_lane(thin, 0, C) + at_lane(from_lane(thin, C, C), LEAD, C)


def pack_kernel(sizes, ready, series_ref, future_ref, mask_ref, dense_ref, send_ref, rows_ref, one_ref, two_ref):
    n_mode, nb = sizes[1:3]
    ready()
    one_ref[...] = series_ref[...].astype(F32)
    two_ref[...] = mask_ref[...].astype(F32)
    for j in range(n_mode):
        for k in range(nb):
            b = j * nb + k
            for c in range(C):
                send_ref[j, k * LEAD + c, :] = one_ref[c, b, :]
                send_ref[j, (nb + k) * LEAD + c, :] = future_ref[c, b, :]
            send_ref[j, k * LEAD + C, :] = two_ref[b, :]
            send_ref[j, (nb + k) * LEAD + C, :] = jnp.zeros_like(two_ref[b, :])
    rows_ref[:, : D + FF] = dense_ref[:, D : 2 * D + FF].astype(BF)
    rows_ref[:, D + FF :] = thin_rows(dense_ref).astype(BF)


def own_rows(got_ref, all_ref):
    steps = got_ref.shape[2]
    for j in range(got_ref.shape[0]):
        all_ref[:, j * steps : (j + 1) * steps] = got_ref[j]
    half = all_ref.shape[0] // 2
    inputs = all_ref[:half, :]
    mask = inputs
    inputs = jnp.where(iota(inputs.shape, 0) % LEAD == C, 0.0, inputs)
    return inputs, mask, all_ref[half:, :]


def spectra_kernel(sizes, got_ref, cos_ref, sin_ref, dense_ref, send_ref, all_ref):
    n_data, n_mode, nb, _ = sizes
    n_all = n_data * n_mode
    modes = M // n_mode
    wide = D // n_data
    share = FF // n_all
    x, mask, _ = own_rows(got_ref, all_ref)
    count = jnp.sum(jnp.where(iota(mask.shape, 0) % LEAD == C, mask, 0.0))
    low = cos_ref[...].astype(BF)
    inner = mm(low, rows_at(x, 0, LANES).astype(BF), NT)
    low = (-sin_ref[...]).astype(BF)
    inner += mm(low, rows_at(x, nb * LEAD, LANES).astype(BF), NT)
    thin = thin_rows(dense_ref).astype(BF)
    query = mm(thin, dense_ref[:, :D].astype(BF), TN)[:LEAD]
    down = mm(thin, dense_ref[:, 2 * D + FF : 2 * D + 2 * FF].astype(BF), TN)[LEAD : 2 * LEAD]
    row = iota((LEAD, LANES), 0)
    lane = iota((LEAD, LANES), 1)
    for i in range(n_data):
        ours = at_lane(from_lane(query, i * wide, wide), HALF, wide)
        ours = jnp.where((row == C) & (lane == HALF), count, ours)
        for j in range(n_mode):
            d = i * n_mode + j
            block = inner[j * modes : (j + 1) * modes]
            if modes < 16:
                block = jnp.concatenate([block, jnp.zeros((16 - modes, LANES), F32)], axis=0)
            theirs = at_lane(from_lane(down, d * share, share), HALF, share)
            send_ref[d] = block + jnp.concatenate([ours, theirs], axis=0)


def tables_kernel(
    got_ref, cos_ref, sin_ref, a_ref, at_ref, rest_ref, rest_t_ref, target_ref, keep_ref, all_ref
):
    x, mask, target = own_rows(got_ref, all_ref)
    count = x.shape[0]
    keep = [
        jnp.broadcast_to(mask[at + C : at + LEAD], (LEAD, S)) for at in range(0, count, LEAD)
    ]
    keep = jnp.concatenate(keep, axis=0)
    twice = lambda rows: jnp.concatenate([rows_at(rows, 0, HALF)] * 2, axis=0).T
    a_ref[:, 2 * M :] = twice(x).astype(BF)
    at_ref[2 * M :, :] = rows_at(x, 0, HALF).astype(BF)
    target_ref[...] = twice(target)
    keep_ref[...] = twice(keep)
    basis = jnp.concatenate([cos_ref[...], -sin_ref[...]], axis=0)
    low = basis.astype(BF)
    at_ref[: 2 * M, :] = low
    rest_ref[...] = (basis - low.astype(F32)).astype(BF)
    turned = basis.T
    low = turned.astype(BF)
    a_ref[:, : 2 * M] = low
    rest_t_ref[...] = (turned - low.astype(F32)).astype(BF)


def mix_kernel(sizes, got_ref, mixer_ref, send_ref, spec_ref, thin_ref, wide_ref, out_ref):
    n_data, n_mode, nb, _ = sizes
    n_all = n_data * n_mode
    modes = M // n_mode
    nbm = nb * modes
    wide = D // n_data
    share = FF // n_all
    got = got_ref[...]
    thin = jnp.sum(got, axis=0)
    thin_ref[...] = thin
    query = from_lane(thin[:LEAD], HALF, wide)
    query = jnp.where(iota(query.shape, 0) < C, query, 0.0)
    down = from_lane(thin[LEAD:], HALF, share)
    high, low = split(down)
    down = jnp.concatenate([high, low], axis=0).astype(BF)
    spread = []
    for part in range(2):
        block = at_lane(query, part * wide, wide)
        zero = jnp.zeros_like(block)
        for k in range(nb):
            blocks = [block if g == k else zero for g in range(nb)]
            spread.append(jnp.concatenate(blocks, axis=1))
    spread = jnp.concatenate(spread, axis=0)
    inner = got.reshape(n_all * 16, LANES)
    inner = by_halves(fold(jnp.where(iota(inner.shape, 1) < HALF, inner, 0.0)))
    high, low = split(rows_at(spread, 0, HALF))
    spec = mm(inner, jnp.concatenate([high, high], axis=0).astype(BF))
    spec += mm(inner, jnp.concatenate([low, jnp.zeros_like(low)], axis=0).astype(BF))
    for k in range(nb):
        wide_ref[k] = spec[:, k * LANES : (k + 1) * LANES]
    for m in range(modes):
        spec = [wide_ref[k, pl.ds(m, n_all, stride=16), :][:, : 2 * wide] for k in range(nb)]
        spec = jnp.concatenate(spec, axis=0).astype(BF)
        spec_ref[m] = spec
        mixed = mm(spec, mixer_ref[m])
        for k in range(nb):
            out_ref[pl.ds(k * modes + m, n_all, stride=nbm), :] = mixed[
                k * n_all : (k + 1) * n_all
            ]
    for d in range(n_all):
        send_ref[d, :nbm, :] = out_ref[d * nbm : (d + 1) * nbm, :].astype(BF)
        send_ref[d, nbm:, :] = down


def mix_back_kernel(
    sizes, got_ref, mixer_ref, first_ref, stat_ref, send_ref, grad_ref, thin_ref, in_ref, wide_ref
):
    n_data, n_mode, nb, _ = sizes
    n_all = n_data * n_mode
    modes = M // n_mode
    nbm = nb * modes
    wide = D // n_data
    share = FF // n_all
    thin = jnp.zeros((16, LANES), F32)
    for d in range(n_all):
        in_ref[d * nbm : (d + 1) * nbm, :] = got_ref[d, :nbm, :].astype(F32)
        thin += got_ref[d, nbm:, :].astype(F32)
    thin = thin[:LEAD] + thin[LEAD:]
    thin_ref[...] = thin
    if modes < 16:
        wide_ref[...] = jnp.zeros_like(wide_ref)
    for m in range(modes):
        grad = [in_ref[pl.ds(k * modes + m, n_all, stride=nbm), :] for k in range(nb)]
        grad = jnp.concatenate(grad, axis=0).astype(BF)
        grad_ref[m] = grad
        back = mm(grad, mixer_ref[m], NT).astype(BF).astype(F32)
        if 2 * wide < LANES:
            back = jnp.concatenate(
                [back, jnp.zeros((back.shape[0], LANES - 2 * wide), F32)], axis=1
            )
        for k in range(nb):
            wide_ref[k, pl.ds(m, n_all, stride=16), :] = back[k * n_all : (k + 1) * n_all]
    inner = first_ref[...].reshape(n_all * 16, LANES)
    inner = jnp.where(iota(inner.shape, 1) < HALF, inner, 0.0)
    inner = by_halves(fold(inner))
    total = jnp.zeros((LEAD, LANES), F32)
    for k in range(nb):
        query = mm(inner, wide_ref[k].astype(BF), TN)
        query = query[:HALF] + query[HALF:]
        for part in range(2):
            at = (part * nb + k) * LEAD
            total += from_lane(query[at : at + LEAD], part * wide, wide)
    block = total + at_lane(from_lane(thin, 0, share), HALF, share)
    row, lane = iota(block.shape, 0), iota(block.shape, 1)
    stats = jnp.where(lane < HALF, stat_ref[:1, :], stat_ref[1:2, :])
    block = jnp.where(row == C, stats, block)
    for d in range(n_all):
        send_ref[d] = block


def spectral_kernel(
    modes,
    wide,
    ready,
    spec_ref,
    grad_ref,
    w_ref,
    m_ref,
    v_ref,
    ema_ref,
    w_out,
    m_out,
    v_out,
    ema_out,
    low_out,
    pair_ref,
    turn_ref,
):
    ready()
    lower = iota((wide, LANES), 1) < HALF
    half_lower = iota((wide // 2, LANES), 1) < HALF
    for m in range(modes):
        slopes = mm(spec_ref[m], grad_ref[m], TN)
        other = pltpu.roll(slopes[wide:], HALF, 1)
        pair_ref[m] = jnp.where(lower, slopes[:wide] + other, slopes[:wide] - other)
        even = pair_ref[m, pl.ds(0, wide // 2, stride=2), :]
        odd = pair_ref[m, pl.ds(1, wide // 2, stride=2), :]
        real = jnp.where(half_lower, even, pltpu.roll(odd, HALF, 1))
        imag = jnp.where(half_lower, pltpu.roll(even, HALF, 1), odd)
        turn_ref[0, pl.ds(m, wide // 2, stride=modes), :] = real
        turn_ref[1, pl.ds(m, wide // 2, stride=modes), :] = imag
    for part in range(2):
        for at in range(wide // 2):
            cols = slice(at * LANES, (at + 1) * LANES)
            grad = turn_ref[part, at * modes : (at + 1) * modes, :]
            new = adamw(
                w_ref[part, :, cols],
                grad,
                m_ref[part, :, cols],
                v_ref[part, :, cols],
                ema_ref[part, :, cols],
                RATE_SPEC,
            )
            for ref, value in zip((w_out, m_out, v_out, ema_out, low_out), new, strict=True):
                ref[part, :, cols] = value


def rows_kernel(
    sizes,
    n_big,
    got_ref,
    thin_ref,
    steps_ref,
    w_ref,
    m_ref,
    v_ref,
    ema_ref,
    *refs,
):
    big_refs, (loss_ref, w_out, m_out, v_out, ema_out, low_out) = refs[:n_big], refs[n_big:]
    n_data, n_mode, _, total = sizes
    n_all = n_data * n_mode
    wide = D // n_data
    share = FF // n_all
    rows = w_ref.shape[0]
    query = []
    for at in range(D // LANES):
        block = jnp.zeros((LEAD, LANES), F32)
        for i in range(at * LANES // wide, (at + 1) * LANES // wide):
            part = sum(got_ref[i * n_mode + j, :LEAD, :] for j in range(n_mode))
            block += at_lane(part, i * wide % LANES, wide)
        query.append(block)
    query = jnp.concatenate(query, axis=1)
    down = []
    for at in range(FF // LANES):
        block = jnp.zeros((LEAD, LANES), F32)
        for d in range(at * LANES // share, (at + 1) * LANES // share):
            block += at_lane(from_lane(got_ref[d, :LEAD, :], HALF, share), d * share % LANES, share)
        down.append(block)
    down = jnp.where(iota((LEAD, FF), 0) < C, jnp.concatenate(down, axis=1), 0.0)
    norm = SPECTRAL_WEIGHT / (total * M * S)
    stats = sum(got_ref[d, C : C + 1, :] for d in range(n_all))
    steps = steps_ref[C : C + 1, HALF : HALF + 1]
    loss_ref[...] = stats[:, :1] / steps + norm * stats[:, HALF : HALF + 1]

    keep = iota((LEAD, D), 0) < C
    query = jnp.where(keep, query, 0.0)
    query = jnp.concatenate(split(query), axis=0).astype(BF)
    down = jnp.concatenate(split(down), axis=0).astype(BF)
    thin = thin_rows(w_ref)
    embed = at_lane(thin, 0, C) + at_lane(from_lane(thin, 0, C), LEAD, C)
    head = from_lane(thin, LEAD, C)
    head = at_lane(head, 0, C) + at_lane(head, LEAD, C)

    def back(weights, sums):
        sums = jnp.concatenate([sums, jnp.zeros((LANES - 16, sums.shape[1]), BF)], axis=0)
        out = mm(weights.astype(BF), sums, NT)
        return from_lane(out, 0, LEAD) + from_lane(out, LEAD, LEAD)

    own = jnp.concatenate([thin_ref[...], jnp.zeros((LANES - LEAD, LANES), F32)], axis=0).T
    embed_grad = own[HALF : HALF + rows] + back(w_ref[:, :D], query)
    head_grad = own[HALF + rows : HALF + 2 * rows] + back(
        w_ref[:, 2 * D + FF : 2 * D + 2 * FF], down
    )
    last = at_lane(embed_grad, 0, C) + at_lane(head_grad, C, C)

    def update(grad, cols):
        new = adamw(w_ref[:, cols], grad, m_ref[:, cols], v_ref[:, cols], ema_ref[:, cols], RATE_DENSE)
        for ref, value in zip((w_out, m_out, v_out, ema_out, low_out), new, strict=True):
            ref[:, cols] = value

    update(mm(embed[:, :16].astype(BF), query), slice(0, D))
    update(sum(ref[...].astype(F32) for ref in big_refs), slice(D, 2 * D + FF))
    update(mm(head[:, :16].astype(BF), down), slice(2 * D + FF, 2 * D + 2 * FF))
    update(last[:, : 2 * C], slice(2 * D + 2 * FF, 2 * D + 2 * FF + 2 * C))


def per_device(
    series,
    future_values,
    step_mask,
    mode_index,
    dense,
    dense_m,
    dense_v,
    dense_ema,
    spectral,
    spec_m,
    fourier_variance_moment,
    spec_ema,
):
    n_mode = lax.axis_size("mode")
    n_data = lax.axis_size("dp")
    n_all = n_mode * n_data
    time_rows, batch, chans = series.shape
    nb = batch // n_mode
    total = batch * n_data
    modes = M // n_mode
    wide = D // n_data
    rows = dense.shape[0]
    shape = jax.ShapeDtypeStruct
    sizes = (n_data, n_mode, nb, total)
    tiled = rows % 16 == 0 and n_mode == 4 and n_data >= 4

    send, weights = call(
        partial(pack_kernel, sizes),
        (shape((n_mode, 2 * nb * LEAD, time_rows), F32), shape((rows, D + FF + LANES), BF)),
        (series.transpose(2, 1, 0), future_values.transpose(2, 1, 0), step_mask.T, dense),
        [pltpu.VMEM((chans, batch, time_rows), F32), pltpu.VMEM((batch, time_rows), F32)],
        name="pack",
        ahead=(0, 1, 2, 3),
    )
    me = jnp.stack([lax.axis_index("dp"), lax.axis_index("mode")]).astype(jnp.int32)
    own = exchange(send, "mode")
    cosv, sinv = tables(mode_index)
    weights = [gather_rows(weights)] if not tiled else gather_tiles_first(weights)
    if tiled:
        weights = gather_tiles_second(*weights)

    whole_rows = [pltpu.VMEM((2 * nb * LEAD, S), F32)]
    send = call(
        partial(spectra_kernel, sizes),
        shape((n_all, 16, LANES), F32),
        (own, cosv, sinv, dense),
        whole_rows,
        name="spectra",
    )
    first = exchange(send, AXES)
    ins = call(
        tables_kernel,
        (
            shape((S, 4 * M), BF),
            shape((3 * M, S), BF),
            shape((2 * M, S), BF),
            shape((S, 2 * M), BF),
            shape((S, LANES), F32),
            shape((S, LANES), F32),
        ),
        (own, cosv, sinv),
        whole_rows,
        name="tables",
        cost=10**10,
    )
    first, *ins = together(first, *ins)
    if tiled:
        weights = gather_tiles_third(*weights)

    w_low = spectral.astype(BF).reshape(2, modes, wide, E)
    mixer = jnp.concatenate(
        [
            jnp.concatenate([w_low[0], w_low[1]], axis=2),
            jnp.concatenate([-w_low[1], w_low[0]], axis=2),
        ],
        axis=1,
    )
    scratch = [
        pltpu.VMEM((nb, n_all * 16, LANES), F32),
        pltpu.VMEM((n_all * nb * modes, LANES), F32),
    ]
    send, spec, thin = call(
        partial(mix_kernel, sizes),
        (
            shape((n_all, nb * modes + 16, LANES), BF),
            shape((modes, total, 2 * wide), BF),
            shape((16, LANES), F32),
        ),
        (first, mixer),
        scratch,
        name="mix",
    )
    if tiled:
        send, *weights = together(send, *weights)
        weights = gather_tiles_last(weights)
    got = exchange(send, AXES)
    steps = thin

    send, stats, *big = block(
        steps[C, HALF].reshape(1),
        me,
        weights,
        (got, *ins),
        sizes + (True,) if tiled else sizes,
    )
    got = exchange(send, AXES)
    if tiled:
        big = scatter_tiles_first(*big)
        got, *big = together(got, *big)
        big = scatter_tiles_second(*big)
    send, grad_mixed, thin = call(
        partial(mix_back_kernel, sizes),
        (
            shape((n_all, LEAD, LANES), F32),
            shape((modes, total, LANES), BF),
            shape((LEAD, LANES), F32),
        ),
        (got, mixer, first, stats),
        scratch[::-1],
        name="mix_back",
        cost=10**10,
    )
    if tiled:
        grad_mixed, big = together(grad_mixed, big)
    spec_out = call(
        partial(spectral_kernel, modes, wide),
        (shape(spectral.shape, F32),) * 4 + (shape(spectral.shape, BF),),
        (spec, grad_mixed, spectral, spec_m, fourier_variance_moment, spec_ema),
        [
            pltpu.VMEM((modes, wide, LANES), F32),
            pltpu.VMEM((2, modes * wide // 2, LANES), F32),
        ],
        name="spectral",
        ahead=(0, 1, 2, 3, 4, 5),
        cost=10**10,
    )
    got = exchange(send, AXES)
    big = scatter_tiles_third(*big) if tiled else [scatter_rows(big[0], rows)]
    loss, *dense_out = call(
        partial(rows_kernel, sizes, len(big)),
        (shape((1, 1), F32),) + (shape(dense.shape, F32),) * 4 + (shape(dense.shape, BF),),
        (got, thin, steps, dense, dense_m, dense_v, dense_ema, *big),
        name="rows",
    )
    return (loss.reshape(()),) + tuple(dense_out) + tuple(spec_out)


def solution(mesh):
    rows = P(("dp", "mode"), None)
    mixing = P(None, "mode", "dp")
    return jax.shard_map(
        per_device,
        mesh=mesh,
        in_specs=(P("mode", "dp", None), P("mode", "dp", None), P("mode", "dp"), P())
        + (rows,) * 4
        + (mixing,) * 4,
        out_specs=(P(),) + (rows,) * 5 + (mixing,) * 5,
        check_vma=False,
    )
```
